32 devices in a mesh: teach: 4 (over y, x), stud: 2 (over core), mdl: 4 (over z).
Axes of the slice: x: 2, y: 2, z: 4, core: 2. Of those that a mesh axis runs over, the one named last changes fastest.
Arguments:
- states: bfloat16 [1024, 512], P(('teach', 'stud')), may hold values from -6 to 6
- task_ids: int32 [1024, 1], P(('teach', 'stud')), may hold values from 0 to 3; in each aligned block of 128 rows (0 to 127, 128 to 255, ...) at most 48 rows name the same one
- student_batch: int32 [1024, 1], P(('teach', 'stud')), may hold values from 0 to 7; in each aligned block of 128 rows (0 to 127, 128 to 255, ...) at most 32 rows name the same one
- teach_in: bfloat16 [4, 512, 1024], P('teach', None, 'mdl'), may hold values from -0.25 to 0.25
- teach_out: bfloat16 [4, 1024, 512], P('teach', 'mdl'), may hold values from -0.1875 to 0.1875
- student_up: bfloat16 [512, 1024], P(None, 'mdl'), may hold values from -0.25 to 0.25
- student_down: bfloat16 [512, 1024], P(None, 'mdl'), may hold values from -0.1875 to 0.1875
Outputs:
- grad_up: float32 [512, 1024], P(('teach', 'stud'), 'mdl')
- grad_down: float32 [512, 1024], P(('teach', 'stud'), 'mdl')
The draws below stay inside these ranges and needn't reach their ends.
Inputs may be any that keep to these rules, and one draw needn't show every extreme that they name: `task_ids`: teacher t lives at index t // 1 of teach. Among one device's 128 states no teacher is named more than 48 times, and in every draw some teacher is named exactly 48 times there; every teacher is named somewhere. `student_batch`: batch b belongs to teach index b // 2 and stud index b % 2. Among one device's 128 states no batch is named more than 32 times, some batch exactly 32 times; every batch holds one state or more.
All inputs are finite; a program needn't handle non-finite values.
Results may differ from the reference program's by a relative error of at most 0.0023.
Values may be sent and summed in bfloat16 or wider, within the bound.
No kernel may reach another device: no remote copies, remote signals or barrier semaphores. Data moves between devices by JAX's collectives and lax.ppermute only.
A program may use at most 64 MiB of HBM per device.

```python
import math
import jax
import jax.numpy as jnp
import numpy as np
from jax import lax

DS = 512
TW = 1024
HS = 1024
ACT = 512
ROWS = 128
NTEACH = 4
NB = 8
STATES = 1024
CAPT = 48
CAP2 = 32


def steps_of(own_key, extent, cuts, low, high):
    def one(position, parts):
        draws = jax.random.uniform(jax.random.fold_in(jax.random.fold_in(own_key, 6), position), (parts,), jnp.float32, low / len(cuts), high / len(cuts))
        return jnp.repeat(jnp.exp(draws), extent[position] // parts).reshape((-1,) + (1,) * (len(extent) - position - 1))

    level = one(*cuts[0])
    for cut in cuts[1:]:
        level = level * one(*cut)
    return level


def deal_out(own_key, own, number, rows, number_of, top, most, slope):
    order = jax.random.permutation(own_key, number_of)
    packed, common = load_shares(number_of, rows * top, most, slope, True), load_shares(number_of, rows * top, most, slope, False)
    places = jnp.arange(number_of)

    def named(tallies, offset_by):
        used = int((tallies > 0).sum())
        fixed = max(1, used // 4)
        moved = fixed + (places - fixed + offset_by * (used - fixed)) % max(1, number_of - fixed)
        return jnp.zeros((number_of,), jnp.int32).at[order[jnp.where(places < fixed, places, moved)]].set(jnp.asarray(tallies, jnp.int32))

    tallies = jnp.where(number % 4 == 0, named(packed, number // 4), named(common, number - number // 4 - 1))
    mixed = jax.random.permutation(jax.random.fold_in(own, 3), number_of)
    giver, sink = mixed[0:number_of // 2 * 2:2], mixed[1:number_of // 2 * 2:2]
    room = jnp.minimum(tallies[giver] - 1, most - tallies[sink]) // 2
    room = jnp.where((giver == order[0]) | (sink == order[0]) | (tallies[sink] == 0), 0, jnp.maximum(room, 0))
    moved = jax.random.randint(jax.random.fold_in(own, 4), (number_of // 2,), 0, 1 << 20) % (room + 1)
    tallies = tallies.at[giver].add(-moved).at[sink].add(moved)
    members = jnp.searchsorted(jnp.cumsum(tallies), jnp.arange(rows * top), side="right").astype(jnp.int32)
    listing = members.reshape(top, rows).T
    listing = listing[jax.random.permutation(jax.random.fold_in(own, 1), rows)]
    offset_by = jax.random.randint(jax.random.fold_in(own, 2), (rows, 1), 0, top)
    return jnp.take_along_axis(listing, (jnp.arange(top)[None, :] + offset_by) % top, axis=1)


def load_shares(number_of, total, bound, lean, full):
    portions = [(1 << 20) // math.isqrt(grade ** lean) + 1 for grade in range(1, number_of + 1)]
    largest = bound if full else min(bound, max(-(-total // number_of), total * portions[0] // sum(portions)))
    least = 1 if total - largest >= number_of - 1 else 0
    given, spare = [largest] + [least] * (number_of - 1), total - largest - least * (number_of - 1)
    while spare > 0:
        movable = [i for i in range(1, number_of) if given[i] < largest] or [i for i in range(1, number_of) if given[i] < bound]
        whole, budget = sum([portions[i] for i in movable]), spare
        for i in movable:
            addition = min(bound - given[i], max(1, budget * portions[i] // whole), spare)
            given[i] = given[i] + addition
            spare = spare - addition
    return np.array(given)


def noise(stream_key, dims, width, limit, shards=(), kind=jnp.bfloat16):
    array = jax.random.normal(stream_key, dims, jnp.float32) * width
    if len(shards) > 0:
        array = steps_of(stream_key, dims, shards, -0.22, 0.18) * array
    return jnp.clip(array, min=-limit, max=limit).astype(kind)


def setup_inputs(seed: int = 0) -> dict:
    arg_keys = jax.random.split(jax.random.key(seed), 8)
    states = noise(arg_keys[0], (STATES, DS), 1.0, 6.0, ((0, 8),))
    task_ids_keys = jax.random.split(jax.random.fold_in(arg_keys[1], 1), STATES // ROWS)
    task_ids_turns = jax.random.permutation(jax.random.fold_in(arg_keys[1], 3), STATES // ROWS)
    task_ids = jax.vmap(lambda own, number: deal_out(jax.random.fold_in(arg_keys[1], 2), own, number, ROWS, NTEACH, 1, CAPT, 2))(task_ids_keys, task_ids_turns).reshape((STATES, 1))
    student_batch_keys = jax.random.split(jax.random.fold_in(arg_keys[2], 1), STATES // ROWS)
    student_batch_turns = jax.random.permutation(jax.random.fold_in(arg_keys[2], 3), STATES // ROWS)
    student_batch = jax.vmap(lambda own, number: deal_out(jax.random.fold_in(arg_keys[2], 2), own, number, ROWS, NB, 1, CAP2, 2))(student_batch_keys, student_batch_turns).reshape((STATES, 1))
    teach_in = noise(arg_keys[3], (NTEACH, DS, TW), DS ** -0.5, 0.25, ((0, 4), (2, 4)))
    teach_out = noise(arg_keys[4], (NTEACH, TW, ACT), TW ** -0.5, 0.1875, ((0, 4), (1, 4)))
    student_up = noise(arg_keys[5], (DS, HS), DS ** -0.5, 0.25, ((1, 4),))
    student_down = noise(arg_keys[6], (ACT, HS), HS ** -0.5, 0.1875, ((1, 4),))
    return {"states": states, "task_ids": task_ids, "student_batch": student_batch, "teach_in": teach_in, "teach_out": teach_out, "student_up": student_up, "student_down": student_down}


def silu_slope(value):
    sig = jax.nn.sigmoid(value)
    return sig * (1.0 + value * (1.0 - sig))


def reference(states, task_ids, student_batch, teach_in, teach_out, student_up, student_down):
    task_list = task_ids[:, 0]
    batch_list = student_batch[:, 0]
    room = NB * CAPT

    def one_teacher(index):
        chosen = task_list == index
        picked = jnp.nonzero(chosen, size=room, fill_value=0)[0].astype(jnp.int32)
        live = (jnp.arange(room, dtype=jnp.int32) < jnp.sum(chosen.astype(jnp.int32))).astype(jnp.float32)
        rows_in = states[picked]
        hidden = jax.nn.silu(jnp.dot(rows_in, teach_in[index], preferred_element_type=jnp.float32)).astype(jnp.bfloat16)
        labels = jnp.dot(hidden, teach_out[index], preferred_element_type=jnp.float32) * live[:, None]
        return picked, labels

    picked, labels = lax.map(one_teacher, jnp.arange(NTEACH, dtype=jnp.int32))
    targets = jnp.zeros((STATES, ACT), labels.dtype).at[picked.reshape(-1)].add(labels.reshape(-1, ACT))
    counts = jnp.sum((batch_list[:, None] == jnp.arange(NB, dtype=jnp.int32)[None, :]).astype(jnp.float32), axis=0)
    weight = 2.0 / counts[batch_list]
    block = math.gcd(STATES, 4096)

    def accumulate(carry, index):
        grad_up, grad_down = carry
        start = index * block
        rows_in = lax.dynamic_slice_in_dim(states, start, block, 0)
        goal = lax.dynamic_slice_in_dim(targets, start, block, 0)
        scale = lax.dynamic_slice_in_dim(weight, start, block, 0)
        pre = jnp.dot(rows_in, student_up, preferred_element_type=jnp.float32)
        act = jax.nn.silu(pre).astype(jnp.bfloat16)
        pred = jnp.dot(act, student_down.T, preferred_element_type=jnp.float32)
        scaled = ((pred - goal) * scale[:, None]).astype(jnp.bfloat16)
        grad_down = grad_down + jnp.dot(scaled.T, act, preferred_element_type=jnp.float32)
        back = jnp.dot(scaled, student_down, preferred_element_type=jnp.float32)
        pre_grad = (back * silu_slope(pre)).astype(jnp.bfloat16)
        grad_up = grad_up + jnp.dot(rows_in.T, pre_grad, preferred_element_type=jnp.float32)
        return (grad_up, grad_down), None

    start_carry = (jnp.zeros((DS, HS), jnp.float32), jnp.zeros((ACT, HS), jnp.float32))
    (grad_up, grad_down), _ = lax.scan(accumulate, start_carry, jnp.arange(STATES // block, dtype=jnp.int32))
    return grad_up, grad_down
```

```python
import jax
import jax.numpy as jnp
from jax import lax
from jax.sharding import PartitionSpec as P

LANES = 128


def silu_slope(value):
    sig = jax.nn.sigmoid(value)
    return sig * (1.0 + value * (1.0 - sig))


def partner_table(size, step):
    if size & (size - 1) == 0:
        return [(i, i ^ step) for i in range(size)]
    return [(i, (i + step) % size) for i in range(size)]


def partner_to(axis, step):
    size, me = lax.axis_size(axis), lax.axis_index(axis)
    return me ^ step if size & (size - 1) == 0 else (me + step) % size


def partner_from(axis, step):
    size, me = lax.axis_size(axis), lax.axis_index(axis)
    return me ^ step if size & (size - 1) == 0 else (me + size - step) % size


def send(block, axis, step):
    return lax.ppermute(block, axis, partner_table(lax.axis_size(axis), step))


def on_device(states, task_ids, student_batch, teach_in, teach_out, student_up, student_down):
    row_count, width = states.shape
    owners, studs, parts = lax.axis_size("teach"), lax.axis_size("stud"), lax.axis_size("mdl")
    local_teachers = teach_in.shape[0]
    teachers = owners * local_teachers
    batches = owners * studs
    room = 3 * row_count // (2 * teachers)
    extra = -(-batches // LANES) * LANES
    task_list, batch_list = task_ids[:, 0], student_batch[:, 0]
    named = (task_list[:, None] == jnp.arange(teachers, dtype=jnp.int32)[None, :]).astype(jnp.float32)
    earlier = (jnp.arange(row_count)[:, None] > jnp.arange(row_count)[None, :]).astype(jnp.float32)
    before = jnp.sum(jnp.dot(earlier, named) * named, axis=1).astype(jnp.int32)
    block_of = jnp.array([partner_to("teach", k) for k in range(owners)])
    step_of = jnp.sum(
        (block_of[None, :] == (task_list // local_teachers)[:, None]) * jnp.arange(owners)[None, :], axis=1
    )
    slot = (step_of * local_teachers + task_list % local_teachers) * room + before
    dispatch = (slot[None, :] == jnp.arange(teachers * room, dtype=jnp.int32)[:, None]).astype(jnp.bfloat16)
    member = (batch_list[:, None] == jnp.arange(extra, dtype=jnp.int32)[None, :]).astype(jnp.bfloat16)
    own_counts = jnp.sum(member.astype(jnp.float32), axis=0)
    outgoing = jnp.dot(dispatch, states, preferred_element_type=jnp.float32).astype(jnp.bfloat16)
    tags = jnp.dot(dispatch, member, preferred_element_type=jnp.float32)
    head = (jnp.arange(teachers * room) % (local_teachers * room) == 0).astype(jnp.float32)
    tags = (tags + head[:, None] * (2.0 * own_counts)[None, :]).astype(jnp.bfloat16)
    outgoing = jnp.concatenate([outgoing, tags], axis=1).reshape(owners, local_teachers * room, width + extra)
    arrived = [outgoing[0]] + [send(outgoing[k], "teach", k) for k in range(1, owners)]
    slots = local_teachers * room * owners
    rows = jnp.stack(arrived)
    tags = rows[:, :, width:].astype(jnp.float32)
    doubled = jnp.floor(tags[:, :1] * 0.5)
    counts = jnp.sum(doubled[:, 0], axis=0)
    tags = jnp.concatenate([tags[:, :1] - 2.0 * doubled, tags[:, 1:]], axis=1).reshape(slots, extra)
    others = [send(counts[None, :], "stud", k) for k in range(1, studs)]
    counts = counts + sum(o[0] for o in others)
    rows = rows[:, :, :width].reshape(owners, local_teachers, room, width)
    hidden = jnp.einsum("ntcd,tdh->ntch", rows, teach_in, preferred_element_type=jnp.float32)
    hidden = jax.nn.silu(hidden).astype(jnp.bfloat16)
    labels = jnp.einsum("ntch,tha->ntca", hidden, teach_out, preferred_element_type=jnp.float32)
    rows = rows.reshape(slots, width)
    pre = jnp.dot(rows, student_up, preferred_element_type=jnp.float32)
    act = jax.nn.silu(pre).astype(jnp.bfloat16)
    pred = jnp.einsum("rh,ah->ra", act, student_down, preferred_element_type=jnp.float32)
    error = (pred - labels.reshape(pred.shape)).reshape(parts, slots // parts, -1)
    mine = lax.axis_index("mdl")
    total = lax.dynamic_index_in_dim(error, mine, 0, False)
    for k in range(1, parts):
        total = total + send(
            lax.dynamic_index_in_dim(error, partner_to("mdl", k), 0, False), "mdl", k
        )
    weight = jnp.sum(tags * jnp.where(counts > 0, 2.0 / counts, 0.0)[None, :], axis=1)
    weight = lax.dynamic_index_in_dim(weight.reshape(parts, -1), mine, 0, False)
    scaled = (total * weight[:, None]).astype(jnp.bfloat16)
    full = jnp.zeros((parts,) + scaled.shape, scaled.dtype)
    full = lax.dynamic_update_index_in_dim(full, scaled, mine, 0)
    for k in range(1, parts):
        full = lax.dynamic_update_index_in_dim(full, send(scaled, "mdl", k), partner_from("mdl", k), 0)
    scaled = full.reshape(slots, -1)
    grad_down = jnp.einsum("ra,rh->ah", scaled, act, preferred_element_type=jnp.float32)
    back = jnp.dot(scaled, student_down, preferred_element_type=jnp.float32)
    pre_grad = (back * silu_slope(pre)).astype(jnp.bfloat16)
    grad_up = jnp.einsum("rd,rh->dh", rows, pre_grad, preferred_element_type=jnp.float32)

    def share(grad):
        height = grad.shape[0] // (owners * studs)
        grad = grad.reshape(owners, studs, height, -1)
        half = lax.dynamic_index_in_dim(grad, lax.axis_index("stud"), 1, False)
        for k in range(1, studs):
            half = half + send(lax.dynamic_index_in_dim(grad, partner_to("stud", k), 1, False), "stud", k)
        part = lax.dynamic_index_in_dim(half, lax.axis_index("teach"), 0, False)
        for k in range(1, owners):
            block = lax.dynamic_index_in_dim(half, partner_to("teach", k), 0, False)
            part = part + send(block.astype(jnp.bfloat16), "teach", k).astype(jnp.float32)
        return part

    return share(grad_up), share(grad_down)


def solution(mesh):
    in_specs = (
        P(("teach", "stud"), None),
        P(("teach", "stud"), None),
        P(("teach", "stud"), None),
        P("teach", None, "mdl"),
        P("teach", "mdl", None),
        P(None, "mdl"),
        P(None, "mdl"),
    )
    out_specs = (P(("teach", "stud"), "mdl"), P(("teach", "stud"), "mdl"))
    return jax.shard_map(
        on_device, mesh=mesh, in_specs=in_specs, out_specs=out_specs, check_vma=False
    )
```

```python
import functools

import jax
import jax.numpy as jnp
from jax import lax
from jax.experimental import pallas as pl
from jax.experimental.pallas import tpu as pltpu
from jax.sharding import PartitionSpec as P

LANES = 128
ROW_TILE = 16
VMEM = pl.BlockSpec(memory_space=pltpu.VMEM)


def up_to(value, step):
    return -(-value // step) * step


def is_power(size):
    return size & (size - 1) == 0


def partner_to(size, me, step):
    return me ^ step if is_power(size) else (me + step) % size


def partner_from(size, me, step):
    return me ^ step if is_power(size) else (me + size - step) % size


def send(block, axis, step):
    size = lax.axis_size(axis)
    return lax.ppermute(block, axis, [(i, partner_to(size, i, step)) for i in range(size)])


def call(body, outs, operands, flops):
    moved = sum(a.size * a.dtype.itemsize for a in operands) + sum(
        o.size * o.dtype.itemsize for o in outs
    )
    return pl.pallas_call(
        body,
        out_shape=outs,
        in_specs=[VMEM] * len(operands),
        out_specs=[VMEM] * len(outs),
        cost_estimate=pl.CostEstimate(flops=flops, bytes_accessed=moved, transcendentals=0),
        compiler_params=pltpu.CompilerParams(vmem_limit_bytes=24 * 1024 * 1024),
    )(*operands)


def dot(left, right, contract=((1,), (0,))):
    return lax.dot_general(left, right, (contract, ((), ())), preferred_element_type=jnp.float32)


def dispatch_body(owners, local, room, extra, states, task, batch, *outs):
    rows, width = states.shape
    me = lax.axis_index("teach")
    task_list, batch_list = task[...], batch[...]
    group = up_to(owners * local, ROW_TILE)
    named = lax.broadcasted_iota(jnp.int32, (group, rows), 0) == task_list
    earlier = lax.broadcasted_iota(jnp.int32, (rows, rows), 0) < lax.broadcasted_iota(
        jnp.int32, (rows, rows), 1
    )
    named = named.astype(jnp.float32)
    before = dot(named.astype(jnp.bfloat16), earlier.astype(jnp.float32).astype(jnp.bfloat16))
    before = jnp.sum(before * named, axis=0, keepdims=True).astype(jnp.int32)
    owner = task_list // local if local > 1 else task_list
    step = owner ^ me if is_power(owners) else (owner - me + owners) % owners
    place = step * local + task_list % local if local > 1 else step
    slot = place * room + before
    index = lax.broadcasted_iota(jnp.int32, (owners * local * room, rows), 0)
    chosen = (index == slot).astype(jnp.float32)
    head = (index % (local * room) == 0).astype(jnp.float32)
    member = (lax.broadcasted_iota(jnp.int32, (extra, rows), 0) == batch_list).astype(jnp.float32)
    moved = dot(chosen.astype(jnp.bfloat16), states[...]).astype(jnp.bfloat16)
    tags = dot(
        (chosen + 2.0 * head).astype(jnp.bfloat16), member.astype(jnp.bfloat16), ((1,), (1,))
    ).astype(jnp.bfloat16)
    for k, out in enumerate(outs):
        span = slice(k * local * room, (k + 1) * local * room)
        out[:, :width] = moved[span]
        out[:, width:] = tags[span]


def forward_body(owners, local, room, parts, *refs):
    blocks, refs = refs[:owners], refs[owners:]
    teach_in, teach_out, student_up, student_down = refs[:4]
    rows_out, act_out, slope_out, tags_out, counts_out, own = refs[4:10]
    sends, error = refs[10:-1], refs[-1]
    width = student_up.shape[0]
    full = [block[...] for block in blocks]
    counts = None
    for block in full:
        mine = jnp.floor(block[:1, width:].astype(jnp.float32) * 0.5)
        counts = mine if counts is None else counts + mine
    counts_out[...] = counts
    for l in range(local):
        span = slice(l * owners * room, (l + 1) * owners * room)
        for k, block in enumerate(full):
            start = l * owners * room + k * room
            rows_out[start : start + room] = block[l * room : (l + 1) * room, :width]
            tag = block[l * room : (l + 1) * room, width:].astype(jnp.float32)
            if l == 0:
                head = lax.broadcasted_iota(jnp.int32, tag.shape, 0) == 0
                tag = jnp.where(head, tag - 2.0 * jnp.floor(tag * 0.5), tag)
            tags_out[start : start + room] = tag
        rows = rows_out[span]
        hidden = dot(rows, teach_in[l])
        hidden = (hidden / (1.0 + jnp.exp(-hidden))).astype(jnp.bfloat16)
        labels = dot(hidden, teach_out[l])
        pre = dot(rows, student_up[...])
        sig = 1.0 / (1.0 + jnp.exp(-pre))
        act = (pre * sig).astype(jnp.bfloat16)
        act_out[span] = act
        slope_out[span] = sig * (1.0 + pre * (1.0 - sig))
        error[span] = dot(act, student_down[...], ((1,), (1,))) - labels
    me = lax.axis_index("mdl")
    height = own.shape[0]
    own[...] = error[pl.ds(pl.multiple_of(me * height, 8), height)]
    for k, out in enumerate(sends):
        there = partner_to(parts, me, k + 1)
        out[...] = error[pl.ds(pl.multiple_of(there * height, 8), height)]


def backward_body(parts, *refs):
    chunks, refs = refs[:parts], refs[parts:]
    rows, act, slope, student_down, grad_up, grad_down, scaled = refs
    me = lax.axis_index("mdl")
    height = chunks[0].shape[0]
    for k, chunk in enumerate(chunks):
        there = partner_from(parts, me, k)
        scaled[pl.ds(pl.multiple_of(there * height, 8), height)] = chunk[...].astype(jnp.float32)
    full = scaled[...].astype(jnp.bfloat16)
    grad_down[...] = dot(full, act[...], ((0,), (0,)))
    pre_grad = (dot(full, student_down[...]) * slope[...]).astype(jnp.bfloat16)
    grad_up[...] = dot(rows[...], pre_grad, ((0,), (0,)))


def on_device(states, task_ids, student_batch, teach_in, teach_out, student_up, student_down):
    row_count, width = states.shape
    owners, studs, parts = lax.axis_size("teach"), lax.axis_size("stud"), lax.axis_size("mdl")
    local, _, hidden = teach_in.shape
    actions = teach_out.shape[2]
    units = student_up.shape[1]
    teachers, batches = owners * local, owners * studs
    room = up_to(3 * row_count // (2 * teachers), ROW_TILE)
    extra = up_to(batches, LANES)
    slots = teachers * room
    height = slots // parts
    f32, bf16 = jnp.float32, jnp.bfloat16
    block = jax.ShapeDtypeStruct((local * room, width + extra), bf16)
    blocks = call(
        functools.partial(dispatch_body, owners, local, room, extra),
        [block] * owners,
        (states, task_ids.reshape(1, row_count), student_batch.reshape(1, row_count)),
        2 * slots * row_count * width,
    )
    blocks = [blocks[0]] + [send(blocks[k], "teach", k) for k in range(1, owners)]
    rows, act, slope, tags, counts, own, *outgoing = pl.pallas_call(
        functools.partial(forward_body, owners, local, room, parts),
        out_shape=[
            jax.ShapeDtypeStruct((slots, width), bf16),
            jax.ShapeDtypeStruct((slots, units), bf16),
            jax.ShapeDtypeStruct((slots, units), f32),
            jax.ShapeDtypeStruct((slots, extra), f32),
            jax.ShapeDtypeStruct((1, extra), f32),
        ]
        + [jax.ShapeDtypeStruct((height, actions), f32)] * parts,
        in_specs=[VMEM] * (owners + 4),
        out_specs=[VMEM] * (5 + parts),
        scratch_shapes=[pltpu.VMEM((slots, actions), f32)],
        cost_estimate=pl.CostEstimate(
            flops=2 * slots * 2 * width * (hidden + units), bytes_accessed=2 << 20, transcendentals=0
        ),
        compiler_params=pltpu.CompilerParams(vmem_limit_bytes=24 * 1024 * 1024),
    )(*blocks, teach_in, teach_out, student_up, student_down)
    mine = lax.axis_index("mdl")
    total = own
    for k in range(1, parts):
        total = total + send(outgoing[k - 1], "mdl", k)
    for other in [send(counts, "stud", k) for k in range(1, studs)]:
        counts = counts + other
    weight = jnp.sum(tags * jnp.where(counts > 0, 2.0 / counts, 0.0), axis=1)
    weight = lax.dynamic_index_in_dim(weight.reshape(parts, height), mine, 0, False)
    scaled = (total * weight[:, None]).astype(bf16)
    chunks = [scaled] + [send(scaled, "mdl", k) for k in range(1, parts)]
    grad_up, grad_down = pl.pallas_call(
        functools.partial(backward_body, parts),
        out_shape=[
            jax.ShapeDtypeStruct((width, units), f32),
            jax.ShapeDtypeStruct((actions, units), f32),
        ],
        in_specs=[VMEM] * (parts + 4),
        out_specs=[VMEM] * 2,
        scratch_shapes=[pltpu.VMEM((slots, actions), f32)],
        cost_estimate=pl.CostEstimate(
            flops=6 * slots * width * units, bytes_accessed=2 << 20, transcendentals=0
        ),
        compiler_params=pltpu.CompilerParams(vmem_limit_bytes=24 * 1024 * 1024),
    )(*chunks, rows, act, slope, student_down)
    heights = (width // (owners * studs), actions // (owners * studs))

    def pieces(stud):
        return jnp.concatenate(
            [
                lax.dynamic_index_in_dim(g.reshape(owners, studs, h, units), stud, 1, False)
                for g, h in zip((grad_up, grad_down), heights)
            ],
            axis=1,
        )

    half = pieces(lax.axis_index("stud"))
    for k in range(1, studs):
        half = half + send(pieces(partner_to(studs, lax.axis_index("stud"), k)), "stud", k)
    me = lax.axis_index("teach")
    part = lax.dynamic_index_in_dim(half, me, 0, False)
    arrived = [
        send(lax.dynamic_index_in_dim(half, partner_to(owners, me, k), 0, False).astype(bf16), "teach", k)
        for k in range(1, owners)
    ]
    for piece in arrived:
        part = part + piece.astype(f32)
    return part[: heights[0]], part[heights[0] :]


def solution(mesh):
    in_specs = (
        P(("teach", "stud"), None),
        P(("teach", "stud"), None),
        P(("teach", "stud"), None),
        P("teach", None, "mdl"),
        P("teach", "mdl", None),
        P(None, "mdl"),
        P(None, "mdl"),
    )
    out_specs = (P(("teach", "stud"), "mdl"), P(("teach", "stud"), "mdl"))
    return jax.shard_map(
        on_device, mesh=mesh, in_specs=in_specs, out_specs=out_specs, check_vma=False
    )
```

```python
import functools

import jax
import jax.numpy as jnp
from jax import lax
from jax.experimental import pallas as pl
from jax.experimental.pallas import tpu as pltpu
from jax.sharding import PartitionSpec as P

LANES = 128
ROW_TILE = 16
VMEM = pl.BlockSpec(memory_space=pltpu.VMEM)
HBM = pl.BlockSpec(memory_space=pltpu.HBM)


def up_to(value, step):
    return -(-value // step) * step


def is_power(size):
    return size & (size - 1) == 0


def partner_to(size, me, step):
    return me ^ step if is_power(size) else (me + step) % size


def partner_from(size, me, step):
    return me ^ step if is_power(size) else (me + size - step) % size


def send(block, axis, step):
    size = lax.axis_size(axis)
    return lax.ppermute(block, axis, [(i, partner_to(size, i, step)) for i in range(size)])


def dot(left, right, contract=((1,), (0,))):
    return lax.dot_general(left, right, (contract, ((), ())), preferred_element_type=jnp.float32)


def dispatch_body(owners, local, room, extra, *refs):
    sources, refs = refs[:3], refs[3:]
    weights, refs = refs[:4], refs[4:]
    outs, refs = refs[:owners], refs[owners:]
    weights_out, refs = refs[:4], refs[4:]
    states, task, batch, sems = refs
    rows, width = states.shape
    copies = [
        pltpu.make_async_copy(source, target, sems.at[i])
        for i, (source, target) in enumerate(
            zip((*sources, *weights), (states, task, batch, *weights_out))
        )
    ]
    for i in (1, 2, 0, 3, 4, 5, 6):
        copies[i].start()
    copies[1].wait()
    copies[2].wait()
    me = lax.axis_index("teach")
    task_list, batch_list = task[...], batch[...]
    group = up_to(owners * local, ROW_TILE)
    named = lax.broadcasted_iota(jnp.int32, (group, rows), 0) == task_list
    earlier = lax.broadcasted_iota(jnp.int32, (rows, rows), 0) < lax.broadcasted_iota(
        jnp.int32, (rows, rows), 1
    )
    named = named.astype(jnp.float32)
    before = dot(named.astype(jnp.bfloat16), earlier.astype(jnp.float32).astype(jnp.bfloat16))
    before = jnp.sum(before * named, axis=0, keepdims=True).astype(jnp.int32)
    owner = task_list // local if local > 1 else task_list
    step = owner ^ me if is_power(owners) else (owner - me + owners) % owners
    place = step * local + task_list % local if local > 1 else step
    slot = place * room + before
    index = lax.broadcasted_iota(jnp.int32, (owners * local * room, rows), 0)
    chosen = (index == slot).astype(jnp.float32)
    head = (index % (local * room) == 0).astype(jnp.float32)
    member = (lax.broadcasted_iota(jnp.int32, (extra, rows), 0) == batch_list).astype(jnp.float32)
    copies[0].wait()
    moved = dot(chosen.astype(jnp.bfloat16), states[...]).astype(jnp.bfloat16)
    tags = dot(
        (chosen + 2.0 * head).astype(jnp.bfloat16), member.astype(jnp.bfloat16), ((1,), (1,))
    ).astype(jnp.bfloat16)
    for k, out in enumerate(outs):
        span = slice(k * local * room, (k + 1) * local * room)
        out[:, :width] = moved[span]
        out[:, width:] = tags[span]
    for copy in copies[3:]:
        copy.wait()


def forward_body(owners, local, room, parts, *refs):
    blocks, refs = refs[:owners], refs[owners:]
    teach_in, teach_out, student_up, student_down = refs[:4]
    rows_out, act_out, slope_out, tags_out, counts_out, own = refs[4:10]
    sends, error = refs[10:-1], refs[-1]
    width = student_up.shape[0]
    full = [block[...] for block in blocks]
    counts = None
    for block in full:
        mine = jnp.floor(block[:1, width:].astype(jnp.float32) * 0.5)
        counts = mine if counts is None else counts + mine
    counts_out[...] = counts
    for l in range(local):
        span = slice(l * owners * room, (l + 1) * owners * room)
        for k, block in enumerate(full):
            start = l * owners * room + k * room
            rows_out[start : start + room] = block[l * room : (l + 1) * room, :width]
            tag = block[l * room : (l + 1) * room, width:].astype(jnp.float32)
            if l == 0:
                head = lax.broadcasted_iota(jnp.int32, tag.shape, 0) == 0
                tag = jnp.where(head, tag - 2.0 * jnp.floor(tag * 0.5), tag)
            tags_out[start : start + room] = tag
        rows = rows_out[span]
        hidden = dot(rows, teach_in[l])
        hidden = (hidden / (1.0 + jnp.exp(-hidden))).astype(jnp.bfloat16)
        labels = dot(hidden, teach_out[l])
        pre = dot(rows, student_up[...])
        sig = 1.0 / (1.0 + jnp.exp(-pre))
        act = (pre * sig).astype(jnp.bfloat16)
        act_out[span] = act
        slope_out[span] = sig * (1.0 + pre * (1.0 - sig))
        error[span] = dot(act, student_down[...], ((1,), (1,))) - labels
    me = lax.axis_index("mdl")
    height = own.shape[0]
    own[...] = error[pl.ds(pl.multiple_of(me * height, 8), height)]
    for k, out in enumerate(sends):
        there = partner_to(parts, me, k + 1)
        out[...] = error[pl.ds(pl.multiple_of(there * height, 8), height)]


def backward_body(parts, *refs):
    chunks, refs = refs[:parts], refs[parts:]
    rows, act, slope, student_down, grad_up, grad_down, scaled = refs
    me = lax.axis_index("mdl")
    height = chunks[0].shape[0]
    for k, chunk in enumerate(chunks):
        there = partner_from(parts, me, k)
        scaled[pl.ds(pl.multiple_of(there * height, 8), height)] = chunk[...].astype(jnp.float32)
    full = scaled[...].astype(jnp.bfloat16)
    grad_down[...] = dot(full, act[...], ((0,), (0,)))
    pre_grad = (dot(full, student_down[...]) * slope[...]).astype(jnp.bfloat16)
    grad_up[...] = dot(rows[...], pre_grad, ((0,), (0,)))


def on_device(states, task_ids, student_batch, teach_in, teach_out, student_up, student_down):
    row_count, width = states.shape
    owners, studs, parts = lax.axis_size("teach"), lax.axis_size("stud"), lax.axis_size("mdl")
    local, _, hidden = teach_in.shape
    actions = teach_out.shape[2]
    units = student_up.shape[1]
    teachers, batches = owners * local, owners * studs
    room = up_to(3 * row_count // (2 * teachers), ROW_TILE)
    extra = up_to(batches, LANES)
    slots = teachers * room
    height = slots // parts
    f32, bf16 = jnp.float32, jnp.bfloat16
    block = jax.ShapeDtypeStruct((local * room, width + extra), bf16)
    weights = (teach_in, teach_out, student_up, student_down)
    results = pl.pallas_call(
        functools.partial(dispatch_body, owners, local, room, extra),
        out_shape=[pltpu.VMEM(block.shape, bf16)] * owners + [pltpu.VMEM(w.shape, w.dtype) for w in weights],
        in_specs=[HBM] * 7,
        out_specs=[VMEM] * (owners + 4),
        scratch_shapes=[
            pltpu.VMEM(states.shape, states.dtype),
            pltpu.VMEM((1, row_count), jnp.int32),
            pltpu.VMEM((1, row_count), jnp.int32),
            pltpu.SemaphoreType.DMA((7,)),
        ],
        cost_estimate=pl.CostEstimate(
            flops=2 * slots * row_count * width, bytes_accessed=2 << 20, transcendentals=0
        ),
        compiler_params=pltpu.CompilerParams(vmem_limit_bytes=56 * 1024 * 1024),
    )(states, task_ids.reshape(1, row_count), student_batch.reshape(1, row_count), *weights)
    blocks, weights = results[:owners], results[owners:]
    blocks = [blocks[0]] + [send(blocks[k], "teach", k) for k in range(1, owners)]
    rows, act, slope, tags, counts, own, *outgoing = pl.pallas_call(
        functools.partial(forward_body, owners, local, room, parts),
        out_shape=[
            jax.ShapeDtypeStruct((slots, width), bf16),
            jax.ShapeDtypeStruct((slots, units), bf16),
            jax.ShapeDtypeStruct((slots, units), f32),
            jax.ShapeDtypeStruct((slots, extra), f32),
            jax.ShapeDtypeStruct((1, extra), f32),
        ]
        + [jax.ShapeDtypeStruct((height, actions), f32)] * parts,
        in_specs=[VMEM] * (owners + 4),
        out_specs=[VMEM] * (5 + parts),
        scratch_shapes=[pltpu.VMEM((slots, actions), f32)],
        cost_estimate=pl.CostEstimate(
            flops=2 * slots * 2 * width * (hidden + units), bytes_accessed=2 << 20, transcendentals=0
        ),
        compiler_params=pltpu.CompilerParams(vmem_limit_bytes=24 * 1024 * 1024),
    )(*blocks, *weights)
    mine = lax.axis_index("mdl")
    total = own
    for piece in [send(outgoing[k - 1], "mdl", k) for k in range(parts - 1, 0, -1)]:
        total = total + piece
    for other in [send(counts, "stud", k) for k in range(1, studs)]:
        counts = counts + other
    weight = jnp.sum(tags * jnp.where(counts > 0, 2.0 / counts, 0.0), axis=1)
    weight = lax.dynamic_index_in_dim(weight.reshape(parts, height), mine, 0, False)
    scaled = (total * weight[:, None]).astype(bf16)
    chunks = [scaled] + [send(scaled, "mdl", k) for k in range(1, parts)]
    grad_up, grad_down = pl.pallas_call(
        functools.partial(backward_body, parts),
        out_shape=[
            jax.ShapeDtypeStruct((width, units), f32),
            jax.ShapeDtypeStruct((actions, units), f32),
        ],
        in_specs=[VMEM] * (parts + 4),
        out_specs=[VMEM] * 2,
        scratch_shapes=[pltpu.VMEM((slots, actions), f32)],
        cost_estimate=pl.CostEstimate(
            flops=6 * slots * width * units, bytes_accessed=2 << 20, transcendentals=0
        ),
        compiler_params=pltpu.CompilerParams(vmem_limit_bytes=24 * 1024 * 1024),
    )(*chunks, rows, act, slope, weights[3])
    heights = (width // (owners * studs), actions // (owners * studs))

    def pieces(stud):
        return jnp.concatenate(
            [
                lax.dynamic_index_in_dim(g.reshape(owners, studs, h, units), stud, 1, False)
                for g, h in zip((grad_up, grad_down), heights)
            ],
            axis=1,
        )

    half = pieces(lax.axis_index("stud"))
    for k in range(1, studs):
        half = half + send(pieces(partner_to(studs, lax.axis_index("stud"), k)), "stud", k)
    me = lax.axis_index("teach")
    part = lax.dynamic_index_in_dim(half, me, 0, False)
    arrived = [
        send(lax.dynamic_index_in_dim(half, partner_to(owners, me, k), 0, False).astype(bf16), "teach", k)
        for k in range(1, owners)
    ]
    for piece in arrived:
        part = part + piece.astype(f32)
    return part[: heights[0]], part[heights[0] :]


def solution(mesh):
    in_specs = (
        P(("teach", "stud"), None),
        P(("teach", "stud"), None),
        P(("teach", "stud"), None),
        P("teach", None, "mdl"),
        P("teach", "mdl", None),
        P(None, "mdl"),
        P(None, "mdl"),
    )
    out_specs = (P(("teach", "stud"), "mdl"), P(("teach", "stud"), "mdl"))
    return jax.shard_map(
        on_device, mesh=mesh, in_specs=in_specs, out_specs=out_specs, check_vma=False
    )
```

```python
import functools

import jax
import jax.numpy as jnp
from jax import lax
from jax.experimental import pallas as pl
from jax.experimental.pallas import tpu as pltpu
from jax.sharding import PartitionSpec as P

LANES = 128
ROW_TILE = 16
PACK_ROWS = 16
PACK_TOP = 14.0
VMEM = pl.BlockSpec(memory_space=pltpu.VMEM)
HBM = pl.BlockSpec(memory_space=pltpu.HBM)


def up_to(value, step):
    return -(-value // step) * step


def is_power(size):
    return size & (size - 1) == 0


def partner_to(size, me, step):
    return me ^ step if is_power(size) else (me + step) % size


def partner_from(size, me, step):
    return me ^ step if is_power(size) else (me + size - step) % size


def send(block, axis, step):
    size = lax.axis_size(axis)
    return lax.ppermute(block, axis, [(i, partner_to(size, i, step)) for i in range(size)])


def pack(value):
    largest = jnp.max(jnp.abs(value))
    power = jnp.clip(jnp.ceil(jnp.log2(largest)), -100.0, 100.0)
    rows = jnp.broadcast_to(power, (PACK_ROWS, value.shape[1]))
    return jnp.concatenate([value * jnp.exp2(PACK_TOP - power), rows]).astype(jnp.float16)


def unpack(block):
    block = block.astype(jnp.float32)
    return block[:-PACK_ROWS] * jnp.exp2(block[-1:, :1] - PACK_TOP)


def dot(left, right, contract=((1,), (0,))):
    return lax.dot_general(left, right, (contract, ((), ())), preferred_element_type=jnp.float32)


def dispatch_body(owners, local, room, extra, *refs):
    sources, refs = refs[:3], refs[3:]
    weights, refs = refs[:4], refs[4:]
    outs, refs = refs[:owners], refs[owners:]
    weights_out, refs = refs[:4], refs[4:]
    states, task, batch, sems = refs
    rows, width = states.shape
    copies = [
        pltpu.make_async_copy(source, target, sems.at[i])
        for i, (source, target) in enumerate(
            zip((*sources, *weights), (states, task, batch, *weights_out))
        )
    ]
    for i in (1, 2, 0, 3, 4, 5, 6):
        copies[i].start()
    copies[1].wait()
    copies[2].wait()
    me = lax.axis_index("teach")
    task_list, batch_list = task[...], batch[...]
    group = up_to(owners * local, ROW_TILE)
    named = lax.broadcasted_iota(jnp.int32, (group, rows), 0) == task_list
    earlier = lax.broadcasted_iota(jnp.int32, (rows, rows), 0) < lax.broadcasted_iota(
        jnp.int32, (rows, rows), 1
    )
    named = named.astype(jnp.float32)
    before = dot(named.astype(jnp.bfloat16), earlier.astype(jnp.float32).astype(jnp.bfloat16))
    before = jnp.sum(before * named, axis=0, keepdims=True).astype(jnp.int32)
    owner = task_list // local if local > 1 else task_list
    step = owner ^ me if is_power(owners) else (owner - me + owners) % owners
    place = step * local + task_list % local if local > 1 else step
    slot = place * room + before
    index = lax.broadcasted_iota(jnp.int32, (owners * local * room, rows), 0)
    chosen = (index == slot).astype(jnp.float32)
    head = (index % (local * room) == 0).astype(jnp.float32)
    member = (lax.broadcasted_iota(jnp.int32, (extra, rows), 0) == batch_list).astype(jnp.float32)
    copies[0].wait()
    moved = dot(chosen.astype(jnp.bfloat16), states[...]).astype(jnp.bfloat16)
    tags = dot(
        (chosen + 2.0 * head).astype(jnp.bfloat16), member.astype(jnp.bfloat16), ((1,), (1,))
    ).astype(jnp.bfloat16)
    for k, out in enumerate(outs):
        span = slice(k * local * room, (k + 1) * local * room)
        out[:, :width] = moved[span]
        out[:, width:] = tags[span]
    for copy in copies[3:]:
        copy.wait()


def forward_body(owners, local, room, *refs):
    blocks, refs = refs[:owners], refs[owners:]
    teach_in, teach_out, student_up, student_down = refs[:4]
    rows_out, act_out, slope_out, tags_out, counts_out, *halves = refs[4:-1]
    error = refs[-1]
    width = student_up.shape[0]
    full = [block[...] for block in blocks]
    counts = None
    for block in full:
        mine = jnp.floor(block[:1, width:].astype(jnp.float32) * 0.5)
        counts = mine if counts is None else counts + mine
    counts_out[...] = counts
    for l in range(local):
        span = slice(l * owners * room, (l + 1) * owners * room)
        for k, block in enumerate(full):
            start = l * owners * room + k * room
            rows_out[start : start + room] = block[l * room : (l + 1) * room, :width]
            tag = block[l * room : (l + 1) * room, width:].astype(jnp.float32)
            if l == 0:
                head = lax.broadcasted_iota(jnp.int32, tag.shape, 0) == 0
                tag = jnp.where(head, tag - 2.0 * jnp.floor(tag * 0.5), tag)
            tags_out[start : start + room] = tag
        rows = rows_out[span]
        hidden = dot(rows, teach_in[l])
        hidden = (hidden / (1.0 + jnp.exp(-hidden))).astype(jnp.bfloat16)
        labels = dot(hidden, teach_out[l])
        pre = dot(rows, student_up[...])
        sig = 1.0 / (1.0 + jnp.exp(-pre))
        act = (pre * sig).astype(jnp.bfloat16)
        act_out[span] = act
        slope_out[span] = sig * (1.0 + pre * (1.0 - sig))
        error[span] = dot(act, student_down[...], ((1,), (1,))) - labels
    me = lax.axis_index("mdl")
    height = halves[0].shape[0]
    for k, out in enumerate(halves):
        out[...] = error[pl.ds(pl.multiple_of(((me & 1) ^ k) * height, 8), height)]


def backward_body(*refs):
    chunks, refs = refs[:2], refs[2:]
    rows, act, slope, student_down, grad_up, grad_down, scaled = refs
    me = lax.axis_index("mdl")
    height = chunks[0].shape[0]
    for k, chunk in enumerate(chunks):
        there = (me & 1) ^ k
        scaled[pl.ds(pl.multiple_of(there * height, 8), height)] = chunk[...].astype(jnp.float32)
    full = scaled[...].astype(jnp.bfloat16)
    grad_down[...] = dot(full, act[...], ((0,), (0,)))
    pre_grad = (dot(full, student_down[...]) * slope[...]).astype(jnp.bfloat16)
    grad_up[...] = dot(rows[...], pre_grad, ((0,), (0,)))


def on_device(states, task_ids, student_batch, teach_in, teach_out, student_up, student_down):
    row_count, width = states.shape
    owners, studs, parts = lax.axis_size("teach"), lax.axis_size("stud"), lax.axis_size("mdl")
    local, _, hidden = teach_in.shape
    actions = teach_out.shape[2]
    units = student_up.shape[1]
    teachers, batches = owners * local, owners * studs
    room = up_to(3 * row_count // (2 * teachers), ROW_TILE)
    extra = up_to(batches, LANES)
    slots = teachers * room
    height = slots // 2
    f32, bf16 = jnp.float32, jnp.bfloat16
    block = jax.ShapeDtypeStruct((local * room, width + extra), bf16)
    weights = (teach_in, teach_out, student_up, student_down)
    results = pl.pallas_call(
        functools.partial(dispatch_body, owners, local, room, extra),
        out_shape=[pltpu.VMEM(block.shape, bf16)] * owners + [pltpu.VMEM(w.shape, w.dtype) for w in weights],
        in_specs=[HBM] * 7,
        out_specs=[VMEM] * (owners + 4),
        scratch_shapes=[
            pltpu.VMEM(states.shape, states.dtype),
            pltpu.VMEM((1, row_count), jnp.int32),
            pltpu.VMEM((1, row_count), jnp.int32),
            pltpu.SemaphoreType.DMA((7,)),
        ],
        cost_estimate=pl.CostEstimate(
            flops=2 * slots * row_count * width, bytes_accessed=2 << 20, transcendentals=0
        ),
        compiler_params=pltpu.CompilerParams(vmem_limit_bytes=56 * 1024 * 1024),
    )(states, task_ids.reshape(1, row_count), student_batch.reshape(1, row_count), *weights)
    blocks, weights = results[:owners], results[owners:]
    blocks = [blocks[0]] + [send(blocks[k], "teach", k) for k in range(1, owners)]
    rows, act, slope, tags, counts, own, other = pl.pallas_call(
        functools.partial(forward_body, owners, local, room),
        out_shape=[
            jax.ShapeDtypeStruct((slots, width), bf16),
            jax.ShapeDtypeStruct((slots, units), bf16),
            jax.ShapeDtypeStruct((slots, units), f32),
            jax.ShapeDtypeStruct((slots, extra), f32),
            jax.ShapeDtypeStruct((1, extra), f32),
        ]
        + [jax.ShapeDtypeStruct((height, actions), f32)] * 2,
        in_specs=[VMEM] * (owners + 4),
        out_specs=[VMEM] * 7,
        scratch_shapes=[pltpu.VMEM((slots, actions), f32)],
        cost_estimate=pl.CostEstimate(
            flops=2 * slots * 2 * width * (hidden + units), bytes_accessed=2 << 20, transcendentals=0
        ),
        compiler_params=pltpu.CompilerParams(vmem_limit_bytes=24 * 1024 * 1024),
    )(*blocks, *weights)
    total = own + unpack(send(pack(other), "mdl", 1))
    step = 2
    while step < parts:
        total = total + unpack(send(pack(total), "mdl", step))
        step *= 2
    for piece in [send(counts, "stud", k) for k in range(1, studs)]:
        counts = counts + piece
    weight = jnp.sum(tags * jnp.where(counts > 0, 2.0 / counts, 0.0), axis=1)
    weight = lax.dynamic_index_in_dim(weight.reshape(2, height), lax.axis_index("mdl") & 1, 0, False)
    scaled = (total * weight[:, None]).astype(bf16)
    chunks = [scaled, send(scaled, "mdl", 1)]
    grad_up, grad_down = pl.pallas_call(
        backward_body,
        out_shape=[
            jax.ShapeDtypeStruct((width, units), f32),
            jax.ShapeDtypeStruct((actions, units), f32),
        ],
        in_specs=[VMEM] * 6,
        out_specs=[VMEM] * 2,
        scratch_shapes=[pltpu.VMEM((slots, actions), f32)],
        cost_estimate=pl.CostEstimate(
            flops=6 * slots * width * units, bytes_accessed=2 << 20, transcendentals=0
        ),
        compiler_params=pltpu.CompilerParams(vmem_limit_bytes=24 * 1024 * 1024),
    )(*chunks, rows, act, slope, weights[3])
    heights = (width // (owners * studs), actions // (owners * studs))

    def pieces(stud):
        return jnp.concatenate(
            [
                lax.dynamic_index_in_dim(g.reshape(owners, studs, h, units), stud, 1, False)
                for g, h in zip((grad_up, grad_down), heights)
            ],
            axis=1,
        )

    half = pieces(lax.axis_index("stud"))
    for k in range(1, studs):
        half = half + send(pieces(partner_to(studs, lax.axis_index("stud"), k)), "stud", k)
    me = lax.axis_index("teach")
    part = lax.dynamic_index_in_dim(half, me, 0, False)
    arrived = [
        send(lax.dynamic_index_in_dim(half, partner_to(owners, me, k), 0, False).astype(bf16), "teach", k)
        for k in range(1, owners)
    ]
    for piece in arrived:
        part = part + piece.astype(f32)
    return part[: heights[0]], part[heights[0] :]


def solution(mesh):
    in_specs = (
        P(("teach", "stud"), None),
        P(("teach", "stud"), None),
        P(("teach", "stud"), None),
        P("teach", None, "mdl"),
        P("teach", "mdl", None),
        P(None, "mdl"),
        P(None, "mdl"),
    )
    out_specs = (P(("teach", "stud"), "mdl"), P(("teach", "stud"), "mdl"))
    return jax.shard_map(
        on_device, mesh=mesh, in_specs=in_specs, out_specs=out_specs, check_vma=False
    )
```

```python
import functools

import jax
import jax.numpy as jnp
from jax import lax
from jax.experimental import pallas as pl
from jax.experimental.pallas import tpu as pltpu
from jax.sharding import PartitionSpec as P

LANES = 128
ROW_TILE = 16
PACK_ROWS = 8
PACK_TOP = 14.0
TINY = 1e-37
VMEM = pl.BlockSpec(memory_space=pltpu.VMEM)
HBM = pl.BlockSpec(memory_space=pltpu.HBM)


def up_to(value, step):
    return -(-value // step) * step


def is_power(size):
    return size & (size - 1) == 0


def partner_to(size, me, step):
    return me ^ step if is_power(size) else (me + step) % size


def partner_from(size, me, step):
    return me ^ step if is_power(size) else (me + size - step) % size


def send(block, axis, step):
    size = lax.axis_size(axis)
    return lax.ppermute(block, axis, [(i, partner_to(size, i, step)) for i in range(size)])


def pack(value, out):
    height = value.shape[0]
    largest = jnp.max(jnp.max(jnp.abs(value), axis=0, keepdims=True), axis=1, keepdims=True)
    power = jnp.clip(jnp.ceil(jnp.log2(jnp.maximum(largest, TINY))), -100.0, 100.0)
    out[:height] = value * jnp.exp2(PACK_TOP - power)
    out[height:] = jnp.broadcast_to(power, (PACK_ROWS, value.shape[1]))


def unpack(block):
    height = block.shape[0] - PACK_ROWS
    return block[:height] * jnp.exp2(block[height : height + 1, :1] - PACK_TOP)


def cross(block, step):
    return send(block.astype(jnp.float16), "mdl", step).astype(jnp.float32)


def dot(left, right, contract=((1,), (0,))):
    return lax.dot_general(left, right, (contract, ((), ())), preferred_element_type=jnp.float32)


def dispatch_body(owners, local, room, extra, *refs):
    sources, refs = refs[:3], refs[3:]
    weights, refs = refs[:4], refs[4:]
    outs, refs = refs[:owners], refs[owners:]
    weights_out, refs = refs[:4], refs[4:]
    states, task, batch, sems = refs
    rows, width = states.shape
    copies = [
        pltpu.make_async_copy(source, target, sems.at[i])
        for i, (source, target) in enumerate(
            zip((*sources, *weights), (states, task, batch, *weights_out))
        )
    ]
    for i in (1, 2, 0, 3, 4, 5, 6):
        copies[i].start()
    copies[1].wait()
    copies[2].wait()
    me = lax.axis_index("teach")
    task_list, batch_list = task[...], batch[...]
    group = up_to(owners * local, ROW_TILE)
    named = lax.broadcasted_iota(jnp.int32, (group, rows), 0) == task_list
    earlier = lax.broadcasted_iota(jnp.int32, (rows, rows), 0) < lax.broadcasted_iota(
        jnp.int32, (rows, rows), 1
    )
    named = named.astype(jnp.float32)
    before = dot(named.astype(jnp.bfloat16), earlier.astype(jnp.float32).astype(jnp.bfloat16))
    before = jnp.sum(before * named, axis=0, keepdims=True).astype(jnp.int32)
    owner = task_list // local if local > 1 else task_list
    step = owner ^ me if is_power(owners) else (owner - me + owners) % owners
    place = step * local + task_list % local if local > 1 else step
    slot = place * room + before
    index = lax.broadcasted_iota(jnp.int32, (owners * local * room, rows), 0)
    chosen = (index == slot).astype(jnp.float32)
    head = (index % (local * room) == 0).astype(jnp.float32)
    member = (lax.broadcasted_iota(jnp.int32, (extra, rows), 0) == batch_list).astype(jnp.float32)
    copies[0].wait()
    moved = dot(chosen.astype(jnp.bfloat16), states[...]).astype(jnp.bfloat16)
    tags = dot(
        (chosen + 2.0 * head).astype(jnp.bfloat16), member.astype(jnp.bfloat16), ((1,), (1,))
    ).astype(jnp.bfloat16)
    for k, out in enumerate(outs):
        span = slice(k * local * room, (k + 1) * local * room)
        out[:, :width] = moved[span]
        out[:, width:] = tags[span]
    for copy in copies[3:]:
        copy.wait()


def forward_body(owners, local, room, *refs):
    blocks, refs = refs[:owners], refs[owners:]
    teach_in, teach_out, student_up, student_down = refs[:4]
    rows_out, act_out, slope_out, tags_out, counts_out, own, other, error = refs[4:]
    width = student_up.shape[0]
    full = [block[...] for block in blocks]
    counts = None
    for block in full:
        mine = jnp.floor(block[:1, width:].astype(jnp.float32) * 0.5)
        counts = mine if counts is None else counts + mine
    counts_out[...] = counts
    for l in range(local):
        span = slice(l * owners * room, (l + 1) * owners * room)
        for k, block in enumerate(full):
            start = l * owners * room + k * room
            rows_out[start : start + room] = block[l * room : (l + 1) * room, :width]
            tag = block[l * room : (l + 1) * room, width:].astype(jnp.float32)
            if l == 0:
                head = lax.broadcasted_iota(jnp.int32, tag.shape, 0) == 0
                tag = jnp.where(head, tag - 2.0 * jnp.floor(tag * 0.5), tag)
            tags_out[start : start + room] = tag
        rows = rows_out[span]
        hidden = dot(rows, teach_in[l])
        hidden = (hidden / (1.0 + jnp.exp(-hidden))).astype(jnp.bfloat16)
        labels = dot(hidden, teach_out[l])
        pre = dot(rows, student_up[...])
        sig = 1.0 / (1.0 + jnp.exp(-pre))
        act = (pre * sig).astype(jnp.bfloat16)
        act_out[span] = act
        slope_out[span] = sig * (1.0 + pre * (1.0 - sig))
        error[span] = dot(act, student_down[...], ((1,), (1,))) - labels
    me = lax.axis_index("mdl")
    height = own.shape[0]
    own[...] = error[pl.ds(pl.multiple_of((me & 1) * height, 8), height)]
    pack(error[pl.ds(pl.multiple_of(((me & 1) ^ 1) * height, 8), height)], other)


def pair_body(own, arrived, total, packed):
    value = own[...] + unpack(arrived)
    total[...] = value
    pack(value, packed)


def scale_body(studs, *refs):
    own, arrived, tags = refs[:3]
    counts, scaled = refs[3:-1], refs[-1]
    all_counts = counts[0][...]
    for piece in counts[1:]:
        all_counts = all_counts + piece[...]
    height = own.shape[0]
    me = lax.axis_index("mdl")
    tag = tags[pl.ds(pl.multiple_of((me & 1) * height, 8), height)]
    inverse = jnp.where(all_counts > 0, 2.0 / all_counts, 0.0)
    weight = jnp.sum(tag * inverse, axis=1, keepdims=True)
    scaled[...] = ((own[...] + unpack(arrived)) * weight).astype(scaled.dtype)


def backward_body(*refs):
    chunks, refs = refs[:2], refs[2:]
    rows, act, slope, student_down, grad_up, grad_down, scaled = refs
    me = lax.axis_index("mdl")
    height = chunks[0].shape[0]
    for k, chunk in enumerate(chunks):
        there = (me & 1) ^ k
        scaled[pl.ds(pl.multiple_of(there * height, 8), height)] = chunk[...].astype(jnp.float32)
    full = scaled[...].astype(jnp.bfloat16)
    grad_down[...] = dot(full, act[...], ((0,), (0,)))
    pre_grad = (dot(full, student_down[...]) * slope[...]).astype(jnp.bfloat16)
    grad_up[...] = dot(rows[...], pre_grad, ((0,), (0,)))


def on_device(states, task_ids, student_batch, teach_in, teach_out, student_up, student_down):
    row_count, width = states.shape
    owners, studs, parts = lax.axis_size("teach"), lax.axis_size("stud"), lax.axis_size("mdl")
    local, _, hidden = teach_in.shape
    actions = teach_out.shape[2]
    units = student_up.shape[1]
    teachers, batches = owners * local, owners * studs
    room = up_to(3 * row_count // (2 * teachers), ROW_TILE)
    extra = up_to(batches, LANES)
    slots = teachers * room
    height = slots // 2
    f32, bf16 = jnp.float32, jnp.bfloat16
    half = jax.ShapeDtypeStruct((height, actions), f32)
    packed = jax.ShapeDtypeStruct((height + PACK_ROWS, actions), f32)
    block = jax.ShapeDtypeStruct((local * room, width + extra), bf16)
    weights = (teach_in, teach_out, student_up, student_down)
    results = pl.pallas_call(
        functools.partial(dispatch_body, owners, local, room, extra),
        out_shape=[pltpu.VMEM(block.shape, bf16)] * owners + [pltpu.VMEM(w.shape, w.dtype) for w in weights],
        in_specs=[HBM] * 7,
        out_specs=[VMEM] * (owners + 4),
        scratch_shapes=[
            pltpu.VMEM(states.shape, states.dtype),
            pltpu.VMEM((1, row_count), jnp.int32),
            pltpu.VMEM((1, row_count), jnp.int32),
            pltpu.SemaphoreType.DMA((7,)),
        ],
        cost_estimate=pl.CostEstimate(
            flops=2 * slots * row_count * width, bytes_accessed=2 << 20, transcendentals=0
        ),
        compiler_params=pltpu.CompilerParams(vmem_limit_bytes=56 * 1024 * 1024),
    )(states, task_ids.reshape(1, row_count), student_batch.reshape(1, row_count), *weights)
    blocks, weights = results[:owners], results[owners:]
    blocks = [blocks[0]] + [send(blocks[k], "teach", k) for k in range(1, owners)]
    rows, act, slope, tags, counts, own, other = pl.pallas_call(
        functools.partial(forward_body, owners, local, room),
        out_shape=[
            jax.ShapeDtypeStruct((slots, width), bf16),
            jax.ShapeDtypeStruct((slots, units), bf16),
            jax.ShapeDtypeStruct((slots, units), f32),
            jax.ShapeDtypeStruct((slots, extra), f32),
            jax.ShapeDtypeStruct((1, extra), f32),
        ]
        + [half, packed],
        in_specs=[VMEM] * (owners + 4),
        out_specs=[VMEM] * 7,
        scratch_shapes=[pltpu.VMEM((slots, actions), f32)],
        cost_estimate=pl.CostEstimate(
            flops=2 * slots * 2 * width * (hidden + units), bytes_accessed=2 << 20, transcendentals=0
        ),
        compiler_params=pltpu.CompilerParams(vmem_limit_bytes=24 * 1024 * 1024),
    )(*blocks, *weights)
    step = 2
    arrived = cross(other, 1)
    while step < parts:
        own, other = pl.pallas_call(
            pair_body, out_shape=[half, packed], in_specs=[VMEM] * 2, out_specs=[VMEM] * 2
        )(own, arrived)
        arrived = cross(other, step)
        step *= 2
    counts = [counts] + [send(counts, "stud", k) for k in range(1, studs)]
    scaled = pl.pallas_call(
        functools.partial(scale_body, studs),
        out_shape=jax.ShapeDtypeStruct((height, actions), bf16),
        in_specs=[VMEM] * (3 + studs),
        out_specs=VMEM,
    )(own, arrived, tags, *counts)
    chunks = [scaled, send(scaled, "mdl", 1)]
    grad_up, grad_down = pl.pallas_call(
        backward_body,
        out_shape=[
            jax.ShapeDtypeStruct((width, units), f32),
            jax.ShapeDtypeStruct((actions, units), f32),
        ],
        in_specs=[VMEM] * 6,
        out_specs=[VMEM] * 2,
        scratch_shapes=[pltpu.VMEM((slots, actions), f32)],
        cost_estimate=pl.CostEstimate(
            flops=6 * slots * width * units, bytes_accessed=2 << 20, transcendentals=0
        ),
        compiler_params=pltpu.CompilerParams(vmem_limit_bytes=24 * 1024 * 1024),
    )(*chunks, rows, act, slope, weights[3])
    heights = (width // (owners * studs), actions // (owners * studs))

    def pieces(stud):
        return jnp.concatenate(
            [
                lax.dynamic_index_in_dim(g.reshape(owners, studs, h, units), stud, 1, False)
                for g, h in zip((grad_up, grad_down), heights)
            ],
            axis=1,
        )

    half = pieces(lax.axis_index("stud"))
    for k in range(1, studs):
        half = half + send(pieces(partner_to(studs, lax.axis_index("stud"), k)), "stud", k)
    me = lax.axis_index("teach")
    part = lax.dynamic_index_in_dim(half, me, 0, False)
    arrived = [
        send(lax.dynamic_index_in_dim(half, partner_to(owners, me, k), 0, False).astype(bf16), "teach", k)
        for k in range(1, owners)
    ]
    for piece in arrived:
        part = part + piece.astype(f32)
    return part[: heights[0]], part[heights[0] :]


def solution(mesh):
    in_specs = (
        P(("teach", "stud"), None),
        P(("teach", "stud"), None),
        P(("teach", "stud"), None),
        P("teach", None, "mdl"),
        P("teach", "mdl", None),
        P(None, "mdl"),
        P(None, "mdl"),
    )
    out_specs = (P(("teach", "stud"), "mdl"), P(("teach", "stud"), "mdl"))
    return jax.shard_map(
        on_device, mesh=mesh, in_specs=in_specs, out_specs=out_specs, check_vma=False
    )
```

```python
import functools

import jax
import jax.numpy as jnp
from jax import lax
from jax.experimental import pallas as pl
from jax.experimental.pallas import tpu as pltpu
from jax.sharding import PartitionSpec as P

LANES = 128
ROW_TILE = 16
PACK_ROWS = 8
PACK_TOP = 14.0
TINY = 1e-37
VMEM = pl.BlockSpec(memory_space=pltpu.VMEM)
HBM = pl.BlockSpec(memory_space=pltpu.HBM)
SMALL = pltpu.CompilerParams(vmem_limit_bytes=16 * 1024 * 1024)


def up_to(value, step):
    return -(-value // step) * step


def is_power(size):
    return size & (size - 1) == 0


def partner_to(size, me, step):
    return me ^ step if is_power(size) else (me + step) % size


def partner_from(size, me, step):
    return me ^ step if is_power(size) else (me + size - step) % size


def send(block, axis, step):
    size = lax.axis_size(axis)
    return lax.ppermute(block, axis, [(i, partner_to(size, i, step)) for i in range(size)])


def pack(value, out):
    height = value.shape[0]
    largest = jnp.max(jnp.max(jnp.abs(value), axis=0, keepdims=True), axis=1, keepdims=True)
    power = jnp.clip(jnp.ceil(jnp.log2(jnp.maximum(largest, TINY))), -100.0, 100.0)
    out[:height] = value * jnp.exp2(PACK_TOP - power)
    out[height:] = jnp.broadcast_to(power, (PACK_ROWS, value.shape[1]))


def unpack(block):
    height = block.shape[0] - PACK_ROWS
    return block[:height] * jnp.exp2(block[height : height + 1, :1] - PACK_TOP)


def cross(block, step):
    return send(block.astype(jnp.float16), "mdl", step).astype(jnp.float32)


def dot(left, right, contract=((1,), (0,))):
    return lax.dot_general(left, right, (contract, ((), ())), preferred_element_type=jnp.float32)


def dispatch_body(owners, local, room, extra, *refs):
    sources, refs = refs[:3], refs[3:]
    weights, refs = refs[:4], refs[4:]
    outs, refs = refs[:owners], refs[owners:]
    weights_out, refs = refs[:4], refs[4:]
    states, task, batch, sems = refs
    rows, width = states.shape
    copies = [
        pltpu.make_async_copy(source, target, sems.at[i])
        for i, (source, target) in enumerate(
            zip((*sources, *weights), (states, task, batch, *weights_out))
        )
    ]
    for i in (1, 2, 0, 3, 4, 5, 6):
        copies[i].start()
    copies[1].wait()
    copies[2].wait()
    me = lax.axis_index("teach")
    task_list, batch_list = task[...], batch[...]
    group = up_to(owners * local, ROW_TILE)
    named = lax.broadcasted_iota(jnp.int32, (group, rows), 0) == task_list
    earlier = lax.broadcasted_iota(jnp.int32, (rows, rows), 0) < lax.broadcasted_iota(
        jnp.int32, (rows, rows), 1
    )
    named = named.astype(jnp.float32)
    before = dot(named.astype(jnp.bfloat16), earlier.astype(jnp.float32).astype(jnp.bfloat16))
    before = jnp.sum(before * named, axis=0, keepdims=True).astype(jnp.int32)
    owner = task_list // local if local > 1 else task_list
    step = owner ^ me if is_power(owners) else (owner - me + owners) % owners
    place = step * local + task_list % local if local > 1 else step
    slot = place * room + before
    index = lax.broadcasted_iota(jnp.int32, (owners * local * room, rows), 0)
    chosen = (index == slot).astype(jnp.float32)
    head = (index % (local * room) == 0).astype(jnp.float32)
    member = (lax.broadcasted_iota(jnp.int32, (extra, rows), 0) == batch_list).astype(jnp.float32)
    copies[0].wait()
    moved = dot(chosen.astype(jnp.bfloat16), states[...]).astype(jnp.bfloat16)
    tags = dot(
        (chosen + 2.0 * head).astype(jnp.bfloat16), member.astype(jnp.bfloat16), ((1,), (1,))
    ).astype(jnp.bfloat16)
    for k, out in enumerate(outs):
        span = slice(k * local * room, (k + 1) * local * room)
        out[:, :width] = moved[span]
        out[:, width:] = tags[span]
    for copy in copies[3:]:
        copy.wait()


def forward_body(owners, local, room, *refs):
    blocks, refs = refs[:owners], refs[owners:]
    teach_in, teach_out, student_up, student_down = refs[:4]
    rows_out, act_out, slope_out, tags_out, counts_out, own, other, error = refs[4:]
    width = student_up.shape[0]
    full = [block[...] for block in blocks]
    counts = None
    for block in full:
        mine = jnp.floor(block[:1, width:].astype(jnp.float32) * 0.5)
        counts = mine if counts is None else counts + mine
    counts_out[...] = counts
    for l in range(local):
        span = slice(l * owners * room, (l + 1) * owners * room)
        for k, block in enumerate(full):
            start = l * owners * room + k * room
            rows_out[start : start + room] = block[l * room : (l + 1) * room, :width]
            tag = block[l * room : (l + 1) * room, width:].astype(jnp.float32)
            if l == 0:
                head = lax.broadcasted_iota(jnp.int32, tag.shape, 0) == 0
                tag = jnp.where(head, tag - 2.0 * jnp.floor(tag * 0.5), tag)
            tags_out[start : start + room] = tag
        rows = rows_out[span]
        hidden = dot(rows, teach_in[l])
        hidden = (hidden / (1.0 + jnp.exp(-hidden))).astype(jnp.bfloat16)
        labels = dot(hidden, teach_out[l])
        pre = dot(rows, student_up[...])
        sig = 1.0 / (1.0 + jnp.exp(-pre))
        act = (pre * sig).astype(jnp.bfloat16)
        act_out[span] = act
        slope_out[span] = sig * (1.0 + pre * (1.0 - sig))
        error[span] = dot(act, student_down[...], ((1,), (1,))) - labels
    me = lax.axis_index("mdl")
    height = own.shape[0]
    own[...] = error[pl.ds(pl.multiple_of((me & 1) * height, 8), height)]
    pack(error[pl.ds(pl.multiple_of(((me & 1) ^ 1) * height, 8), height)], other)


def pair_body(own, arrived, total, packed):
    value = own[...] + unpack(arrived)
    total[...] = value
    pack(value, packed)


def scale_body(studs, *refs):
    own, arrived, tags = refs[:3]
    counts, scaled = refs[3:-1], refs[-1]
    all_counts = counts[0][...]
    for piece in counts[1:]:
        all_counts = all_counts + piece[...]
    height = own.shape[0]
    me = lax.axis_index("mdl")
    tag = tags[pl.ds(pl.multiple_of((me & 1) * height, 8), height)]
    inverse = jnp.where(all_counts > 0, 2.0 / all_counts, 0.0)
    weight = jnp.sum(tag * inverse, axis=1, keepdims=True)
    scaled[...] = ((own[...] + unpack(arrived)) * weight).astype(scaled.dtype)


def backward_body(*refs):
    chunks, refs = refs[:2], refs[2:]
    rows, act, slope, student_down, grad_up, grad_down, scaled = refs
    me = lax.axis_index("mdl")
    height = chunks[0].shape[0]
    for k, chunk in enumerate(chunks):
        there = (me & 1) ^ k
        scaled[pl.ds(pl.multiple_of(there * height, 8), height)] = chunk[...].astype(jnp.float32)
    full = scaled[...].astype(jnp.bfloat16)
    grad_down[...] = dot(full, act[...], ((0,), (0,)))
    pre_grad = (dot(full, student_down[...]) * slope[...]).astype(jnp.bfloat16)
    grad_up[...] = dot(rows[...], pre_grad, ((0,), (0,)))


def on_device(states, task_ids, student_batch, teach_in, teach_out, student_up, student_down):
    row_count, width = states.shape
    owners, studs, parts = lax.axis_size("teach"), lax.axis_size("stud"), lax.axis_size("mdl")
    local, _, hidden = teach_in.shape
    actions = teach_out.shape[2]
    units = student_up.shape[1]
    teachers, batches = owners * local, owners * studs
    room = up_to(3 * row_count // (2 * teachers), ROW_TILE)
    extra = up_to(batches, LANES)
    slots = teachers * room
    height = slots // 2
    f32, bf16 = jnp.float32, jnp.bfloat16
    half = jax.ShapeDtypeStruct((height, actions), f32)
    packed = jax.ShapeDtypeStruct((height + PACK_ROWS, actions), f32)
    block = jax.ShapeDtypeStruct((local * room, width + extra), bf16)
    weights = (teach_in, teach_out, student_up, student_down)
    results = pl.pallas_call(
        functools.partial(dispatch_body, owners, local, room, extra),
        out_shape=[pltpu.VMEM(block.shape, bf16)] * owners + [pltpu.VMEM(w.shape, w.dtype) for w in weights],
        in_specs=[HBM] * 7,
        out_specs=[VMEM] * (owners + 4),
        scratch_shapes=[
            pltpu.VMEM(states.shape, states.dtype),
            pltpu.VMEM((1, row_count), jnp.int32),
            pltpu.VMEM((1, row_count), jnp.int32),
            pltpu.SemaphoreType.DMA((7,)),
        ],
        cost_estimate=pl.CostEstimate(
            flops=2 * slots * row_count * width, bytes_accessed=2 << 20, transcendentals=0
        ),
        compiler_params=pltpu.CompilerParams(vmem_limit_bytes=56 * 1024 * 1024),
    )(states, task_ids.reshape(1, row_count), student_batch.reshape(1, row_count), *weights)
    blocks, weights = results[:owners], results[owners:]
    blocks = [blocks[0]] + [send(blocks[k], "teach", k) for k in range(1, owners)]
    rows, act, slope, tags, counts, own, other = pl.pallas_call(
        functools.partial(forward_body, owners, local, room),
        out_shape=[
            jax.ShapeDtypeStruct((slots, width), bf16),
            jax.ShapeDtypeStruct((slots, units), bf16),
            jax.ShapeDtypeStruct((slots, units), f32),
            jax.ShapeDtypeStruct((slots, extra), f32),
            jax.ShapeDtypeStruct((1, extra), f32),
        ]
        + [half, packed],
        in_specs=[VMEM] * (owners + 4),
        out_specs=[VMEM] * 7,
        scratch_shapes=[pltpu.VMEM((slots, actions), f32)],
        cost_estimate=pl.CostEstimate(
            flops=2 * slots * 2 * width * (hidden + units), bytes_accessed=2 << 20, transcendentals=0
        ),
        compiler_params=SMALL,
    )(*blocks, *weights)
    step = 2
    arrived = cross(other, 1)
    while step < parts:
        own, other = pl.pallas_call(
            pair_body,
            out_shape=[half, packed],
            in_specs=[VMEM] * 2,
            out_specs=[VMEM] * 2,
            compiler_params=SMALL,
        )(own, arrived)
        arrived = cross(other, step)
        step *= 2
    counts = [counts] + [send(counts, "stud", k) for k in range(1, studs)]
    scaled = pl.pallas_call(
        functools.partial(scale_body, studs),
        out_shape=jax.ShapeDtypeStruct((height, actions), bf16),
        in_specs=[VMEM] * (3 + studs),
        out_specs=VMEM,
        compiler_params=SMALL,
    )(own, arrived, tags, *counts)
    chunks = [scaled, send(scaled, "mdl", 1)]
    grad_up, grad_down = pl.pallas_call(
        backward_body,
        out_shape=[
            jax.ShapeDtypeStruct((width, units), f32),
            jax.ShapeDtypeStruct((actions, units), f32),
        ],
        in_specs=[VMEM] * 6,
        out_specs=[VMEM] * 2,
        scratch_shapes=[pltpu.VMEM((slots, actions), f32)],
        cost_estimate=pl.CostEstimate(
            flops=6 * slots * width * units, bytes_accessed=2 << 20, transcendentals=0
        ),
        compiler_params=SMALL,
    )(*chunks, rows, act, slope, weights[3])
    heights = (width // (owners * studs), actions // (owners * studs))

    def pieces(stud):
        return jnp.concatenate(
            [
                lax.dynamic_index_in_dim(g.reshape(owners, studs, h, units), stud, 1, False)
                for g, h in zip((grad_up, grad_down), heights)
            ],
            axis=1,
        )

    half = pieces(lax.axis_index("stud"))
    for k in range(1, studs):
        half = half + send(pieces(partner_to(studs, lax.axis_index("stud"), k)), "stud", k)
    me = lax.axis_index("teach")
    part = lax.dynamic_index_in_dim(half, me, 0, False)
    arrived = [
        send(lax.dynamic_index_in_dim(half, partner_to(owners, me, k), 0, False).astype(bf16), "teach", k)
        for k in range(1, owners)
    ]
    for piece in arrived:
        part = part + piece.astype(f32)
    return part[: heights[0]], part[heights[0] :]


def solution(mesh):
    in_specs = (
        P(("teach", "stud"), None),
        P(("teach", "stud"), None),
        P(("teach", "stud"), None),
        P("teach", None, "mdl"),
        P("teach", "mdl", None),
        P(None, "mdl"),
        P(None, "mdl"),
    )
    out_specs = (P(("teach", "stud"), "mdl"), P(("teach", "stud"), "mdl"))
    return jax.shard_map(
        on_device, mesh=mesh, in_specs=in_specs, out_specs=out_specs, check_vma=False
    )
```

```python
import functools

import jax
import jax.numpy as jnp
from jax import lax
from jax.experimental import pallas as pl
from jax.experimental.pallas import tpu as pltpu
from jax.sharding import PartitionSpec as P

LANES = 128
ROW_TILE = 16
PACK_ROWS = 8
PACK_TOP = 14.0
TINY = 1e-37
VMEM = pl.BlockSpec(memory_space=pltpu.VMEM)
HBM = pl.BlockSpec(memory_space=pltpu.HBM)
SMALL = pltpu.CompilerParams(vmem_limit_bytes=16 * 1024 * 1024)
LARGE = pltpu.CompilerParams(vmem_limit_bytes=56 * 1024 * 1024)


def up_to(value, step):
    return -(-value // step) * step


def is_power(size):
    return size & (size - 1) == 0


def partner_to(size, me, step):
    return me ^ step if is_power(size) else (me + step) % size


def partner_from(size, me, step):
    return me ^ step if is_power(size) else (me + size - step) % size


def send(block, axis, step):
    size = lax.axis_size(axis)
    return lax.ppermute(block, axis, [(i, partner_to(size, i, step)) for i in range(size)])


def pack(value, out):
    height = value.shape[0]
    largest = jnp.max(jnp.max(jnp.abs(value), axis=0, keepdims=True), axis=1, keepdims=True)
    power = jnp.clip(jnp.ceil(jnp.log2(jnp.maximum(largest, TINY))), -100.0, 100.0)
    out[:height] = value * jnp.exp2(PACK_TOP - power)
    out[height:] = jnp.broadcast_to(power, (PACK_ROWS, value.shape[1]))


def unpack(block):
    height = block.shape[0] - PACK_ROWS
    return block[:height] * jnp.exp2(block[height : height + 1, :1] - PACK_TOP)


def cross(block, step):
    return send(block.astype(jnp.float16), "mdl", step).astype(jnp.float32)


def dot(left, right, contract=((1,), (0,))):
    return lax.dot_general(left, right, (contract, ((), ())), preferred_element_type=jnp.float32)


def dispatch_body(owners, local, room, extra, *refs):
    sources, refs = refs[:3], refs[3:]
    outs, refs = refs[:owners], refs[owners:]
    states, task, batch, sems = refs
    rows, width = states.shape
    copies = [
        pltpu.make_async_copy(source, target, sems.at[i])
        for i, (source, target) in enumerate(zip(sources, (states, task, batch)))
    ]
    for i in (1, 2, 0):
        copies[i].start()
    copies[1].wait()
    copies[2].wait()
    me = lax.axis_index("teach")
    task_list, batch_list = task[...], batch[...]
    group = up_to(owners * local, ROW_TILE)
    named = lax.broadcasted_iota(jnp.int32, (group, rows), 0) == task_list
    earlier = lax.broadcasted_iota(jnp.int32, (rows, rows), 0) < lax.broadcasted_iota(
        jnp.int32, (rows, rows), 1
    )
    named = named.astype(jnp.float32)
    before = dot(named.astype(jnp.bfloat16), earlier.astype(jnp.float32).astype(jnp.bfloat16))
    before = jnp.sum(before * named, axis=0, keepdims=True).astype(jnp.int32)
    owner = task_list // local if local > 1 else task_list
    step = owner ^ me if is_power(owners) else (owner - me + owners) % owners
    place = step * local + task_list % local if local > 1 else step
    slot = place * room + before
    index = lax.broadcasted_iota(jnp.int32, (owners * local * room, rows), 0)
    chosen = (index == slot).astype(jnp.float32)
    head = (index % (local * room) == 0).astype(jnp.float32)
    member = (lax.broadcasted_iota(jnp.int32, (extra, rows), 0) == batch_list).astype(jnp.float32)
    tags = dot(
        (chosen + 2.0 * head).astype(jnp.bfloat16), member.astype(jnp.bfloat16), ((1,), (1,))
    ).astype(jnp.bfloat16)
    copies[0].wait()
    moved = dot(chosen.astype(jnp.bfloat16), states[...]).astype(jnp.bfloat16)
    for k, out in enumerate(outs):
        span = slice(k * local * room, (k + 1) * local * room)
        out[:, :width] = moved[span]
        out[:, width:] = tags[span]


def weights_body(*refs):
    sources, outs, sems = refs[1:5], refs[5:9], refs[9]
    copies = [
        pltpu.make_async_copy(source, target, sems.at[i])
        for i, (source, target) in enumerate(zip(sources, outs))
    ]
    for copy in copies:
        copy.start()
    for copy in copies:
        copy.wait()


def student(rows, student_up):
    pre = dot(rows, student_up[...])
    sig = 1.0 / (1.0 + jnp.exp(-pre))
    return (pre * sig).astype(jnp.bfloat16), sig * (1.0 + pre * (1.0 - sig))


def half_error(local, first, rows, weights, act_out, slope_out):
    teach_in, teach_out, student_up, student_down = weights
    per_teacher = 2 * rows.shape[0] // local
    labels = None
    for l in range(local):
        hidden = dot(rows, teach_in[l])
        hidden = hidden / (1.0 + jnp.exp(-hidden))
        if local > 1:
            index = first + lax.broadcasted_iota(jnp.int32, hidden.shape, 0)
            hidden = jnp.where(index // per_teacher == l, hidden, 0.0)
        part = dot(hidden.astype(jnp.bfloat16), teach_out[l])
        labels = part if labels is None else labels + part
    act, slope = student(rows, student_up)
    act_out[...] = act
    slope_out[...] = slope
    return dot(act, student_down[...], ((1,), (1,))) - labels


def half_start(height, other):
    me = lax.axis_index("mdl")
    return pl.multiple_of(((me & 1) ^ other) * height, ROW_TILE)


def forward_other_body(owners, local, room, *refs):
    blocks, refs = refs[:owners], refs[owners:]
    weights, refs = refs[:4], refs[4:]
    rows_own, rows_other, tags_out, counts_out, packed, act, slope, rows_all, tags_all = refs
    width = rows_own.shape[1]
    full = [block[...] for block in blocks]
    counts = None
    for block in full:
        mine = jnp.floor(block[:1, width:].astype(jnp.float32) * 0.5)
        counts = mine if counts is None else counts + mine
    counts_out[...] = counts
    for l in range(local):
        for k, block in enumerate(full):
            start = (l * owners + k) * room
            rows_all[start : start + room] = block[l * room : (l + 1) * room, :width]
            tag = block[l * room : (l + 1) * room, width:].astype(jnp.float32)
            if l == 0:
                head = lax.broadcasted_iota(jnp.int32, tag.shape, 0) == 0
                tag = jnp.where(head, tag - 2.0 * jnp.floor(tag * 0.5), tag)
            tags_all[start : start + room] = tag
    height = rows_own.shape[0]
    mine, there = half_start(height, 0), half_start(height, 1)
    rows_own[...] = rows_all[pl.ds(mine, height)]
    tags_out[...] = tags_all[pl.ds(mine, height)]
    rows = rows_all[pl.ds(there, height)]
    rows_other[...] = rows
    pack(half_error(local, there, rows, weights, act, slope), packed)


def forward_own_body(local, rows, *refs):
    weights, (error, act, slope) = refs[:4], refs[4:]
    first = half_start(rows.shape[0], 0)
    error[...] = half_error(local, first, rows[...], weights, act, slope)


def neighbour_body(rows_own, rows_other, student_up, act_own, slope_own, act_other, slope_other):
    act_own[...], slope_own[...] = student(rows_own[...], student_up)
    act_other[...], slope_other[...] = student(rows_other[...], student_up)


def pair_body(own, arrived, total, packed):
    value = own[...] + unpack(arrived)
    total[...] = value
    pack(value, packed)


def scale_body(*refs):
    own, arrived, tags = refs[:3]
    counts, scaled = refs[3:-1], refs[-1]
    all_counts = counts[0][...]
    for piece in counts[1:]:
        all_counts = all_counts + piece[...]
    inverse = jnp.where(all_counts > 0, 2.0 / all_counts, 0.0)
    weight = jnp.sum(tags[...] * inverse, axis=1, keepdims=True)
    scaled[...] = ((own[...] + unpack(arrived)) * weight).astype(scaled.dtype)


def backward_body(first, groups, *refs):
    student_down, refs = refs[0], refs[1:]
    grad_up, grad_down = refs[-2:]
    if first:
        up, down = None, None
    else:
        up, down = refs[4 * groups][...], refs[4 * groups + 1][...]
    for i in range(groups):
        scaled, rows, act, slope = refs[4 * i : 4 * i + 4]
        error = scaled[...]
        part = dot(error, act[...], ((0,), (0,)))
        down = part if down is None else down + part
        pre_grad = (dot(error, student_down[...]) * slope[...]).astype(jnp.bfloat16)
        part = dot(rows[...], pre_grad, ((0,), (0,)))
        up = part if up is None else up + part
    grad_up[...] = up
    grad_down[...] = down


def kernel(body, outs, operands, flops, scratch=(), params=SMALL, places=None):
    return pl.pallas_call(
        body,
        out_shape=outs,
        in_specs=places or [VMEM] * len(operands),
        out_specs=[VMEM] * len(outs),
        scratch_shapes=list(scratch),
        cost_estimate=pl.CostEstimate(flops=flops, bytes_accessed=1 << 18, transcendentals=0),
        compiler_params=params,
    )(*operands)


def on_device(states, task_ids, student_batch, teach_in, teach_out, student_up, student_down):
    row_count, width = states.shape
    owners, studs, parts = lax.axis_size("teach"), lax.axis_size("stud"), lax.axis_size("mdl")
    local, _, hidden = teach_in.shape
    actions = teach_out.shape[2]
    units = student_up.shape[1]
    teachers, batches = owners * local, owners * studs
    room = up_to(3 * row_count // (2 * teachers), ROW_TILE)
    extra = up_to(batches, LANES)
    slots = teachers * room
    height = slots // 2
    f32, bf16 = jnp.float32, jnp.bfloat16

    def shape(rows, columns, dtype):
        return jax.ShapeDtypeStruct((rows, columns), dtype)

    half, packed = shape(height, actions, f32), shape(height + PACK_ROWS, actions, f32)
    half_rows = shape(height, width, bf16)
    half_act, half_slope = shape(height, units, bf16), shape(height, units, f32)
    tokens = [ids.reshape(1, row_count) for ids in (task_ids, student_batch)]
    blocks = kernel(
        functools.partial(dispatch_body, owners, local, room, extra),
        [pltpu.VMEM((local * room, width + extra), bf16)] * owners,
        (states, *tokens),
        2 * slots * row_count * width,
        [pltpu.VMEM(a.shape, a.dtype) for a in (states, *tokens)] + [pltpu.SemaphoreType.DMA((3,))],
        LARGE,
        [HBM] * 3,
    )
    arrived = {k: send(blocks[k], "teach", k) for k in range(owners - 1, 0, -1)}
    weights = (teach_in, teach_out, student_up, student_down)
    weights = kernel(
        weights_body,
        [pltpu.VMEM(w.shape, w.dtype) for w in weights],
        (blocks[0], *[pltpu.with_memory_space_constraint(w, pltpu.HBM) for w in weights]),
        0,
        [pltpu.SemaphoreType.DMA((4,))],
        SMALL,
        [VMEM] + [HBM] * 4,
    )
    blocks = [blocks[0]] + [arrived[k] for k in range(1, owners)]
    work = 2 * height * 2 * width * (hidden + units)
    rows_own, rows_other, tags, counts, other, act_other, slope_other = kernel(
        functools.partial(forward_other_body, owners, local, room),
        [half_rows, half_rows, shape(height, extra, f32), shape(1, extra, f32), packed]
        + [half_act, half_slope],
        (*blocks, *weights),
        work,
        [pltpu.VMEM((slots, width), bf16), pltpu.VMEM((slots, extra), f32)],
    )
    arrived = cross(other, 1)
    own, act_own, slope_own = kernel(
        functools.partial(forward_own_body, local),
        [half, half_act, half_slope],
        (rows_own, *weights),
        work,
    )
    all_counts, mates = [counts], []
    for k in range(1, studs):
        all_counts.append(send(counts, "stud", k))
        mates.append((send(rows_own, "stud", k), send(rows_other, "stud", k)))
    own, arrived, all_counts, mates = lax.optimization_barrier((own, arrived, all_counts, mates))
    step = 2
    while step < parts:
        own, other = kernel(pair_body, [half, packed], (own, arrived), 0)
        arrived = cross(other, step)
        step *= 2
    groups = [(rows_own, act_own, slope_own, rows_other, act_other, slope_other)]
    for first, second in mates:
        known = kernel(
            neighbour_body,
            [half_act, half_slope] * 2,
            (first, second, weights[2]),
            4 * height * width * units,
        )
        groups.append((first, *known[:2], second, *known[2:]))
    own, arrived, groups = lax.optimization_barrier((own, arrived, groups))
    (scaled,) = kernel(scale_body, [shape(height, actions, bf16)], (own, arrived, tags, *all_counts), 0)
    from_pair = send(scaled, "mdl", 1)
    ours = [scaled] + [send(scaled, "stud", k) for k in range(1, studs)]
    work = 6 * height * width * units
    grads = [shape(width, units, f32), shape(actions, units, f32)]
    sums = kernel(
        functools.partial(backward_body, True, studs),
        grads,
        [weights[3]] + [a for s, g in zip(ours, groups) for a in (s, *g[:3])],
        studs * work,
    )
    from_pair, sums = lax.optimization_barrier((from_pair, sums))
    for k in range(studs):
        theirs = send(from_pair, "stud", k) if k else from_pair
        sums = kernel(
            functools.partial(backward_body, False, 1),
            grads,
            (weights[3], theirs, *groups[k][3:], *sums),
            work,
        )
    grad_up, grad_down = sums
    heights = (width // (owners * studs), actions // (owners * studs))

    def pieces(stud):
        return jnp.concatenate(
            [
                lax.dynamic_index_in_dim(g.reshape(owners, studs, h, units), stud, 1, False)
                for g, h in zip((grad_up, grad_down), heights)
            ],
            axis=1,
        )

    half = pieces(lax.axis_index("stud"))
    me = lax.axis_index("teach")
    part = lax.dynamic_index_in_dim(half, me, 0, False)
    arrived = [
        send(lax.dynamic_index_in_dim(half, partner_to(owners, me, k), 0, False).astype(bf16), "teach", k)
        for k in range(owners - 1, 0, -1)
    ]
    for piece in arrived:
        part = part + piece.astype(f32)
    return part[: heights[0]], part[heights[0] :]


def solution(mesh):
    in_specs = (
        P(("teach", "stud"), None),
        P(("teach", "stud"), None),
        P(("teach", "stud"), None),
        P("teach", None, "mdl"),
        P("teach", "mdl", None),
        P(None, "mdl"),
        P(None, "mdl"),
    )
    out_specs = (P(("teach", "stud"), "mdl"), P(("teach", "stud"), "mdl"))
    return jax.shard_map(
        on_device, mesh=mesh, in_specs=in_specs, out_specs=out_specs, check_vma=False
    )
```

```python
import functools

import jax
import jax.numpy as jnp
from jax import lax
from jax.experimental import pallas as pl
from jax.experimental.pallas import tpu as pltpu
from jax.sharding import PartitionSpec as P

LANES = 128
ROW_TILE = 16
PACK_ROWS = 8
PACK_TOP = 14.0
TINY = 1e-37
VMEM = pl.BlockSpec(memory_space=pltpu.VMEM)
HBM = pl.BlockSpec(memory_space=pltpu.HBM)
SMALL = pltpu.CompilerParams(vmem_limit_bytes=16 * 1024 * 1024)
LARGE = pltpu.CompilerParams(vmem_limit_bytes=56 * 1024 * 1024)


def up_to(value, step):
    return -(-value // step) * step


def is_power(size):
    return size & (size - 1) == 0


def partner_to(size, me, step):
    return me ^ step if is_power(size) else (me + step) % size


def partner_from(size, me, step):
    return me ^ step if is_power(size) else (me + size - step) % size


def send(block, axis, step):
    size = lax.axis_size(axis)
    return lax.ppermute(block, axis, [(i, partner_to(size, i, step)) for i in range(size)])


def pack(value, out):
    height = value.shape[0]
    largest = jnp.max(jnp.max(jnp.abs(value), axis=0, keepdims=True), axis=1, keepdims=True)
    power = jnp.clip(jnp.ceil(jnp.log2(jnp.maximum(largest, TINY))), -100.0, 100.0)
    out[:height] = value * jnp.exp2(PACK_TOP - power)
    out[height:] = jnp.broadcast_to(power, (PACK_ROWS, value.shape[1]))


def unpack(block):
    height = block.shape[0] - PACK_ROWS
    return block[:height] * jnp.exp2(block[height : height + 1, :1] - PACK_TOP)


def cross(block, step):
    return send(block.astype(jnp.float16), "mdl", step).astype(jnp.float32)


def dot(left, right, contract=((1,), (0,))):
    return lax.dot_general(left, right, (contract, ((), ())), preferred_element_type=jnp.float32)


def dispatch_body(owners, local, room, extra, *refs):
    sources, refs = refs[:3], refs[3:]
    outs, refs = refs[:owners], refs[owners:]
    states, task, batch, sems = refs
    rows, width = states.shape
    copies = [
        pltpu.make_async_copy(source, target, sems.at[i])
        for i, (source, target) in enumerate(zip(sources, (states, task, batch)))
    ]
    for i in (1, 2, 0):
        copies[i].start()
    copies[1].wait()
    copies[2].wait()
    me = lax.axis_index("teach")
    task_list, batch_list = task[...], batch[...]
    group = up_to(owners * local, ROW_TILE)
    named = lax.broadcasted_iota(jnp.int32, (group, rows), 0) == task_list
    earlier = lax.broadcasted_iota(jnp.int32, (rows, rows), 0) < lax.broadcasted_iota(
        jnp.int32, (rows, rows), 1
    )
    named = named.astype(jnp.float32)
    before = dot(named.astype(jnp.bfloat16), earlier.astype(jnp.float32).astype(jnp.bfloat16))
    before = jnp.sum(before * named, axis=0, keepdims=True).astype(jnp.int32)
    owner = task_list // local if local > 1 else task_list
    step = owner ^ me if is_power(owners) else (owner - me + owners) % owners
    place = step * local + task_list % local if local > 1 else step
    slot = place * room + before
    index = lax.broadcasted_iota(jnp.int32, (owners * local * room, rows), 0)
    chosen = (index == slot).astype(jnp.float32)
    head = (index % (local * room) == 0).astype(jnp.float32)
    member = (lax.broadcasted_iota(jnp.int32, (extra, rows), 0) == batch_list).astype(jnp.float32)
    tags = dot(
        (chosen + 2.0 * head).astype(jnp.bfloat16), member.astype(jnp.bfloat16), ((1,), (1,))
    ).astype(jnp.bfloat16)
    copies[0].wait()
    moved = dot(chosen.astype(jnp.bfloat16), states[...]).astype(jnp.bfloat16)
    for k, out in enumerate(outs):
        span = slice(k * local * room, (k + 1) * local * room)
        out[:, :width] = moved[span]
        out[:, width:] = tags[span]


def weights_body(*refs):
    sources, outs, sems = refs[1:5], refs[5:9], refs[9]
    copies = [
        pltpu.make_async_copy(source, target, sems.at[i])
        for i, (source, target) in enumerate(zip(sources, outs))
    ]
    for copy in copies:
        copy.start()
    for copy in copies:
        copy.wait()


def student(rows, student_up):
    pre = dot(rows, student_up[...])
    sig = 1.0 / (1.0 + jnp.exp(-pre))
    return (pre * sig).astype(jnp.bfloat16), sig * (1.0 + pre * (1.0 - sig))


def half_error(local, first, rows, weights, act_out, slope_out):
    teach_in, teach_out, student_up, student_down = weights
    per_teacher = 2 * rows.shape[0] // local
    labels = None
    for l in range(local):
        hidden = dot(rows, teach_in[l])
        hidden = hidden / (1.0 + jnp.exp(-hidden))
        if local > 1:
            index = first + lax.broadcasted_iota(jnp.int32, hidden.shape, 0)
            hidden = jnp.where(index // per_teacher == l, hidden, 0.0)
        part = dot(hidden.astype(jnp.bfloat16), teach_out[l])
        labels = part if labels is None else labels + part
    act, slope = student(rows, student_up)
    act_out[...] = act
    slope_out[...] = slope
    return dot(act, student_down[...], ((1,), (1,))) - labels


def half_start(height, other):
    me = lax.axis_index("mdl")
    return pl.multiple_of(((me & 1) ^ other) * height, ROW_TILE)


def forward_other_body(owners, local, room, *refs):
    blocks, refs = refs[:owners], refs[owners:]
    weights, refs = refs[:4], refs[4:]
    rows_own, rows_other, tags_out, counts_out, packed, act, slope, rows_all, tags_all = refs
    width = rows_own.shape[1]
    full = [block[...] for block in blocks]
    counts = None
    for block in full:
        mine = jnp.floor(block[:1, width:].astype(jnp.float32) * 0.5)
        counts = mine if counts is None else counts + mine
    counts_out[...] = counts
    for l in range(local):
        for k, block in enumerate(full):
            start = (l * owners + k) * room
            rows_all[start : start + room] = block[l * room : (l + 1) * room, :width]
            tag = block[l * room : (l + 1) * room, width:].astype(jnp.float32)
            if l == 0:
                head = lax.broadcasted_iota(jnp.int32, tag.shape, 0) == 0
                tag = jnp.where(head, tag - 2.0 * jnp.floor(tag * 0.5), tag)
            tags_all[start : start + room] = tag
    height = rows_own.shape[0]
    mine, there = half_start(height, 0), half_start(height, 1)
    rows_own[...] = rows_all[pl.ds(mine, height)]
    tags_out[...] = tags_all[pl.ds(mine, height)]
    rows = rows_all[pl.ds(there, height)]
    rows_other[...] = rows
    pack(half_error(local, there, rows, weights, act, slope), packed)


def forward_own_body(local, rows, *refs):
    weights, (error, act, slope) = refs[:4], refs[4:]
    first = half_start(rows.shape[0], 0)
    error[...] = half_error(local, first, rows[...], weights, act, slope)


def neighbour_body(rows_own, rows_other, student_up, act_own, slope_own, act_other, slope_other):
    act_own[...], slope_own[...] = student(rows_own[...], student_up)
    act_other[...], slope_other[...] = student(rows_other[...], student_up)


def pair_body(own, arrived, total, packed):
    value = own[...] + unpack(arrived)
    total[...] = value
    pack(value, packed)


def scale_body(*refs):
    own, arrived, tags = refs[:3]
    counts, scaled = refs[3:-1], refs[-1]
    all_counts = counts[0][...]
    for piece in counts[1:]:
        all_counts = all_counts + piece[...]
    inverse = jnp.where(all_counts > 0, 2.0 / all_counts, 0.0)
    weight = jnp.sum(tags[...] * inverse, axis=1, keepdims=True)
    scaled[...] = ((own[...] + unpack(arrived)) * weight).astype(scaled.dtype)


def backward_body(first, groups, *refs):
    student_down, refs = refs[0], refs[1:]
    grad_up, grad_down = refs[-2:]
    if first:
        up, down = None, None
    else:
        up, down = refs[4 * groups][...], refs[4 * groups + 1][...]
    for i in range(groups):
        scaled, rows, act, slope = refs[4 * i : 4 * i + 4]
        error = scaled[...]
        part = dot(error, act[...], ((0,), (0,)))
        down = part if down is None else down + part
        pre_grad = (dot(error, student_down[...]) * slope[...]).astype(jnp.bfloat16)
        part = dot(rows[...], pre_grad, ((0,), (0,)))
        up = part if up is None else up + part
    grad_up[...] = up
    grad_down[...] = down


def kernel(body, outs, operands, flops, scratch=(), params=SMALL, places=None):
    return pl.pallas_call(
        body,
        out_shape=outs,
        in_specs=places or [VMEM] * len(operands),
        out_specs=[VMEM] * len(outs),
        scratch_shapes=list(scratch),
        cost_estimate=pl.CostEstimate(flops=flops, bytes_accessed=1 << 18, transcendentals=0),
        compiler_params=params,
    )(*operands)


def on_device(states, task_ids, student_batch, teach_in, teach_out, student_up, student_down):
    row_count, width = states.shape
    owners, studs, parts = lax.axis_size("teach"), lax.axis_size("stud"), lax.axis_size("mdl")
    local, _, hidden = teach_in.shape
    actions = teach_out.shape[2]
    units = student_up.shape[1]
    teachers, batches = owners * local, owners * studs
    room = up_to(3 * row_count // (2 * teachers), ROW_TILE)
    extra = up_to(batches, LANES)
    slots = teachers * room
    height = slots // 2
    f32, bf16 = jnp.float32, jnp.bfloat16

    def shape(rows, columns, dtype):
        return jax.ShapeDtypeStruct((rows, columns), dtype)

    half, packed = shape(height, actions, f32), shape(height + PACK_ROWS, actions, f32)
    half_rows = shape(height, width, bf16)
    half_act, half_slope = shape(height, units, bf16), shape(height, units, f32)
    tokens = [ids.reshape(1, row_count) for ids in (task_ids, student_batch)]
    blocks = kernel(
        functools.partial(dispatch_body, owners, local, room, extra),
        [pltpu.VMEM((local * room, width + extra), bf16)] * owners,
        (states, *tokens),
        2 * slots * row_count * width,
        [pltpu.VMEM(a.shape, a.dtype) for a in (states, *tokens)] + [pltpu.SemaphoreType.DMA((3,))],
        LARGE,
        [HBM] * 3,
    )
    arrived = {k: send(blocks[k], "teach", k) for k in range(owners - 1, 0, -1)}
    weights = (teach_in, teach_out, student_up, student_down)
    weights = kernel(
        weights_body,
        [pltpu.VMEM(w.shape, w.dtype) for w in weights],
        (blocks[0], *[pltpu.with_memory_space_constraint(w, pltpu.HBM) for w in weights]),
        0,
        [pltpu.SemaphoreType.DMA((4,))],
        SMALL,
        [VMEM] + [HBM] * 4,
    )
    blocks = [blocks[0]] + list(arrived.values())
    work = 2 * height * 2 * width * (hidden + units)
    rows_own, rows_other, tags, counts, other, act_other, slope_other = kernel(
        functools.partial(forward_other_body, owners, local, room),
        [half_rows, half_rows, shape(height, extra, f32), shape(1, extra, f32), packed]
        + [half_act, half_slope],
        (*blocks, *weights),
        work,
        [pltpu.VMEM((slots, width), bf16), pltpu.VMEM((slots, extra), f32)],
    )
    arrived = cross(other, 1)
    own, act_own, slope_own = kernel(
        functools.partial(forward_own_body, local),
        [half, half_act, half_slope],
        (rows_own, *weights),
        work,
    )
    all_counts, mates = [counts], []
    for k in range(1, studs):
        all_counts.append(send(counts, "stud", k))
        mates.append((send(rows_own, "stud", k), send(rows_other, "stud", k)))
    own, arrived, all_counts, mates = lax.optimization_barrier((own, arrived, all_counts, mates))
    step = 2
    while step < parts:
        own, other = kernel(pair_body, [half, packed], (own, arrived), 0)
        arrived = cross(other, step)
        step *= 2
    groups = [(rows_own, act_own, slope_own, rows_other, act_other, slope_other)]
    for first, second in mates:
        known = kernel(
            neighbour_body,
            [half_act, half_slope] * 2,
            (first, second, weights[2]),
            4 * height * width * units,
        )
        groups.append((first, *known[:2], second, *known[2:]))
    own, arrived, groups = lax.optimization_barrier((own, arrived, groups))
    (scaled,) = kernel(scale_body, [shape(height, actions, bf16)], (own, arrived, tags, *all_counts), 0)
    from_pair = send(scaled, "mdl", 1)
    ours = [scaled] + [send(scaled, "stud", k) for k in range(1, studs)]
    work = 6 * height * width * units
    grads = [shape(width, units, f32), shape(actions, units, f32)]
    sums = kernel(
        functools.partial(backward_body, True, studs),
        grads,
        [weights[3]] + [a for s, g in zip(ours, groups) for a in (s, *g[:3])],
        studs * work,
    )
    from_pair, sums = lax.optimization_barrier((from_pair, sums))
    for k in range(studs):
        theirs = send(from_pair, "stud", k) if k else from_pair
        sums = kernel(
            functools.partial(backward_body, False, 1),
            grads,
            (weights[3], theirs, *groups[k][3:], *sums),
            work,
        )
    grad_up, grad_down = sums
    heights = (width // (owners * studs), actions // (owners * studs))

    def pieces(stud):
        return jnp.concatenate(
            [
                lax.dynamic_index_in_dim(g.reshape(owners, studs, h, units), stud, 1, False)
                for g, h in zip((grad_up, grad_down), heights)
            ],
            axis=1,
        )

    half = pieces(lax.axis_index("stud"))
    me = lax.axis_index("teach")
    part = lax.dynamic_index_in_dim(half, me, 0, False)
    arrived = [
        send(lax.dynamic_index_in_dim(half, partner_to(owners, me, k), 0, False).astype(bf16), "teach", k)
        for k in range(owners - 1, 0, -1)
    ]
    for piece in arrived:
        part = part + piece.astype(f32)
    return part[: heights[0]], part[heights[0] :]


def solution(mesh):
    in_specs = (
        P(("teach", "stud"), None),
        P(("teach", "stud"), None),
        P(("teach", "stud"), None),
        P("teach", None, "mdl"),
        P("teach", "mdl", None),
        P(None, "mdl"),
        P(None, "mdl"),
    )
    out_specs = (P(("teach", "stud"), "mdl"), P(("teach", "stud"), "mdl"))
    return jax.shard_map(
        on_device, mesh=mesh, in_specs=in_specs, out_specs=out_specs, check_vma=False
    )
```

```python
import functools

import jax
import jax.numpy as jnp
from jax import lax
from jax.experimental import pallas as pl
from jax.experimental.pallas import tpu as pltpu
from jax.sharding import PartitionSpec as P

LANES = 128
ROW_TILE = 16
PACK_ROWS = 8
PACK_TOP = 14.0
TINY = 1e-37
VMEM = pl.BlockSpec(memory_space=pltpu.VMEM)
HBM = pl.BlockSpec(memory_space=pltpu.HBM)
SMALL = pltpu.CompilerParams(vmem_limit_bytes=16 * 1024 * 1024)
LARGE = pltpu.CompilerParams(vmem_limit_bytes=56 * 1024 * 1024)


def up_to(value, step):
    return -(-value // step) * step


def is_power(size):
    return size & (size - 1) == 0


def partner_to(size, me, step):
    return me ^ step if is_power(size) else (me + step) % size


def partner_from(size, me, step):
    return me ^ step if is_power(size) else (me + size - step) % size


def send(block, axis, step):
    size = lax.axis_size(axis)
    return lax.ppermute(block, axis, [(i, partner_to(size, i, step)) for i in range(size)])


def pack(value, out):
    height = value.shape[0]
    largest = jnp.max(jnp.max(jnp.abs(value), axis=0, keepdims=True), axis=1, keepdims=True)
    power = jnp.clip(jnp.ceil(jnp.log2(jnp.maximum(largest, TINY))), -100.0, 100.0)
    out[:height] = value * jnp.exp2(PACK_TOP - power)
    out[height:] = jnp.broadcast_to(power, (PACK_ROWS, value.shape[1]))


def unpack(block):
    height = block.shape[0] - PACK_ROWS
    return block[:height] * jnp.exp2(block[height : height + 1, :1] - PACK_TOP)


def cross(block, step):
    return send(block.astype(jnp.float16), "mdl", step).astype(jnp.float32)


def dot(left, right, contract=((1,), (0,))):
    return lax.dot_general(left, right, (contract, ((), ())), preferred_element_type=jnp.float32)


def dispatch_body(owners, local, room, extra, *refs):
    sources, refs = refs[:3], refs[3:]
    outs, refs = refs[:owners], refs[owners:]
    states, task, batch, sems = refs
    rows, width = states.shape
    copies = [
        pltpu.make_async_copy(source, target, sems.at[i])
        for i, (source, target) in enumerate(zip(sources, (states, task, batch)))
    ]
    for i in (1, 2, 0):
        copies[i].start()
    copies[1].wait()
    copies[2].wait()
    me = lax.axis_index("teach")
    task_list, batch_list = task[...], batch[...]
    group = up_to(owners * local, ROW_TILE)
    named = lax.broadcasted_iota(jnp.int32, (group, rows), 0) == task_list
    earlier = lax.broadcasted_iota(jnp.int32, (rows, rows), 0) < lax.broadcasted_iota(
        jnp.int32, (rows, rows), 1
    )
    named = named.astype(jnp.float32)
    before = dot(named.astype(jnp.bfloat16), earlier.astype(jnp.float32).astype(jnp.bfloat16))
    before = jnp.sum(before * named, axis=0, keepdims=True).astype(jnp.int32)
    owner = task_list // local if local > 1 else task_list
    step = owner ^ me if is_power(owners) else (owner - me + owners) % owners
    place = step * local + task_list % local if local > 1 else step
    slot = place * room + before
    index = lax.broadcasted_iota(jnp.int32, (owners * local * room, rows), 0)
    chosen = (index == slot).astype(jnp.float32)
    head = (index % (local * room) == 0).astype(jnp.float32)
    member = (lax.broadcasted_iota(jnp.int32, (extra, rows), 0) == batch_list).astype(jnp.float32)
    tags = dot(
        (chosen + 2.0 * head).astype(jnp.bfloat16), member.astype(jnp.bfloat16), ((1,), (1,))
    ).astype(jnp.bfloat16)
    copies[0].wait()
    moved = dot(chosen.astype(jnp.bfloat16), states[...]).astype(jnp.bfloat16)
    for k, out in enumerate(outs):
        span = slice(k * local * room, (k + 1) * local * room)
        out[:, :width] = moved[span]
        out[:, width:] = tags[span]


def weights_body(*refs):
    sources, outs, sems = refs[1:5], refs[5:9], refs[9]
    copies = [
        pltpu.make_async_copy(source, target, sems.at[i])
        for i, (source, target) in enumerate(zip(sources, outs))
    ]
    for copy in copies:
        copy.start()
    for copy in copies:
        copy.wait()


def student(rows, student_up):
    pre = dot(rows, student_up[...])
    sig = 1.0 / (1.0 + jnp.exp(-pre))
    return (pre * sig).astype(jnp.bfloat16), sig * (1.0 + pre * (1.0 - sig))


def half_error(local, first, rows, weights, act_out, slope_out):
    teach_in, teach_out, student_up, student_down = weights
    per_teacher = 2 * rows.shape[0] // local
    labels = None
    for l in range(local):
        hidden = dot(rows, teach_in[l])
        hidden = hidden / (1.0 + jnp.exp(-hidden))
        if local > 1:
            index = first + lax.broadcasted_iota(jnp.int32, hidden.shape, 0)
            hidden = jnp.where(index // per_teacher == l, hidden, 0.0)
        part = dot(hidden.astype(jnp.bfloat16), teach_out[l])
        labels = part if labels is None else labels + part
    act, slope = student(rows, student_up)
    act_out[...] = act
    slope_out[...] = slope
    return dot(act, student_down[...], ((1,), (1,))) - labels


def half_start(height, other):
    me = lax.axis_index("mdl")
    return pl.multiple_of(((me & 1) ^ other) * height, ROW_TILE)


def forward_other_body(owners, local, room, *refs):
    blocks, refs = refs[:owners], refs[owners:]
    weights, refs = refs[:4], refs[4:]
    rows_own, rows_other, tags_out, counts_out, packed, act, slope, rows_all, tags_all = refs
    width = rows_own.shape[1]
    full = [block[...] for block in blocks]
    counts = None
    for block in full:
        mine = jnp.floor(block[:1, width:].astype(jnp.float32) * 0.5)
        counts = mine if counts is None else counts + mine
    counts_out[...] = counts
    for l in range(local):
        for k, block in enumerate(full):
            start = (l * owners + k) * room
            rows_all[start : start + room] = block[l * room : (l + 1) * room, :width]
            tag = block[l * room : (l + 1) * room, width:].astype(jnp.float32)
            if l == 0:
                head = lax.broadcasted_iota(jnp.int32, tag.shape, 0) == 0
                tag = jnp.where(head, tag - 2.0 * jnp.floor(tag * 0.5), tag)
            tags_all[start : start + room] = tag
    height = rows_own.shape[0]
    mine, there = half_start(height, 0), half_start(height, 1)
    rows_own[...] = rows_all[pl.ds(mine, height)]
    tags_out[...] = tags_all[pl.ds(mine, height)]
    rows = rows_all[pl.ds(there, height)]
    rows_other[...] = rows
    pack(half_error(local, there, rows, weights, act, slope), packed)


def forward_own_body(local, rows, *refs):
    weights, (error, act, slope) = refs[:4], refs[4:]
    first = half_start(rows.shape[0], 0)
    error[...] = half_error(local, first, rows[...], weights, act, slope)


def neighbour_body(rows_own, rows_other, student_up, act_own, slope_own, act_other, slope_other):
    act_own[...], slope_own[...] = student(rows_own[...], student_up)
    act_other[...], slope_other[...] = student(rows_other[...], student_up)


def pair_body(own, arrived, total, packed):
    value = own[...] + unpack(arrived)
    total[...] = value
    pack(value, packed)


def scale_body(*refs):
    own, arrived, tags = refs[:3]
    counts, scaled = refs[3:-1], refs[-1]
    all_counts = counts[0][...]
    for piece in counts[1:]:
        all_counts = all_counts + piece[...]
    inverse = jnp.where(all_counts > 0, 2.0 / all_counts, 0.0)
    weight = jnp.sum(tags[...] * inverse, axis=1, keepdims=True)
    scaled[...] = ((own[...] + unpack(arrived)) * weight).astype(scaled.dtype)


def backward_body(first, groups, *refs):
    student_down, refs = refs[0], refs[1:]
    grad_up, grad_down = refs[-2:]
    if first:
        up, down = None, None
    else:
        up, down = refs[4 * groups][...], refs[4 * groups + 1][...]
    for i in range(groups):
        scaled, rows, act, slope = refs[4 * i : 4 * i + 4]
        error = scaled[...]
        part = dot(error, act[...], ((0,), (0,)))
        down = part if down is None else down + part
        pre_grad = (dot(error, student_down[...]) * slope[...]).astype(jnp.bfloat16)
        part = dot(rows[...], pre_grad, ((0,), (0,)))
        up = part if up is None else up + part
    grad_up[...] = up
    grad_down[...] = down


def kernel(body, outs, operands, flops, scratch=(), params=SMALL, places=None):
    return pl.pallas_call(
        body,
        out_shape=outs,
        in_specs=places or [VMEM] * len(operands),
        out_specs=[VMEM] * len(outs),
        scratch_shapes=list(scratch),
        cost_estimate=pl.CostEstimate(flops=flops, bytes_accessed=1 << 18, transcendentals=0),
        compiler_params=params,
    )(*operands)


def on_device(states, task_ids, student_batch, teach_in, teach_out, student_up, student_down):
    row_count, width = states.shape
    owners, studs, parts = lax.axis_size("teach"), lax.axis_size("stud"), lax.axis_size("mdl")
    local, _, hidden = teach_in.shape
    actions = teach_out.shape[2]
    units = student_up.shape[1]
    teachers, batches = owners * local, owners * studs
    room = up_to(3 * row_count // (2 * teachers), ROW_TILE)
    extra = up_to(batches, LANES)
    slots = teachers * room
    height = slots // 2
    f32, bf16 = jnp.float32, jnp.bfloat16

    def shape(rows, columns, dtype):
        return jax.ShapeDtypeStruct((rows, columns), dtype)

    half, packed = shape(height, actions, f32), shape(height + PACK_ROWS, actions, f32)
    half_rows = shape(height, width, bf16)
    half_act, half_slope = shape(height, units, bf16), shape(height, units, f32)
    tokens = [ids.reshape(1, row_count) for ids in (task_ids, student_batch)]
    blocks = kernel(
        functools.partial(dispatch_body, owners, local, room, extra),
        [pltpu.VMEM((local * room, width + extra), bf16)] * owners,
        (states, *tokens),
        2 * slots * row_count * width,
        [pltpu.VMEM(a.shape, a.dtype) for a in (states, *tokens)] + [pltpu.SemaphoreType.DMA((3,))],
        LARGE,
        [HBM] * 3,
    )
    arrived = {k: send(blocks[k], "teach", k) for k in range(owners - 1, 0, -1)}
    weights = (teach_in, teach_out, student_up, student_down)
    weights = kernel(
        weights_body,
        [pltpu.VMEM(w.shape, w.dtype) for w in weights],
        (blocks[0], *[pltpu.with_memory_space_constraint(w, pltpu.HBM) for w in weights]),
        0,
        [pltpu.SemaphoreType.DMA((4,))],
        SMALL,
        [VMEM] + [HBM] * 4,
    )
    blocks = [blocks[0]] + list(arrived.values())
    work = 2 * height * 2 * width * (hidden + units)
    rows_own, rows_other, tags, counts, other, act_other, slope_other = kernel(
        functools.partial(forward_other_body, owners, local, room),
        [half_rows, half_rows, shape(height, extra, f32), shape(1, extra, f32), packed]
        + [half_act, half_slope],
        (*blocks, *weights),
        work,
        [pltpu.VMEM((slots, width), bf16), pltpu.VMEM((slots, extra), f32)],
    )
    arrived = cross(other, 1)
    own, act_own, slope_own = kernel(
        functools.partial(forward_own_body, local),
        [half, half_act, half_slope],
        (rows_own, *weights),
        work,
    )
    step = 2
    while step < parts:
        own, other = kernel(pair_body, [half, packed], (own, arrived), 0)
        arrived = cross(other, step)
        step *= 2
    all_counts, mates = [counts], []
    for k in range(1, studs):
        all_counts.append(send(counts, "stud", k))
        mates.append((send(rows_own, "stud", k), send(rows_other, "stud", k)))
    own, arrived, all_counts, mates = lax.optimization_barrier((own, arrived, all_counts, mates))
    (scaled,) = kernel(scale_body, [shape(height, actions, bf16)], (own, arrived, tags, *all_counts), 0)
    from_pair = send(scaled, "mdl", 1)
    known = [
        kernel(
            neighbour_body,
            [half_act, half_slope] * 2,
            (first, second, weights[2]),
            4 * height * width * units,
        )
        for first, second in mates
    ]
    work = 6 * height * width * units
    grads = [shape(width, units, f32), shape(actions, units, f32)]
    sums = kernel(
        functools.partial(backward_body, True, 1),
        grads,
        (weights[3], scaled, rows_own, act_own, slope_own),
        work,
    )
    scaled, from_pair, sums, known = lax.optimization_barrier((scaled, from_pair, sums, known))
    theirs = [(send(scaled, "stud", k), send(from_pair, "stud", k)) for k in range(1, studs)]
    sums = kernel(
        functools.partial(backward_body, False, 1),
        grads,
        (weights[3], from_pair, rows_other, act_other, slope_other, *sums),
        work,
    )
    for error, rows, state in zip(theirs, mates, known):
        sums = kernel(
            functools.partial(backward_body, False, 2),
            grads,
            (weights[3], error[0], rows[0], *state[:2], error[1], rows[1], *state[2:], *sums),
            2 * work,
        )
    grad_up, grad_down = sums
    heights = (width // (owners * studs), actions // (owners * studs))

    def pieces(stud):
        return jnp.concatenate(
            [
                lax.dynamic_index_in_dim(g.reshape(owners, studs, h, units), stud, 1, False)
                for g, h in zip((grad_up, grad_down), heights)
            ],
            axis=1,
        )

    half = pieces(lax.axis_index("stud"))
    me = lax.axis_index("teach")
    part = lax.dynamic_index_in_dim(half, me, 0, False)
    arrived = [
        send(lax.dynamic_index_in_dim(half, partner_to(owners, me, k), 0, False).astype(bf16), "teach", k)
        for k in range(owners - 1, 0, -1)
    ]
    for piece in arrived:
        part = part + piece.astype(f32)
    return part[: heights[0]], part[heights[0] :]


def solution(mesh):
    in_specs = (
        P(("teach", "stud"), None),
        P(("teach", "stud"), None),
        P(("teach", "stud"), None),
        P("teach", None, "mdl"),
        P("teach", "mdl", None),
        P(None, "mdl"),
        P(None, "mdl"),
    )
    out_specs = (P(("teach", "stud"), "mdl"), P(("teach", "stud"), "mdl"))
    return jax.shard_map(
        on_device, mesh=mesh, in_specs=in_specs, out_specs=out_specs, check_vma=False
    )
```

```python
import functools

import jax
import jax.numpy as jnp
from jax import lax
from jax.experimental import pallas as pl
from jax.experimental.pallas import tpu as pltpu
from jax.sharding import PartitionSpec as P

LANES = 128
ROW_TILE = 16
PACK_ROWS = 8
PACK_TOP = 14.0
TINY = 1e-37
VMEM = pl.BlockSpec(memory_space=pltpu.VMEM)
HBM = pl.BlockSpec(memory_space=pltpu.HBM)
SMALL = pltpu.CompilerParams(vmem_limit_bytes=16 * 1024 * 1024)
LARGE = pltpu.CompilerParams(vmem_limit_bytes=56 * 1024 * 1024)


def up_to(value, step):
    return -(-value // step) * step


def is_power(size):
    return size & (size - 1) == 0


def partner_to(size, me, step):
    return me ^ step if is_power(size) else (me + step) % size


def partner_from(size, me, step):
    return me ^ step if is_power(size) else (me + size - step) % size


def send(block, axis, step):
    size = lax.axis_size(axis)
    return lax.ppermute(block, axis, [(i, partner_to(size, i, step)) for i in range(size)])


def pack(value, out):
    height = value.shape[0]
    largest = jnp.max(jnp.max(jnp.abs(value), axis=0, keepdims=True), axis=1, keepdims=True)
    power = jnp.clip(jnp.ceil(jnp.log2(jnp.maximum(largest, TINY))), -100.0, 100.0)
    out[:height] = value * jnp.exp2(PACK_TOP - power)
    out[height:] = jnp.broadcast_to(power, (PACK_ROWS, value.shape[1]))


def unpack(block):
    height = block.shape[0] - PACK_ROWS
    return block[:height] * jnp.exp2(block[height : height + 1, :1] - PACK_TOP)


def cross(block, step):
    return send(block.astype(jnp.float16), "mdl", step).astype(jnp.float32)


def dot(left, right, contract=((1,), (0,))):
    return lax.dot_general(left, right, (contract, ((), ())), preferred_element_type=jnp.float32)


def dispatch_body(owners, local, room, extra, *refs):
    sources, refs = refs[:3], refs[3:]
    outs, refs = refs[:owners], refs[owners:]
    states, task, batch, sems = refs
    rows, width = states.shape
    copies = [
        pltpu.make_async_copy(source, target, sems.at[i])
        for i, (source, target) in enumerate(zip(sources, (states, task, batch)))
    ]
    for i in (1, 2, 0):
        copies[i].start()
    copies[1].wait()
    copies[2].wait()
    me = lax.axis_index("teach")
    task_list, batch_list = task[...], batch[...]
    group = up_to(owners * local, ROW_TILE)
    named = lax.broadcasted_iota(jnp.int32, (group, rows), 0) == task_list
    earlier = lax.broadcasted_iota(jnp.int32, (rows, rows), 0) < lax.broadcasted_iota(
        jnp.int32, (rows, rows), 1
    )
    named = named.astype(jnp.float32)
    before = dot(named.astype(jnp.bfloat16), earlier.astype(jnp.float32).astype(jnp.bfloat16))
    before = jnp.sum(before * named, axis=0, keepdims=True).astype(jnp.int32)
    owner = task_list // local if local > 1 else task_list
    step = owner ^ me if is_power(owners) else (owner - me + owners) % owners
    place = step * local + task_list % local if local > 1 else step
    slot = place * room + before
    index = lax.broadcasted_iota(jnp.int32, (owners * local * room, rows), 0)
    chosen = (index == slot).astype(jnp.float32)
    head = (index % (local * room) == 0).astype(jnp.float32)
    member = (lax.broadcasted_iota(jnp.int32, (extra, rows), 0) == batch_list).astype(jnp.float32)
    tags = dot(
        (chosen + 2.0 * head).astype(jnp.bfloat16), member.astype(jnp.bfloat16), ((1,), (1,))
    ).astype(jnp.bfloat16)
    copies[0].wait()
    moved = dot(chosen.astype(jnp.bfloat16), states[...]).astype(jnp.bfloat16)
    for k, out in enumerate(outs):
        span = slice(k * local * room, (k + 1) * local * room)
        out[:, :width] = moved[span]
        out[:, width:] = tags[span]


def weights_body(*refs):
    sources, outs, sems = refs[1:5], refs[5:9], refs[9]
    copies = [
        pltpu.make_async_copy(source, target, sems.at[i])
        for i, (source, target) in enumerate(zip(sources, outs))
    ]
    for copy in copies:
        copy.start()
    for copy in copies:
        copy.wait()


def student(rows, student_up):
    pre = dot(rows, student_up[...])
    sig = 1.0 / (1.0 + jnp.exp(-pre))
    return (pre * sig).astype(jnp.bfloat16), sig * (1.0 + pre * (1.0 - sig))


def forward_body(owners, local, room, *refs):
    blocks, refs = refs[:owners], refs[owners:]
    teach_in, teach_out, student_up, student_down = refs[:4]
    rows_out, tags_out, counts_out, error_out, packed, act_out, slope_out = refs[4:]
    width = rows_out.shape[1]
    full = [block[...] for block in blocks]
    counts = None
    for block in full:
        mine = jnp.floor(block[:1, width:].astype(jnp.float32) * 0.5)
        counts = mine if counts is None else counts + mine
    counts_out[...] = counts
    for l in range(local):
        span = slice(l * owners * room, (l + 1) * owners * room)
        for k, block in enumerate(full):
            start = (l * owners + k) * room
            rows_out[start : start + room] = block[l * room : (l + 1) * room, :width]
            tag = block[l * room : (l + 1) * room, width:].astype(jnp.float32)
            if l == 0:
                head = lax.broadcasted_iota(jnp.int32, tag.shape, 0) == 0
                tag = jnp.where(head, tag - 2.0 * jnp.floor(tag * 0.5), tag)
            tags_out[start : start + room] = tag
        rows = rows_out[span]
        hidden = dot(rows, teach_in[l])
        hidden = (hidden / (1.0 + jnp.exp(-hidden))).astype(jnp.bfloat16)
        act, slope = student(rows, student_up)
        act_out[span] = act
        slope_out[span] = slope
        error_out[span] = dot(act, student_down[...], ((1,), (1,))) - dot(hidden, teach_out[l])
    pack(error_out[...], packed)


def neighbour_body(rows, student_up, act, slope):
    act[...], slope[...] = student(rows[...], student_up)


def pair_body(own, arrived, total, packed):
    value = own[...] + unpack(arrived)
    total[...] = value
    pack(value, packed)


def scale_body(*refs):
    own, arrived, tags = refs[:3]
    counts, scaled = refs[3:-1], refs[-1]
    all_counts = counts[0][...]
    for piece in counts[1:]:
        all_counts = all_counts + piece[...]
    inverse = jnp.where(all_counts > 0, 2.0 / all_counts, 0.0)
    weight = jnp.sum(tags[...] * inverse, axis=1, keepdims=True)
    scaled[...] = ((own[...] + unpack(arrived)) * weight).astype(scaled.dtype)


def backward_body(first, groups, *refs):
    student_down, refs = refs[0], refs[1:]
    grad_up, grad_down = refs[-2:]
    if first:
        up, down = None, None
    else:
        up, down = refs[4 * groups][...], refs[4 * groups + 1][...]
    for i in range(groups):
        scaled, rows, act, slope = refs[4 * i : 4 * i + 4]
        error = scaled[...]
        part = dot(error, act[...], ((0,), (0,)))
        down = part if down is None else down + part
        pre_grad = (dot(error, student_down[...]) * slope[...]).astype(jnp.bfloat16)
        part = dot(rows[...], pre_grad, ((0,), (0,)))
        up = part if up is None else up + part
    grad_up[...] = up
    grad_down[...] = down


def kernel(body, outs, operands, flops, scratch=(), params=SMALL, places=None):
    return pl.pallas_call(
        body,
        out_shape=outs,
        in_specs=places or [VMEM] * len(operands),
        out_specs=[VMEM] * len(outs),
        scratch_shapes=list(scratch),
        cost_estimate=pl.CostEstimate(flops=flops, bytes_accessed=1 << 18, transcendentals=0),
        compiler_params=params,
    )(*operands)


def on_device(states, task_ids, student_batch, teach_in, teach_out, student_up, student_down):
    row_count, width = states.shape
    owners, studs, parts = lax.axis_size("teach"), lax.axis_size("stud"), lax.axis_size("mdl")
    local, _, hidden = teach_in.shape
    actions = teach_out.shape[2]
    units = student_up.shape[1]
    teachers, batches = owners * local, owners * studs
    room = up_to(3 * row_count // (2 * teachers), ROW_TILE)
    extra = up_to(batches, LANES)
    slots = teachers * room
    f32, bf16 = jnp.float32, jnp.bfloat16

    def shape(rows, columns, dtype):
        return jax.ShapeDtypeStruct((rows, columns), dtype)

    whole, packed = shape(slots, actions, f32), shape(slots + PACK_ROWS, actions, f32)
    state = [shape(slots, units, bf16), shape(slots, units, f32)]
    tokens = [ids.reshape(1, row_count) for ids in (task_ids, student_batch)]
    blocks = kernel(
        functools.partial(dispatch_body, owners, local, room, extra),
        [pltpu.VMEM((local * room, width + extra), bf16)] * owners,
        (states, *tokens),
        2 * slots * row_count * width,
        [pltpu.VMEM(a.shape, a.dtype) for a in (states, *tokens)] + [pltpu.SemaphoreType.DMA((3,))],
        LARGE,
        [HBM] * 3,
    )
    arrived = {k: send(blocks[k], "teach", k) for k in range(owners - 1, 0, -1)}
    weights = (teach_in, teach_out, student_up, student_down)
    weights = kernel(
        weights_body,
        [pltpu.VMEM(w.shape, w.dtype) for w in weights],
        (blocks[0], *[pltpu.with_memory_space_constraint(w, pltpu.HBM) for w in weights]),
        0,
        [pltpu.SemaphoreType.DMA((4,))],
        SMALL,
        [VMEM] + [HBM] * 4,
    )
    blocks = [blocks[0]] + list(arrived.values())
    rows, tags, counts, error, other, act, slope = kernel(
        functools.partial(forward_body, owners, local, room),
        [shape(slots, width, bf16), shape(slots, extra, f32), shape(1, extra, f32), whole, packed]
        + state,
        (*blocks, *weights),
        4 * slots * width * (hidden + units),
    )
    arrived = cross(other, 1)
    step = 2
    while step < parts:
        error, other = kernel(pair_body, [whole, packed], (error, arrived), 0)
        arrived = cross(other, step)
        step *= 2
    all_counts, mates = [counts], []
    for k in range(1, studs):
        all_counts.append(send(counts, "stud", k))
        mates.append(send(rows, "stud", k))
    known = [
        kernel(neighbour_body, state, (theirs, weights[2]), 2 * slots * width * units)
        for theirs in mates
    ]
    error, arrived, all_counts, mates, known = lax.optimization_barrier(
        (error, arrived, all_counts, mates, known)
    )
    (scaled,) = kernel(scale_body, [shape(slots, actions, bf16)], (error, arrived, tags, *all_counts), 0)
    work = 6 * slots * width * units
    grads = [shape(width, units, f32), shape(actions, units, f32)]
    theirs = [send(scaled, "stud", k) for k in range(1, studs)]
    sums = kernel(
        functools.partial(backward_body, True, 1), grads, (weights[3], scaled, rows, act, slope), work
    )
    for scaled, rows, state in zip(theirs, mates, known):
        sums = kernel(
            functools.partial(backward_body, False, 1),
            grads,
            (weights[3], scaled, rows, *state, *sums),
            work,
        )
    grad_up, grad_down = sums
    heights = (width // (owners * studs), actions // (owners * studs))

    def pieces(stud):
        return jnp.concatenate(
            [
                lax.dynamic_index_in_dim(g.reshape(owners, studs, h, units), stud, 1, False)
                for g, h in zip((grad_up, grad_down), heights)
            ],
            axis=1,
        )

    half = pieces(lax.axis_index("stud"))
    me = lax.axis_index("teach")
    part = lax.dynamic_index_in_dim(half, me, 0, False)
    arrived = [
        send(lax.dynamic_index_in_dim(half, partner_to(owners, me, k), 0, False).astype(bf16), "teach", k)
        for k in range(owners - 1, 0, -1)
    ]
    for piece in arrived:
        part = part + piece.astype(f32)
    return part[: heights[0]], part[heights[0] :]


def solution(mesh):
    in_specs = (
        P(("teach", "stud"), None),
        P(("teach", "stud"), None),
        P(("teach", "stud"), None),
        P("teach", None, "mdl"),
        P("teach", "mdl", None),
        P(None, "mdl"),
        P(None, "mdl"),
    )
    out_specs = (P(("teach", "stud"), "mdl"), P(("teach", "stud"), "mdl"))
    return jax.shard_map(
        on_device, mesh=mesh, in_specs=in_specs, out_specs=out_specs, check_vma=False
    )
```

```python
import functools

import jax
import jax.numpy as jnp
from jax import lax
from jax.experimental import pallas as pl
from jax.experimental.pallas import tpu as pltpu
from jax.sharding import PartitionSpec as P

LANES = 128
ROW_TILE = 16
PACK_ROWS = 8
PACK_TOP = 14.0
TINY = 1e-37
VMEM = pl.BlockSpec(memory_space=pltpu.VMEM)
HBM = pl.BlockSpec(memory_space=pltpu.HBM)
SMALL = pltpu.CompilerParams(vmem_limit_bytes=16 * 1024 * 1024)
LARGE = pltpu.CompilerParams(vmem_limit_bytes=56 * 1024 * 1024)


def up_to(value, step):
    return -(-value // step) * step


def is_power(size):
    return size & (size - 1) == 0


def partner_to(size, me, step):
    return me ^ step if is_power(size) else (me + step) % size


def partner_from(size, me, step):
    return me ^ step if is_power(size) else (me + size - step) % size


def send(block, axis, step):
    size = lax.axis_size(axis)
    return lax.ppermute(block, axis, [(i, partner_to(size, i, step)) for i in range(size)])


def pack(value, out):
    height = value.shape[0]
    largest = jnp.max(jnp.max(jnp.abs(value), axis=0, keepdims=True), axis=1, keepdims=True)
    power = jnp.clip(jnp.ceil(jnp.log2(jnp.maximum(largest, TINY))), -100.0, 100.0)
    out[:height] = value * jnp.exp2(PACK_TOP - power)
    out[height:] = jnp.broadcast_to(power, (PACK_ROWS, value.shape[1]))


def unpack(block):
    height = block.shape[0] - PACK_ROWS
    return block[:height] * jnp.exp2(block[height : height + 1, :1] - PACK_TOP)


def cross(block, step):
    return send(block.astype(jnp.float16), "mdl", step).astype(jnp.float32)


def dot(left, right, contract=((1,), (0,))):
    return lax.dot_general(left, right, (contract, ((), ())), preferred_element_type=jnp.float32)


def dispatch_body(owners, local, room, extra, *refs):
    sources, refs = refs[:3], refs[3:]
    outs, refs = refs[:owners], refs[owners:]
    states, task, batch, sems = refs
    rows, width = states.shape
    copies = [
        pltpu.make_async_copy(source, target, sems.at[i])
        for i, (source, target) in enumerate(zip(sources, (states, task, batch)))
    ]
    for i in (1, 2, 0):
        copies[i].start()
    copies[1].wait()
    copies[2].wait()
    me = lax.axis_index("teach")
    task_list, batch_list = task[...], batch[...]
    group = up_to(owners * local, ROW_TILE)
    named = lax.broadcasted_iota(jnp.int32, (group, rows), 0) == task_list
    earlier = lax.broadcasted_iota(jnp.int32, (rows, rows), 0) < lax.broadcasted_iota(
        jnp.int32, (rows, rows), 1
    )
    named = named.astype(jnp.float32)
    before = dot(named.astype(jnp.bfloat16), earlier.astype(jnp.float32).astype(jnp.bfloat16))
    before = jnp.sum(before * named, axis=0, keepdims=True).astype(jnp.int32)
    owner = task_list // local if local > 1 else task_list
    step = owner ^ me if is_power(owners) else (owner - me + owners) % owners
    place = step * local + task_list % local if local > 1 else step
    slot = place * room + before
    index = lax.broadcasted_iota(jnp.int32, (owners * local * room, rows), 0)
    chosen = (index == slot).astype(jnp.float32)
    head = (index % (local * room) == 0).astype(jnp.float32)
    member = (lax.broadcasted_iota(jnp.int32, (extra, rows), 0) == batch_list).astype(jnp.float32)
    tags = dot(
        (chosen + 2.0 * head).astype(jnp.bfloat16), member.astype(jnp.bfloat16), ((1,), (1,))
    ).astype(jnp.bfloat16)
    copies[0].wait()
    moved = dot(chosen.astype(jnp.bfloat16), states[...]).astype(jnp.bfloat16)
    for k, out in enumerate(outs):
        span = slice(k * local * room, (k + 1) * local * room)
        out[:, :width] = moved[span]
        out[:, width:] = tags[span]


def weights_body(*refs):
    sources, outs, sems = refs[1:5], refs[5:9], refs[9]
    copies = [
        pltpu.make_async_copy(source, target, sems.at[i])
        for i, (source, target) in enumerate(zip(sources, outs))
    ]
    for copy in copies:
        copy.start()
    for copy in copies:
        copy.wait()


def student(rows, student_up):
    pre = dot(rows, student_up[...])
    sig = 1.0 / (1.0 + jnp.exp(-pre))
    return (pre * sig).astype(jnp.bfloat16), sig * (1.0 + pre * (1.0 - sig))


def forward_body(owners, local, room, *refs):
    blocks, refs = refs[:owners], refs[owners:]
    teach_in, teach_out, student_up, student_down = refs[:4]
    rows_out, tags_out, counts_out, error_out, packed, act_out, slope_out = refs[4:]
    width = rows_out.shape[1]
    full = [block[...] for block in blocks]
    counts = None
    for block in full:
        mine = jnp.floor(block[:1, width:].astype(jnp.float32) * 0.5)
        counts = mine if counts is None else counts + mine
    counts_out[...] = counts
    for l in range(local):
        span = slice(l * owners * room, (l + 1) * owners * room)
        for k, block in enumerate(full):
            start = (l * owners + k) * room
            rows_out[start : start + room] = block[l * room : (l + 1) * room, :width]
            tag = block[l * room : (l + 1) * room, width:].astype(jnp.float32)
            if l == 0:
                head = lax.broadcasted_iota(jnp.int32, tag.shape, 0) == 0
                tag = jnp.where(head, tag - 2.0 * jnp.floor(tag * 0.5), tag)
            tags_out[start : start + room] = tag
        rows = rows_out[span]
        hidden = dot(rows, teach_in[l])
        hidden = (hidden / (1.0 + jnp.exp(-hidden))).astype(jnp.bfloat16)
        act, slope = student(rows, student_up)
        act_out[span] = act
        slope_out[span] = slope
        error_out[span] = dot(act, student_down[...], ((1,), (1,))) - dot(hidden, teach_out[l])
    pack(error_out[...], packed)


def chosen_columns(columns, owners, studs):
    height = columns // (owners * studs)
    shape = (owners * height, columns)
    row = lax.broadcasted_iota(jnp.int32, shape, 0)
    column = lax.broadcasted_iota(jnp.int32, shape, 1)
    owner = partner_to(owners, lax.axis_index("teach"), row // height)
    wanted = (owner * studs + lax.axis_index("stud")) * height + row % height
    return (column == wanted).astype(jnp.float32).astype(jnp.bfloat16)


def turn(value, owners, studs):
    chosen = chosen_columns(value.shape[1], owners, studs)
    return dot(chosen, value, ((1,), (1,))).astype(jnp.bfloat16)


def ahead_body(owners, studs, own, rows, student_up, *refs):
    if own:
        _, turned, handed = refs
        handed[...] = rows[...]
    else:
        turned, act, slope = refs
        act[...], slope[...] = student(rows[...], student_up)
    turned[...] = turn(rows[...], owners, studs)


def pair_body(own, arrived, total, packed):
    value = own[...] + unpack(arrived)
    total[...] = value
    pack(value, packed)


def scale_body(*refs):
    own, arrived, tags = refs[:3]
    counts, scaled = refs[3:-1], refs[-1]
    all_counts = counts[0][...]
    for piece in counts[1:]:
        all_counts = all_counts + piece[...]
    inverse = jnp.where(all_counts > 0, 2.0 / all_counts, 0.0)
    weight = jnp.sum(tags[...] * inverse, axis=1, keepdims=True)
    scaled[...] = ((own[...] + unpack(arrived)) * weight).astype(scaled.dtype)


def backward_body(owners, studs, earlier, scaled, turned, act, slope, student_down, *refs):
    error = scaled[...]
    down = dot(turn(error, owners, studs), act[...])
    pre_grad = (dot(error, student_down[...]) * slope[...]).astype(jnp.bfloat16)
    up = dot(turned[...], pre_grad)
    if earlier:
        up, down = up + refs[0][...], down + refs[1][...]
    outs = refs[2 * earlier :]
    if len(outs) == 2:
        outs[0][...], outs[1][...] = up, down
        return
    high, low = up.shape[0] // owners, down.shape[0] // owners
    for k, out in enumerate(outs):
        block = [up[k * high : (k + 1) * high], down[k * low : (k + 1) * low]]
        out[...] = jnp.concatenate(block).astype(out.dtype)


def closing_body(*refs):
    pieces, (grad_up, grad_down, up, down, sems) = refs[:-5], refs[-5:]
    total = pieces[0][...]
    for piece in pieces[1:]:
        total = total + piece[...].astype(jnp.float32)
    cut = up.shape[0]
    up[...] = total[:cut]
    first = pltpu.make_async_copy(up, grad_up, sems.at[0])
    first.start()
    down[...] = total[cut:]
    second = pltpu.make_async_copy(down, grad_down, sems.at[1])
    second.start()
    first.wait()
    second.wait()


def kernel(body, outs, operands, flops, scratch=(), params=SMALL, places=None, to=VMEM):
    return pl.pallas_call(
        body,
        out_shape=outs,
        in_specs=places or [VMEM] * len(operands),
        out_specs=[to] * len(outs),
        scratch_shapes=list(scratch),
        cost_estimate=pl.CostEstimate(flops=flops, bytes_accessed=0, transcendentals=0),
        compiler_params=params,
    )(*operands)


def on_device(states, task_ids, student_batch, teach_in, teach_out, student_up, student_down):
    row_count, width = states.shape
    owners, studs, parts = lax.axis_size("teach"), lax.axis_size("stud"), lax.axis_size("mdl")
    local, _, hidden = teach_in.shape
    actions = teach_out.shape[2]
    units = student_up.shape[1]
    teachers, batches = owners * local, owners * studs
    room = up_to(3 * row_count // (2 * teachers), ROW_TILE)
    extra = up_to(batches, LANES)
    slots = teachers * room
    f32, bf16 = jnp.float32, jnp.bfloat16

    def shape(rows, columns, dtype):
        return jax.ShapeDtypeStruct((rows, columns), dtype)

    whole, packed = shape(slots, actions, f32), shape(slots + PACK_ROWS, actions, f32)
    state = [shape(slots, units, bf16), shape(slots, units, f32)]
    tokens = [ids.reshape(1, row_count) for ids in (task_ids, student_batch)]
    blocks = kernel(
        functools.partial(dispatch_body, owners, local, room, extra),
        [pltpu.VMEM((local * room, width + extra), bf16)] * owners,
        (states, *tokens),
        2 * slots * row_count * width,
        [pltpu.VMEM(a.shape, a.dtype) for a in (states, *tokens)] + [pltpu.SemaphoreType.DMA((3,))],
        LARGE,
        [HBM] * 3,
    )
    arrived = {k: send(blocks[k], "teach", k) for k in range(owners - 1, 0, -1)}
    weights = (teach_in, teach_out, student_up, student_down)
    weights = kernel(
        weights_body,
        [pltpu.VMEM(w.shape, w.dtype) for w in weights],
        (blocks[0], *[pltpu.with_memory_space_constraint(w, pltpu.HBM) for w in weights]),
        0,
        [pltpu.SemaphoreType.DMA((4,))],
        SMALL,
        [VMEM] + [HBM] * 4,
    )
    blocks = [blocks[0]] + list(arrived.values())
    rows, tags, counts, error, other, act, slope = kernel(
        functools.partial(forward_body, owners, local, room),
        [shape(slots, width, bf16), shape(slots, extra, f32), shape(1, extra, f32), whole, packed]
        + state,
        (*blocks, *weights),
        4 * slots * width * (hidden + units),
    )
    arrived = cross(other, 1)
    step = 2
    while step < parts:
        error, other = kernel(pair_body, [whole, packed], (error, arrived), 0)
        arrived = cross(other, step)
        step *= 2
    ahead = functools.partial(ahead_body, owners, studs, False)
    turned = shape(width // studs, slots, bf16)
    ours, handed = kernel(
        functools.partial(ahead_body, owners, studs, True),
        [turned, shape(slots, width, bf16)],
        (rows, weights[2], error),
        0,
    )
    all_counts, known = [counts], []
    for k in range(1, studs):
        all_counts.append(send(counts, "stud", k))
        theirs = send(handed, "stud", k)
        known.append(
            kernel(ahead, [turned] + state, (theirs, weights[2]), 0)
        )
    error, arrived, all_counts, known, ours = lax.optimization_barrier(
        (error, arrived, all_counts, known, ours)
    )
    (scaled,) = kernel(scale_body, [shape(slots, actions, bf16)], (error, arrived, tags, *all_counts), 0)
    work = 6 * slots * width * units
    grads = [shape(width // studs, units, f32), shape(actions // studs, units, f32)]
    heights = [g.shape[0] // owners for g in grads]
    blocks = [shape(sum(heights), units, f32)] + [shape(sum(heights), units, bf16)] * (owners - 1)
    errors = [scaled] + [send(scaled, "stud", k) for k in range(1, studs)]
    states = [[ours, act, slope]] + known
    sums = []
    for k, (error, state) in enumerate(zip(errors, states)):
        sums = kernel(
            functools.partial(backward_body, owners, studs, k > 0),
            blocks if k == studs - 1 else grads,
            (error, *state, weights[3], *sums),
            work,
        )
    pieces = [sums[0]] + [send(sums[k], "teach", k) for k in (*range(owners - 2, 0, -1), owners - 1)]
    outs = [shape(h, units, f32) for h in heights]
    return kernel(
        closing_body,
        outs,
        pieces,
        0,
        [pltpu.VMEM(o.shape, f32) for o in outs] + [pltpu.SemaphoreType.DMA((2,))],
        to=HBM,
    )


def solution(mesh):
    in_specs = (
        P(("teach", "stud"), None),
        P(("teach", "stud"), None),
        P(("teach", "stud"), None),
        P("teach", None, "mdl"),
        P("teach", "mdl", None),
        P(None, "mdl"),
        P(None, "mdl"),
    )
    out_specs = (P(("teach", "stud"), "mdl"), P(("teach", "stud"), "mdl"))
    return jax.shard_map(
        on_device, mesh=mesh, in_specs=in_specs, out_specs=out_specs, check_vma=False
    )
```

```python
import functools

import jax
import jax.numpy as jnp
from jax import lax
from jax.experimental import pallas as pl
from jax.experimental.pallas import tpu as pltpu
from jax.sharding import PartitionSpec as P

LANES = 128
ROW_TILE = 16
PACK_ROWS = 8
PACK_TOP = 14.0
TINY = 1e-37
VMEM = pl.BlockSpec(memory_space=pltpu.VMEM)
HBM = pl.BlockSpec(memory_space=pltpu.HBM)
SMALL = pltpu.CompilerParams(vmem_limit_bytes=16 * 1024 * 1024)
LARGE = pltpu.CompilerParams(vmem_limit_bytes=56 * 1024 * 1024)


def up_to(value, step):
    return -(-value // step) * step


def is_power(size):
    return size & (size - 1) == 0


def partner_to(size, me, step):
    return me ^ step if is_power(size) else (me + step) % size


def partner_from(size, me, step):
    return me ^ step if is_power(size) else (me + size - step) % size


def send(block, axis, step):
    size = lax.axis_size(axis)
    return lax.ppermute(block, axis, [(i, partner_to(size, i, step)) for i in range(size)])


def pack(value, out):
    height = value.shape[0]
    largest = jnp.max(jnp.max(jnp.abs(value), axis=0, keepdims=True), axis=1, keepdims=True)
    power = jnp.clip(jnp.ceil(jnp.log2(jnp.maximum(largest, TINY))), -100.0, 100.0)
    out[:height] = value * jnp.exp2(PACK_TOP - power)
    out[height:] = jnp.broadcast_to(power, (PACK_ROWS, value.shape[1]))


def unpack(block):
    height = block.shape[0] - PACK_ROWS
    return block[:height] * jnp.exp2(block[height : height + 1, :1] - PACK_TOP)


def cross(block, step):
    return send(block.astype(jnp.float16), "mdl", step).astype(jnp.float32)


def dot(left, right, contract=((1,), (0,))):
    return lax.dot_general(left, right, (contract, ((), ())), preferred_element_type=jnp.float32)


def dispatch_body(owners, local, room, extra, *refs):
    sources, refs = refs[:3], refs[3:]
    outs, refs = refs[:owners], refs[owners:]
    states, task, batch, sems = refs
    rows, width = states.shape
    copies = [
        pltpu.make_async_copy(source, target, sems.at[i])
        for i, (source, target) in enumerate(zip(sources, (states, task, batch)))
    ]
    for i in (1, 2, 0):
        copies[i].start()
    copies[1].wait()
    copies[2].wait()
    me = lax.axis_index("teach")
    task_list, batch_list = task[...], batch[...]
    group = up_to(owners * local, ROW_TILE)
    named = lax.broadcasted_iota(jnp.int32, (group, rows), 0) == task_list
    earlier = lax.broadcasted_iota(jnp.int32, (rows, rows), 0) < lax.broadcasted_iota(
        jnp.int32, (rows, rows), 1
    )
    named = named.astype(jnp.float32)
    before = dot(named.astype(jnp.bfloat16), earlier.astype(jnp.float32).astype(jnp.bfloat16))
    before = jnp.sum(before * named, axis=0, keepdims=True).astype(jnp.int32)
    owner = task_list // local if local > 1 else task_list
    step = owner ^ me if is_power(owners) else (owner - me + owners) % owners
    place = step * local + task_list % local if local > 1 else step
    slot = place * room + before
    index = lax.broadcasted_iota(jnp.int32, (owners * local * room, rows), 0)
    chosen = (index == slot).astype(jnp.float32)
    head = (index % (local * room) == 0).astype(jnp.float32)
    member = (lax.broadcasted_iota(jnp.int32, (extra, rows), 0) == batch_list).astype(jnp.float32)
    tags = dot(
        (chosen + 2.0 * head).astype(jnp.bfloat16), member.astype(jnp.bfloat16), ((1,), (1,))
    ).astype(jnp.bfloat16)
    copies[0].wait()
    moved = dot(chosen.astype(jnp.bfloat16), states[...]).astype(jnp.bfloat16)
    for k, out in enumerate(outs):
        span = slice(k * local * room, (k + 1) * local * room)
        out[:, :width] = moved[span]
        out[:, width:] = tags[span]


def weights_body(*refs):
    sources, outs, sems = refs[1:5], refs[5:9], refs[9]
    copies = [
        pltpu.make_async_copy(source, target, sems.at[i])
        for i, (source, target) in enumerate(zip(sources, outs))
    ]
    for copy in copies:
        copy.start()
    for copy in copies:
        copy.wait()


def student(rows, student_up):
    pre = dot(rows, student_up[...])
    sig = 1.0 / (1.0 + jnp.exp(-pre))
    return (pre * sig).astype(jnp.bfloat16), sig * (1.0 + pre * (1.0 - sig))


def forward_body(owners, local, room, *refs):
    blocks, refs = refs[:owners], refs[owners:]
    teach_in, teach_out, student_up, student_down = refs[:4]
    tags_out, counts_out, act_out, slope_out = refs[4:8]
    halves, rows_halves, (rows_out, error_out) = refs[8:12], refs[12:14], refs[14:]
    width = rows_out.shape[1]
    full = [block[...] for block in blocks]
    counts = None
    for block in full:
        mine = jnp.floor(block[:1, width:].astype(jnp.float32) * 0.5)
        counts = mine if counts is None else counts + mine
    counts_out[...] = counts
    for l in range(local):
        span = slice(l * owners * room, (l + 1) * owners * room)
        for k, block in enumerate(full):
            start = (l * owners + k) * room
            rows_out[start : start + room] = block[l * room : (l + 1) * room, :width]
            tag = block[l * room : (l + 1) * room, width:].astype(jnp.float32)
            if l == 0:
                head = lax.broadcasted_iota(jnp.int32, tag.shape, 0) == 0
                tag = jnp.where(head, tag - 2.0 * jnp.floor(tag * 0.5), tag)
            tags_out[start : start + room] = tag
        rows = rows_out[span]
        hidden = dot(rows, teach_in[l])
        hidden = (hidden / (1.0 + jnp.exp(-hidden))).astype(jnp.bfloat16)
        act, slope = student(rows, student_up)
        act_out[span] = act
        slope_out[span] = slope
        error_out[span] = dot(act, student_down[...], ((1,), (1,))) - dot(hidden, teach_out[l])
    height = halves[0].shape[0]
    for i in range(2):
        rows_halves[i][...] = rows_out[i * height : (i + 1) * height]
        value = error_out[i * height : (i + 1) * height]
        halves[2 * i][...] = value
        pack(value, halves[2 * i + 1])


def chosen_columns(columns, owners, studs):
    height = columns // (owners * studs)
    shape = (owners * height, columns)
    row = lax.broadcasted_iota(jnp.int32, shape, 0)
    column = lax.broadcasted_iota(jnp.int32, shape, 1)
    owner = partner_to(owners, lax.axis_index("teach"), row // height)
    wanted = (owner * studs + lax.axis_index("stud")) * height + row % height
    return (column == wanted).astype(jnp.float32).astype(jnp.bfloat16)


def turn(value, owners, studs):
    chosen = chosen_columns(value.shape[1], owners, studs)
    return dot(chosen, value, ((1,), (1,))).astype(jnp.bfloat16)


def ahead_body(owners, studs, first, second, student_up, _, turned, *state):
    rows = jnp.concatenate([first[...], second[...]])
    turned[...] = turn(rows, owners, studs)
    if state:
        state[0][...], state[1][...] = student(rows, student_up)


def pair_body(*refs):
    for i in range(2):
        own, arrived = refs[2 * i : 2 * i + 2]
        total, packed = refs[2 * i + 4 : 2 * i + 6]
        value = own[...] + unpack(arrived)
        total[...] = value
        pack(value, packed)


def scale_body(*refs):
    own, tags = (*refs[2:4], *refs[:2]), refs[4]
    counts, scaled = refs[5:-1], refs[-1]
    all_counts = counts[0][...]
    for piece in counts[1:]:
        all_counts = all_counts + piece[...]
    inverse = jnp.where(all_counts > 0, 2.0 / all_counts, 0.0)
    weight = jnp.sum(tags[...] * inverse, axis=1, keepdims=True)
    height = own[0].shape[0]
    for i in range(2):
        span = slice(i * height, (i + 1) * height)
        total = own[2 * i][...] + unpack(own[2 * i + 1])
        scaled[span] = (total * weight[span]).astype(scaled.dtype)


def backward_body(owners, studs, earlier, scaled, turned, act, slope, student_down, *refs):
    error = scaled[...]
    down = dot(turn(error, owners, studs), act[...])
    pre_grad = (dot(error, student_down[...]) * slope[...]).astype(jnp.bfloat16)
    up = dot(turned[...], pre_grad)
    if earlier:
        up, down = up + refs[0][...], down + refs[1][...]
    outs = refs[2 * earlier :]
    if len(outs) == 2:
        outs[0][...], outs[1][...] = up, down
        return
    high, low = up.shape[0] // owners, down.shape[0] // owners
    for k, out in enumerate(outs):
        block = [up[k * high : (k + 1) * high], down[k * low : (k + 1) * low]]
        out[...] = jnp.concatenate(block).astype(out.dtype)


def closing_body(*refs):
    pieces, (grad_up, grad_down, up, down, sems) = refs[:-5], refs[-5:]
    total = pieces[0][...]
    for piece in pieces[1:]:
        total = total + piece[...].astype(jnp.float32)
    cut = up.shape[0]
    up[...] = total[:cut]
    first = pltpu.make_async_copy(up, grad_up, sems.at[0])
    first.start()
    down[...] = total[cut:]
    second = pltpu.make_async_copy(down, grad_down, sems.at[1])
    second.start()
    first.wait()
    second.wait()


def kernel(body, outs, operands, flops, scratch=(), params=SMALL, places=None, to=VMEM):
    return pl.pallas_call(
        body,
        out_shape=outs,
        in_specs=places or [VMEM] * len(operands),
        out_specs=[to] * len(outs),
        scratch_shapes=list(scratch),
        cost_estimate=pl.CostEstimate(flops=flops, bytes_accessed=0, transcendentals=0),
        compiler_params=params,
    )(*operands)


def on_device(states, task_ids, student_batch, teach_in, teach_out, student_up, student_down):
    row_count, width = states.shape
    owners, studs, parts = lax.axis_size("teach"), lax.axis_size("stud"), lax.axis_size("mdl")
    local, _, hidden = teach_in.shape
    actions = teach_out.shape[2]
    units = student_up.shape[1]
    teachers, batches = owners * local, owners * studs
    room = up_to(3 * row_count // (2 * teachers), ROW_TILE)
    extra = up_to(batches, LANES)
    slots = teachers * room
    f32, bf16 = jnp.float32, jnp.bfloat16

    def shape(rows, columns, dtype):
        return jax.ShapeDtypeStruct((rows, columns), dtype)

    height = slots // 2
    half, packed = shape(height, actions, f32), shape(height + PACK_ROWS, actions, f32)
    state = [shape(slots, units, bf16), shape(slots, units, f32)]
    tokens = [ids.reshape(1, row_count) for ids in (task_ids, student_batch)]
    blocks = kernel(
        functools.partial(dispatch_body, owners, local, room, extra),
        [pltpu.VMEM((local * room, width + extra), bf16)] * owners,
        (states, *tokens),
        2 * slots * row_count * width,
        [pltpu.VMEM(a.shape, a.dtype) for a in (states, *tokens)] + [pltpu.SemaphoreType.DMA((3,))],
        LARGE,
        [HBM] * 3,
    )
    arrived = {k: send(blocks[k], "teach", k) for k in range(owners - 1, 0, -1)}
    weights = (teach_in, teach_out, student_up, student_down)
    weights = kernel(
        weights_body,
        [pltpu.VMEM(w.shape, w.dtype) for w in weights],
        (blocks[0], *[pltpu.with_memory_space_constraint(w, pltpu.HBM) for w in weights]),
        0,
        [pltpu.SemaphoreType.DMA((4,))],
        SMALL,
        [VMEM] + [HBM] * 4,
    )
    blocks = [blocks[0]] + list(arrived.values())
    tags, counts, act, slope, first, first_out, second, second_out, *rows = kernel(
        functools.partial(forward_body, owners, local, room),
        [shape(slots, extra, f32), shape(1, extra, f32), *state]
        + [half, packed] * 2
        + [shape(height, width, bf16)] * 2,
        (*blocks, *weights),
        4 * slots * width * (hidden + units),
        [pltpu.VMEM((slots, width), bf16), pltpu.VMEM((slots, actions), f32)],
    )
    steps = [1 << i for i in range(parts.bit_length() - 1)]
    first_in, second_in = cross(first_out, steps[0]), cross(second_out, steps[-1])
    all_counts, mates = [counts], []
    for k in range(1, studs):
        all_counts.append(send(counts, "stud", k))
        mates.append([send(part, "stud", k) for part in rows])
    first_in, second_in, all_counts, mates = lax.optimization_barrier(
        (first_in, second_in, all_counts, mates)
    )
    for there, back in zip(steps[1:], steps[-2::-1]):
        first, first_out, second, second_out = kernel(
            pair_body, [half, packed] * 2, (first, first_in, second, second_in), 0
        )
        first_in, second_in = cross(first_out, there), cross(second_out, back)
    ahead = functools.partial(ahead_body, owners, studs)
    turned = shape(width // studs, slots, bf16)
    (ours,) = kernel(ahead, [turned], (*rows, weights[2], second), 0)
    known = [kernel(ahead, [turned] + state, (*theirs, weights[2], second), 0) for theirs in mates]
    sums = (second, second_in, first, first_in)
    sums, all_counts, known, ours = lax.optimization_barrier((sums, all_counts, known, ours))
    (scaled,) = kernel(scale_body, [shape(slots, actions, bf16)], (*sums, tags, *all_counts), 0)
    work = 6 * slots * width * units
    grads = [shape(width // studs, units, f32), shape(actions // studs, units, f32)]
    heights = [g.shape[0] // owners for g in grads]
    blocks = [shape(sum(heights), units, f32)] + [shape(sum(heights), units, bf16)] * (owners - 1)
    errors = [scaled] + [send(scaled, "stud", k) for k in range(1, studs)]
    states = [[ours, act, slope]] + known
    sums = []
    for k, (error, state) in enumerate(zip(errors, states)):
        sums = kernel(
            functools.partial(backward_body, owners, studs, k > 0),
            blocks if k == studs - 1 else grads,
            (error, *state, weights[3], *sums),
            work,
        )
    pieces = [sums[0]] + [send(sums[k], "teach", k) for k in range(owners - 1, 0, -1)]
    outs = [shape(h, units, f32) for h in heights]
    return kernel(
        closing_body,
        outs,
        pieces,
        0,
        [pltpu.VMEM(o.shape, f32) for o in outs] + [pltpu.SemaphoreType.DMA((2,))],
        to=HBM,
    )


def solution(mesh):
    in_specs = (
        P(("teach", "stud"), None),
        P(("teach", "stud"), None),
        P(("teach", "stud"), None),
        P("teach", None, "mdl"),
        P("teach", "mdl", None),
        P(None, "mdl"),
        P(None, "mdl"),
    )
    out_specs = (P(("teach", "stud"), "mdl"), P(("teach", "stud"), "mdl"))
    return jax.shard_map(
        on_device, mesh=mesh, in_specs=in_specs, out_specs=out_specs, check_vma=False
    )
```

```python
import functools

import jax
import jax.numpy as jnp
from jax import lax
from jax.experimental import pallas as pl
from jax.experimental.pallas import tpu as pltpu
from jax.sharding import PartitionSpec as P

LANES = 128
ROW_TILE = 16
PACK_ROWS = 8
PACK_TOP = 14.0
TINY = 1e-37
VMEM = pl.BlockSpec(memory_space=pltpu.VMEM)
HBM = pl.BlockSpec(memory_space=pltpu.HBM)
SMALL = pltpu.CompilerParams(vmem_limit_bytes=16 * 1024 * 1024)
LARGE = pltpu.CompilerParams(vmem_limit_bytes=56 * 1024 * 1024)


def up_to(value, step):
    return -(-value // step) * step


def is_power(size):
    return size & (size - 1) == 0


def partner_to(size, me, step):
    return me ^ step if is_power(size) else (me + step) % size


def partner_from(size, me, step):
    return me ^ step if is_power(size) else (me + size - step) % size


def send(block, axis, step):
    size = lax.axis_size(axis)
    return lax.ppermute(block, axis, [(i, partner_to(size, i, step)) for i in range(size)])


def pack(value, out):
    height = value.shape[0]
    largest = jnp.max(jnp.max(jnp.abs(value), axis=0, keepdims=True), axis=1, keepdims=True)
    power = jnp.clip(jnp.ceil(jnp.log2(jnp.maximum(largest, TINY))), -100.0, 100.0)
    out[:height] = value * jnp.exp2(PACK_TOP - power)
    out[height:] = jnp.broadcast_to(power, (PACK_ROWS, value.shape[1]))


def unpack(block):
    height = block.shape[0] - PACK_ROWS
    return block[:height] * jnp.exp2(block[height : height + 1, :1] - PACK_TOP)


def cross(block, step):
    return send(block.astype(jnp.float16), "mdl", step).astype(jnp.float32)


def dot(left, right, contract=((1,), (0,))):
    return lax.dot_general(left, right, (contract, ((), ())), preferred_element_type=jnp.float32)


def dispatch_body(owners, local, room, extra, *refs):
    sources, refs = refs[:3], refs[3:]
    outs, refs = refs[:owners], refs[owners:]
    states, task, batch, sems = refs
    rows, width = states.shape
    copies = [
        pltpu.make_async_copy(source, target, sems.at[i])
        for i, (source, target) in enumerate(zip(sources, (states, task, batch)))
    ]
    for i in (1, 2, 0):
        copies[i].start()
    copies[1].wait()
    copies[2].wait()
    me = lax.axis_index("teach")
    task_list, batch_list = task[...], batch[...]
    group = up_to(owners * local, ROW_TILE)
    named = lax.broadcasted_iota(jnp.int32, (group, rows), 0) == task_list
    earlier = lax.broadcasted_iota(jnp.int32, (rows, rows), 0) < lax.broadcasted_iota(
        jnp.int32, (rows, rows), 1
    )
    named = named.astype(jnp.float32)
    before = dot(named.astype(jnp.bfloat16), earlier.astype(jnp.float32).astype(jnp.bfloat16))
    before = jnp.sum(before * named, axis=0, keepdims=True).astype(jnp.int32)
    owner = task_list // local if local > 1 else task_list
    step = owner ^ me if is_power(owners) else (owner - me + owners) % owners
    place = step * local + task_list % local if local > 1 else step
    slot = place * room + before
    index = lax.broadcasted_iota(jnp.int32, (owners * local * room, rows), 0)
    chosen = (index == slot).astype(jnp.float32)
    head = (index % (local * room) == 0).astype(jnp.float32)
    member = (lax.broadcasted_iota(jnp.int32, (extra, rows), 0) == batch_list).astype(jnp.float32)
    tags = dot(
        (chosen + 2.0 * head).astype(jnp.bfloat16), member.astype(jnp.bfloat16), ((1,), (1,))
    ).astype(jnp.bfloat16)
    copies[0].wait()
    moved = dot(chosen.astype(jnp.bfloat16), states[...]).astype(jnp.bfloat16)
    for k, out in enumerate(outs):
        span = slice(k * local * room, (k + 1) * local * room)
        out[:, :width] = moved[span]
        out[:, width:] = tags[span]


def weights_body(*refs):
    sources, outs, sems = refs[1:5], refs[5:9], refs[9]
    copies = [
        pltpu.make_async_copy(source, target, sems.at[i])
        for i, (source, target) in enumerate(zip(sources, outs))
    ]
    for copy in copies:
        copy.start()
    for copy in copies:
        copy.wait()


def student(rows, student_up):
    pre = dot(rows, student_up[...])
    sig = 1.0 / (1.0 + jnp.exp(-pre))
    return (pre * sig).astype(jnp.bfloat16), sig * (1.0 + pre * (1.0 - sig))


def forward_body(owners, local, room, *refs):
    blocks, refs = refs[:owners], refs[owners:]
    teach_in, teach_out, student_up, student_down = refs[:4]
    tags_out, counts_out, act_out, slope_out = refs[4:8]
    halves, rows_halves, (rows_out, error_out) = refs[8:12], refs[12:14], refs[14:]
    width = rows_out.shape[1]
    full = [block[...] for block in blocks]
    counts = None
    for block in full:
        mine = jnp.floor(block[:1, width:].astype(jnp.float32) * 0.5)
        counts = mine if counts is None else counts + mine
    counts_out[...] = counts
    for l in range(local):
        span = slice(l * owners * room, (l + 1) * owners * room)
        for k, block in enumerate(full):
            start = (l * owners + k) * room
            rows_out[start : start + room] = block[l * room : (l + 1) * room, :width]
            tag = block[l * room : (l + 1) * room, width:].astype(jnp.float32)
            if l == 0:
                head = lax.broadcasted_iota(jnp.int32, tag.shape, 0) == 0
                tag = jnp.where(head, tag - 2.0 * jnp.floor(tag * 0.5), tag)
            tags_out[start : start + room] = tag
        rows = rows_out[span]
        hidden = dot(rows, teach_in[l])
        hidden = (hidden / (1.0 + jnp.exp(-hidden))).astype(jnp.bfloat16)
        act, slope = student(rows, student_up)
        act_out[span] = act
        slope_out[span] = slope
        error_out[span] = dot(act, student_down[...], ((1,), (1,))) - dot(hidden, teach_out[l])
    cut = halves[0].shape[0]
    for i, span in enumerate((slice(0, cut), slice(cut, None))):
        rows_halves[i][...] = rows_out[span]
        value = error_out[span]
        halves[2 * i][...] = value
        pack(value, halves[2 * i + 1])


def chosen_columns(columns, owners, studs):
    height = columns // (owners * studs)
    shape = (owners * height, columns)
    row = lax.broadcasted_iota(jnp.int32, shape, 0)
    column = lax.broadcasted_iota(jnp.int32, shape, 1)
    owner = partner_to(owners, lax.axis_index("teach"), row // height)
    wanted = (owner * studs + lax.axis_index("stud")) * height + row % height
    return (column == wanted).astype(jnp.float32).astype(jnp.bfloat16)


def turn(value, owners, studs):
    chosen = chosen_columns(value.shape[1], owners, studs)
    return dot(chosen, value, ((1,), (1,))).astype(jnp.bfloat16)


def ahead_body(owners, studs, first, second, student_up, _, turned, *state):
    rows = jnp.concatenate([first[...], second[...]])
    turned[...] = turn(rows, owners, studs)
    if state:
        state[0][...], state[1][...] = student(rows, student_up)


def pair_body(own, arrived, *refs):
    total, packed = refs[-2:]
    value = own[...] + unpack(arrived)
    total[...] = value
    pack(value, packed)


def scale_body(*refs):
    own, tags = (*refs[2:4], *refs[:2]), refs[4]
    counts, scaled = refs[5:-1], refs[-1]
    all_counts = counts[0][...]
    for piece in counts[1:]:
        all_counts = all_counts + piece[...]
    inverse = jnp.where(all_counts > 0, 2.0 / all_counts, 0.0)
    weight = jnp.sum(tags[...] * inverse, axis=1, keepdims=True)
    cut = own[0].shape[0]
    for i, span in enumerate((slice(0, cut), slice(cut, None))):
        total = own[2 * i][...] + unpack(own[2 * i + 1])
        scaled[span] = (total * weight[span]).astype(scaled.dtype)


def backward_body(owners, studs, earlier, scaled, turned, act, slope, student_down, *refs):
    error = scaled[...]
    down = dot(turn(error, owners, studs), act[...])
    pre_grad = (dot(error, student_down[...]) * slope[...]).astype(jnp.bfloat16)
    up = dot(turned[...], pre_grad)
    if earlier:
        up, down = up + refs[0][...], down + refs[1][...]
    outs = refs[2 * earlier :]
    if len(outs) == 2:
        outs[0][...], outs[1][...] = up, down
        return
    high, low = up.shape[0] // owners, down.shape[0] // owners
    for k, out in enumerate(outs):
        block = [up[k * high : (k + 1) * high], down[k * low : (k + 1) * low]]
        out[...] = jnp.concatenate(block).astype(out.dtype)


def closing_body(*refs):
    pieces, (grad_up, grad_down, up, down, sems) = refs[:-5], refs[-5:]
    total = pieces[0][...]
    for piece in pieces[1:]:
        total = total + piece[...].astype(jnp.float32)
    cut = up.shape[0]
    up[...] = total[:cut]
    first = pltpu.make_async_copy(up, grad_up, sems.at[0])
    first.start()
    down[...] = total[cut:]
    second = pltpu.make_async_copy(down, grad_down, sems.at[1])
    second.start()
    first.wait()
    second.wait()


def kernel(body, outs, operands, flops, scratch=(), params=SMALL, places=None, to=VMEM):
    return pl.pallas_call(
        body,
        out_shape=outs,
        in_specs=places or [VMEM] * len(operands),
        out_specs=[to] * len(outs),
        scratch_shapes=list(scratch),
        cost_estimate=pl.CostEstimate(flops=flops, bytes_accessed=0, transcendentals=0),
        compiler_params=params,
    )(*operands)


def on_device(states, task_ids, student_batch, teach_in, teach_out, student_up, student_down):
    row_count, width = states.shape
    owners, studs, parts = lax.axis_size("teach"), lax.axis_size("stud"), lax.axis_size("mdl")
    local, _, hidden = teach_in.shape
    actions = teach_out.shape[2]
    units = student_up.shape[1]
    teachers, batches = owners * local, owners * studs
    room = up_to(3 * row_count // (2 * teachers), ROW_TILE)
    extra = up_to(batches, LANES)
    slots = teachers * room
    f32, bf16 = jnp.float32, jnp.bfloat16

    def shape(rows, columns, dtype):
        return jax.ShapeDtypeStruct((rows, columns), dtype)

    heights = (slots // 2 + ROW_TILE, slots // 2 - ROW_TILE)
    part = [[shape(h, actions, f32), shape(h + PACK_ROWS, actions, f32)] for h in heights]
    state = [shape(slots, units, bf16), shape(slots, units, f32)]
    tokens = [ids.reshape(1, row_count) for ids in (task_ids, student_batch)]
    blocks = kernel(
        functools.partial(dispatch_body, owners, local, room, extra),
        [pltpu.VMEM((local * room, width + extra), bf16)] * owners,
        (states, *tokens),
        2 * slots * row_count * width,
        [pltpu.VMEM(a.shape, a.dtype) for a in (states, *tokens)] + [pltpu.SemaphoreType.DMA((3,))],
        LARGE,
        [HBM] * 3,
    )
    arrived = {k: send(blocks[k], "teach", k) for k in range(owners - 1, 0, -1)}
    weights = (teach_in, teach_out, student_up, student_down)
    weights = kernel(
        weights_body,
        [pltpu.VMEM(w.shape, w.dtype) for w in weights],
        (blocks[0], *[pltpu.with_memory_space_constraint(w, pltpu.HBM) for w in weights]),
        0,
        [pltpu.SemaphoreType.DMA((4,))],
        SMALL,
        [VMEM] + [HBM] * 4,
    )
    blocks = [blocks[0]] + list(arrived.values())
    tags, counts, act, slope, first, first_out, second, second_out, *rows = kernel(
        functools.partial(forward_body, owners, local, room),
        [shape(slots, extra, f32), shape(1, extra, f32), *state]
        + part[0]
        + part[1]
        + [shape(h, width, bf16) for h in heights],
        (*blocks, *weights),
        4 * slots * width * (hidden + units),
        [pltpu.VMEM((slots, width), bf16), pltpu.VMEM((slots, actions), f32)],
    )
    steps = [1 << i for i in range(parts.bit_length() - 1)]
    first_in, second_in = cross(first_out, steps[0]), cross(second_out, steps[-1])
    all_counts, mates = [counts], []
    for k in range(1, studs):
        all_counts.append(send(counts, "stud", k))
        mates.append([send(part, "stud", k) for part in rows])
    for there, back in zip(steps[1:], steps[-2::-1]):
        first, first_out = kernel(pair_body, part[0], (first, first_in), 0)
        first_in = cross(first_out, there)
        second, second_out = kernel(pair_body, part[1], (second, second_in, first), 0)
        second_in = cross(second_out, back)
    ahead = functools.partial(ahead_body, owners, studs)
    turned = shape(width // studs, slots, bf16)
    (ours,) = kernel(ahead, [turned], (*rows, weights[2], second), 0)
    known = [kernel(ahead, [turned] + state, (*theirs, weights[2], second), 0) for theirs in mates]
    sums = (second, second_in, first, first_in)
    sums, all_counts, known, ours = lax.optimization_barrier((sums, all_counts, known, ours))
    (scaled,) = kernel(scale_body, [shape(slots, actions, bf16)], (*sums, tags, *all_counts), 0)
    work = 6 * slots * width * units
    grads = [shape(width // studs, units, f32), shape(actions // studs, units, f32)]
    heights = [g.shape[0] // owners for g in grads]
    blocks = [shape(sum(heights), units, f32)] + [shape(sum(heights), units, bf16)] * (owners - 1)
    errors = [scaled] + [send(scaled, "stud", k) for k in range(1, studs)]
    states = [[ours, act, slope]] + known
    sums = []
    for k, (error, state) in enumerate(zip(errors, states)):
        sums = kernel(
            functools.partial(backward_body, owners, studs, k > 0),
            blocks if k == studs - 1 else grads,
            (error, *state, weights[3], *sums),
            work,
        )
    pieces = [sums[0]] + [send(sums[k], "teach", k) for k in range(owners - 1, 0, -1)]
    outs = [shape(h, units, f32) for h in heights]
    return kernel(
        closing_body,
        outs,
        pieces,
        0,
        [pltpu.VMEM(o.shape, f32) for o in outs] + [pltpu.SemaphoreType.DMA((2,))],
        to=HBM,
    )


def solution(mesh):
    in_specs = (
        P(("teach", "stud"), None),
        P(("teach", "stud"), None),
        P(("teach", "stud"), None),
        P("teach", None, "mdl"),
        P("teach", "mdl", None),
        P(None, "mdl"),
        P(None, "mdl"),
    )
    out_specs = (P(("teach", "stud"), "mdl"), P(("teach", "stud"), "mdl"))
    return jax.shard_map(
        on_device, mesh=mesh, in_specs=in_specs, out_specs=out_specs, check_vma=False
    )
```

```python
import functools

import jax
import jax.numpy as jnp
from jax import lax
from jax.experimental import pallas as pl
from jax.experimental.pallas import tpu as pltpu
from jax.sharding import PartitionSpec as P

LANES = 128
ROW_TILE = 16
PACK_ROWS = 8
PACK_TOP = 14.0
TINY = 1e-37
VMEM = pl.BlockSpec(memory_space=pltpu.VMEM)
HBM = pl.BlockSpec(memory_space=pltpu.HBM)
SMALL = pltpu.CompilerParams(vmem_limit_bytes=16 * 1024 * 1024)
LARGE = pltpu.CompilerParams(vmem_limit_bytes=56 * 1024 * 1024)


def up_to(value, step):
    return -(-value // step) * step


def is_power(size):
    return size & (size - 1) == 0


def partner_to(size, me, step):
    return me ^ step if is_power(size) else (me + step) % size


def partner_from(size, me, step):
    return me ^ step if is_power(size) else (me + size - step) % size


def send(block, axis, step):
    size = lax.axis_size(axis)
    return lax.ppermute(block, axis, [(i, partner_to(size, i, step)) for i in range(size)])


def pack(value, out):
    height = value.shape[0]
    largest = jnp.max(jnp.max(jnp.abs(value), axis=0, keepdims=True), axis=1, keepdims=True)
    power = jnp.clip(jnp.ceil(jnp.log2(jnp.maximum(largest, TINY))), -100.0, 100.0)
    out[:height] = value * jnp.exp2(PACK_TOP - power)
    out[height:] = jnp.broadcast_to(power, (PACK_ROWS, value.shape[1]))


def unpack(block):
    height = block.shape[0] - PACK_ROWS
    return block[:height] * jnp.exp2(block[height : height + 1, :1] - PACK_TOP)


def cross(block, step):
    return send(block.astype(jnp.float16), "mdl", step).astype(jnp.float32)


def dot(left, right, contract=((1,), (0,))):
    return lax.dot_general(left, right, (contract, ((), ())), preferred_element_type=jnp.float32)


def dispatch_body(owners, local, room, extra, *refs):
    sources, refs = refs[:3], refs[3:]
    outs, refs = refs[:owners], refs[owners:]
    states, task, batch, sems = refs
    rows, width = states.shape
    copies = [
        pltpu.make_async_copy(source, target, sems.at[i])
        for i, (source, target) in enumerate(zip(sources, (states, task, batch)))
    ]
    for i in (1, 2, 0):
        copies[i].start()
    copies[1].wait()
    copies[2].wait()
    me = lax.axis_index("teach")
    task_list, batch_list = task[...], batch[...]
    group = up_to(owners * local, ROW_TILE)
    named = lax.broadcasted_iota(jnp.int32, (group, rows), 0) == task_list
    earlier = lax.broadcasted_iota(jnp.int32, (rows, rows), 0) < lax.broadcasted_iota(
        jnp.int32, (rows, rows), 1
    )
    named = named.astype(jnp.float32)
    before = dot(named.astype(jnp.bfloat16), earlier.astype(jnp.float32).astype(jnp.bfloat16))
    before = jnp.sum(before * named, axis=0, keepdims=True).astype(jnp.int32)
    owner = task_list // local if local > 1 else task_list
    step = owner ^ me if is_power(owners) else (owner - me + owners) % owners
    place = step * local + task_list % local if local > 1 else step
    slot = place * room + before
    index = lax.broadcasted_iota(jnp.int32, (owners * local * room, rows), 0)
    chosen = (index == slot).astype(jnp.float32)
    head = (index % (local * room) == 0).astype(jnp.float32)
    member = (lax.broadcasted_iota(jnp.int32, (extra, rows), 0) == batch_list).astype(jnp.float32)
    tags = dot(
        (chosen + 2.0 * head).astype(jnp.bfloat16), member.astype(jnp.bfloat16), ((1,), (1,))
    ).astype(jnp.bfloat16)
    copies[0].wait()
    moved = dot(chosen.astype(jnp.bfloat16), states[...]).astype(jnp.bfloat16)
    for k, out in enumerate(outs):
        span = slice(k * local * room, (k + 1) * local * room)
        out[:, :width] = moved[span]
        out[:, width:] = tags[span]


def weights_body(*refs):
    sources, outs, sems = refs[1:5], refs[5:9], refs[9]
    copies = [
        pltpu.make_async_copy(source, target, sems.at[i])
        for i, (source, target) in enumerate(zip(sources, outs))
    ]
    for copy in copies:
        copy.start()
    for copy in copies:
        copy.wait()


def student(rows, student_up):
    pre = dot(rows, student_up[...])
    sig = 1.0 / (1.0 + jnp.exp(-pre))
    return (pre * sig).astype(jnp.bfloat16), sig * (1.0 + pre * (1.0 - sig))


def forward_body(owners, local, room, *refs):
    blocks, refs = refs[:owners], refs[owners:]
    teach_in, teach_out, student_up, student_down = refs[:4]
    tags_out, counts_out, act_out, slope_out = refs[4:8]
    halves, rows_halves, (rows_out, error_out) = refs[8:12], refs[12:14], refs[14:]
    width = rows_out.shape[1]
    full = [block[...] for block in blocks]
    counts = None
    for block in full:
        mine = jnp.floor(block[:1, width:].astype(jnp.float32) * 0.5)
        counts = mine if counts is None else counts + mine
    counts_out[...] = counts
    for l in range(local):
        span = slice(l * owners * room, (l + 1) * owners * room)
        for k, block in enumerate(full):
            start = (l * owners + k) * room
            rows_out[start : start + room] = block[l * room : (l + 1) * room, :width]
            tag = block[l * room : (l + 1) * room, width:].astype(jnp.float32)
            if l == 0:
                head = lax.broadcasted_iota(jnp.int32, tag.shape, 0) == 0
                tag = jnp.where(head, tag - 2.0 * jnp.floor(tag * 0.5), tag)
            tags_out[start : start + room] = tag
        rows = rows_out[span]
        hidden = dot(rows, teach_in[l])
        hidden = (hidden / (1.0 + jnp.exp(-hidden))).astype(jnp.bfloat16)
        act, slope = student(rows, student_up)
        act_out[span] = act
        slope_out[span] = slope
        error_out[span] = dot(act, student_down[...], ((1,), (1,))) - dot(hidden, teach_out[l])
    cut = halves[0].shape[0]
    for i, span in enumerate((slice(0, cut), slice(cut, None))):
        rows_halves[i][...] = rows_out[span]
        value = error_out[span]
        halves[2 * i][...] = value
        pack(value, halves[2 * i + 1])


def chosen_columns(columns, owners, studs):
    height = columns // (owners * studs)
    shape = (owners * height, columns)
    row = lax.broadcasted_iota(jnp.int32, shape, 0)
    column = lax.broadcasted_iota(jnp.int32, shape, 1)
    owner = partner_to(owners, lax.axis_index("teach"), row // height)
    wanted = (owner * studs + lax.axis_index("stud")) * height + row % height
    return (column == wanted).astype(jnp.float32).astype(jnp.bfloat16)


def turn(value, owners, studs):
    chosen = chosen_columns(value.shape[1], owners, studs)
    return dot(chosen, value, ((1,), (1,))).astype(jnp.bfloat16)


def ahead_body(owners, studs, first, second, student_up, _, turned, *state):
    rows = jnp.concatenate([first[...], second[...]])
    turned[...] = turn(rows, owners, studs)
    if state:
        state[0][...], state[1][...] = student(rows, student_up)


def pair_body(own, arrived, *refs):
    total, packed = refs[-2:]
    value = own[...] + unpack(arrived)
    total[...] = value
    pack(value, packed)


def scale_body(*refs):
    own, tags = (*refs[2:4], *refs[:2]), refs[4]
    counts, scaled = refs[5:-1], refs[-1]
    all_counts = counts[0][...]
    for piece in counts[1:]:
        all_counts = all_counts + piece[...]
    inverse = jnp.where(all_counts > 0, 2.0 / all_counts, 0.0)
    weight = jnp.sum(tags[...] * inverse, axis=1, keepdims=True)
    cut = own[0].shape[0]
    for i, span in enumerate((slice(0, cut), slice(cut, None))):
        total = own[2 * i][...] + unpack(own[2 * i + 1])
        scaled[span] = (total * weight[span]).astype(scaled.dtype)


def backward_body(owners, studs, earlier, scaled, turned, act, slope, student_down, *refs):
    error = scaled[...]
    down = dot(turn(error, owners, studs), act[...])
    pre_grad = (dot(error, student_down[...]) * slope[...]).astype(jnp.bfloat16)
    up = dot(turned[...], pre_grad)
    if earlier:
        up, down = up + refs[0][...], down + refs[1][...]
    outs = refs[2 * earlier :]
    if len(outs) == 2:
        outs[0][...], outs[1][...] = up, down
        return
    high, low = up.shape[0] // owners, down.shape[0] // owners
    for k, out in enumerate(outs):
        block = [up[k * high : (k + 1) * high], down[k * low : (k + 1) * low]]
        out[...] = jnp.concatenate(block).astype(out.dtype)


def closing_body(*refs):
    pieces, (grad_up, grad_down, up, down, sems) = refs[:-5], refs[-5:]
    total = pieces[0][...]
    for piece in pieces[1:]:
        total = total + piece[...].astype(jnp.float32)
    cut = up.shape[0]
    up[...] = total[:cut]
    first = pltpu.make_async_copy(up, grad_up, sems.at[0])
    first.start()
    down[...] = total[cut:]
    second = pltpu.make_async_copy(down, grad_down, sems.at[1])
    second.start()
    first.wait()
    second.wait()


def kernel(body, outs, operands, flops, scratch=(), params=SMALL, places=None, to=VMEM):
    return pl.pallas_call(
        body,
        out_shape=outs,
        in_specs=places or [VMEM] * len(operands),
        out_specs=[to] * len(outs),
        scratch_shapes=list(scratch),
        cost_estimate=pl.CostEstimate(flops=flops, bytes_accessed=0, transcendentals=0),
        compiler_params=params,
    )(*operands)


def on_device(states, task_ids, student_batch, teach_in, teach_out, student_up, student_down):
    row_count, width = states.shape
    owners, studs, parts = lax.axis_size("teach"), lax.axis_size("stud"), lax.axis_size("mdl")
    local, _, hidden = teach_in.shape
    actions = teach_out.shape[2]
    units = student_up.shape[1]
    teachers, batches = owners * local, owners * studs
    room = up_to(3 * row_count // (2 * teachers), ROW_TILE)
    extra = up_to(batches, LANES)
    slots = teachers * room
    f32, bf16 = jnp.float32, jnp.bfloat16

    def shape(rows, columns, dtype):
        return jax.ShapeDtypeStruct((rows, columns), dtype)

    heights = (slots // 2 + ROW_TILE, slots // 2 - ROW_TILE)
    part = [[shape(h, actions, f32), shape(h + PACK_ROWS, actions, f32)] for h in heights]
    state = [shape(slots, units, bf16), shape(slots, units, f32)]
    tokens = [ids.reshape(1, row_count) for ids in (task_ids, student_batch)]
    blocks = kernel(
        functools.partial(dispatch_body, owners, local, room, extra),
        [pltpu.VMEM((local * room, width + extra), bf16)] * owners,
        (states, *tokens),
        2 * slots * row_count * width,
        [pltpu.VMEM(a.shape, a.dtype) for a in (states, *tokens)] + [pltpu.SemaphoreType.DMA((3,))],
        LARGE,
        [HBM] * 3,
    )
    arrived = {k: send(blocks[k], "teach", k) for k in range(owners - 1, 0, -1)}
    weights = (teach_in, teach_out, student_up, student_down)
    weights = kernel(
        weights_body,
        [pltpu.VMEM(w.shape, w.dtype) for w in weights],
        (blocks[0], *[pltpu.with_memory_space_constraint(w, pltpu.HBM) for w in weights]),
        0,
        [pltpu.SemaphoreType.DMA((4,))],
        SMALL,
        [VMEM] + [HBM] * 4,
    )
    blocks = [blocks[0]] + list(arrived.values())
    tags, counts, act, slope, first, first_out, second, second_out, *rows = kernel(
        functools.partial(forward_body, owners, local, room),
        [shape(slots, extra, f32), shape(1, extra, f32), *state]
        + part[0]
        + part[1]
        + [shape(h, width, bf16) for h in heights],
        (*blocks, *weights),
        4 * slots * width * (hidden + units),
        [pltpu.VMEM((slots, width), bf16), pltpu.VMEM((slots, actions), f32)],
    )
    steps = [1 << i for i in range(parts.bit_length() - 1)]
    first_in, second_in = cross(first_out, steps[0]), cross(second_out, steps[-1])
    all_counts, mates = [counts], []
    for k in range(1, studs):
        all_counts.append(send(counts, "stud", k))
        mates.append([send(part, "stud", k) for part in rows])
    first_in, all_counts = lax.optimization_barrier((first_in, all_counts))
    for there, back in zip(steps[1:], steps[-2::-1]):
        first, first_out = kernel(pair_body, part[0], (first, first_in), 0)
        first_in = cross(first_out, there)
        second, second_out = kernel(pair_body, part[1], (second, second_in, first), 0)
        second_in = cross(second_out, back)
    ahead = functools.partial(ahead_body, owners, studs)
    turned = shape(width // studs, slots, bf16)
    (ours,) = kernel(ahead, [turned], (*rows, weights[2], second), 0)
    known = [kernel(ahead, [turned] + state, (*theirs, weights[2], second), 0) for theirs in mates]
    sums = (second, second_in, first, first_in)
    sums, all_counts, known, ours = lax.optimization_barrier((sums, all_counts, known, ours))
    (scaled,) = kernel(scale_body, [shape(slots, actions, bf16)], (*sums, tags, *all_counts), 0)
    work = 6 * slots * width * units
    grads = [shape(width // studs, units, f32), shape(actions // studs, units, f32)]
    heights = [g.shape[0] // owners for g in grads]
    blocks = [shape(sum(heights), units, f32)] + [shape(sum(heights), units, bf16)] * (owners - 1)
    errors = [scaled] + [send(scaled, "stud", k) for k in range(1, studs)]
    states = [[ours, act, slope]] + known
    sums = []
    for k, (error, state) in enumerate(zip(errors, states)):
        sums = kernel(
            functools.partial(backward_body, owners, studs, k > 0),
            blocks if k == studs - 1 else grads,
            (error, *state, weights[3], *sums),
            work,
        )
    pieces = [sums[0]] + [send(sums[k], "teach", k) for k in range(owners - 1, 0, -1)]
    outs = [shape(h, units, f32) for h in heights]
    return kernel(
        closing_body,
        outs,
        pieces,
        0,
        [pltpu.VMEM(o.shape, f32) for o in outs] + [pltpu.SemaphoreType.DMA((2,))],
        to=HBM,
    )


def solution(mesh):
    in_specs = (
        P(("teach", "stud"), None),
        P(("teach", "stud"), None),
        P(("teach", "stud"), None),
        P("teach", None, "mdl"),
        P("teach", "mdl", None),
        P(None, "mdl"),
        P(None, "mdl"),
    )
    out_specs = (P(("teach", "stud"), "mdl"), P(("teach", "stud"), "mdl"))
    return jax.shard_map(
        on_device, mesh=mesh, in_specs=in_specs, out_specs=out_specs, check_vma=False
    )
```

```python
import functools

import jax
import jax.numpy as jnp
from jax import lax
from jax.experimental import pallas as pl
from jax.experimental.pallas import tpu as pltpu
from jax.sharding import PartitionSpec as P

LANES = 128
ROW_TILE = 16
PACK_ROWS = 8
PACK_TOP = 14.0
TINY = 1e-37
VMEM = pl.BlockSpec(memory_space=pltpu.VMEM)
HBM = pl.BlockSpec(memory_space=pltpu.HBM)
SMALL = pltpu.CompilerParams(vmem_limit_bytes=16 * 1024 * 1024)
LARGE = pltpu.CompilerParams(vmem_limit_bytes=56 * 1024 * 1024)


def up_to(value, step):
    return -(-value // step) * step


def is_power(size):
    return size & (size - 1) == 0


def partner_to(size, me, step):
    return me ^ step if is_power(size) else (me + step) % size


def partner_from(size, me, step):
    return me ^ step if is_power(size) else (me + size - step) % size


def send(block, axis, step):
    size = lax.axis_size(axis)
    return lax.ppermute(block, axis, [(i, partner_to(size, i, step)) for i in range(size)])


def pack(value, out):
    height = value.shape[0]
    largest = jnp.max(jnp.max(jnp.abs(value), axis=0, keepdims=True), axis=1, keepdims=True)
    power = jnp.clip(jnp.ceil(jnp.log2(jnp.maximum(largest, TINY))), -100.0, 100.0)
    out[:height] = value * jnp.exp2(PACK_TOP - power)
    out[height:] = jnp.broadcast_to(power, (PACK_ROWS, value.shape[1]))


def unpack(block):
    height = block.shape[0] - PACK_ROWS
    return block[:height] * jnp.exp2(block[height : height + 1, :1] - PACK_TOP)


def cross(block, step):
    return send(block.astype(jnp.float16), "mdl", step).astype(jnp.float32)


def dot(left, right, contract=((1,), (0,))):
    return lax.dot_general(left, right, (contract, ((), ())), preferred_element_type=jnp.float32)


def dispatch_body(owners, local, room, extra, *refs):
    sources, refs = refs[:3], refs[3:]
    outs, refs = refs[:owners], refs[owners:]
    states, task, batch, sems = refs
    rows, width = states.shape
    copies = [
        pltpu.make_async_copy(source, target, sems.at[i])
        for i, (source, target) in enumerate(zip(sources, (states, task, batch)))
    ]
    for i in (1, 2, 0):
        copies[i].start()
    copies[1].wait()
    copies[2].wait()
    me = lax.axis_index("teach")
    task_list, batch_list = task[...], batch[...]
    group = up_to(owners * local, ROW_TILE)
    named = lax.broadcasted_iota(jnp.int32, (group, rows), 0) == task_list
    earlier = lax.broadcasted_iota(jnp.int32, (rows, rows), 0) < lax.broadcasted_iota(
        jnp.int32, (rows, rows), 1
    )
    named = named.astype(jnp.float32)
    before = dot(named.astype(jnp.bfloat16), earlier.astype(jnp.float32).astype(jnp.bfloat16))
    before = jnp.sum(before * named, axis=0, keepdims=True).astype(jnp.int32)
    owner = task_list // local if local > 1 else task_list
    step = owner ^ me if is_power(owners) else (owner - me + owners) % owners
    place = step * local + task_list % local if local > 1 else step
    slot = place * room + before
    index = lax.broadcasted_iota(jnp.int32, (owners * local * room, rows), 0)
    chosen = (index == slot).astype(jnp.float32)
    head = (index % (local * room) == 0).astype(jnp.float32)
    member = (lax.broadcasted_iota(jnp.int32, (extra, rows), 0) == batch_list).astype(jnp.float32)
    tags = dot(
        (chosen + 2.0 * head).astype(jnp.bfloat16), member.astype(jnp.bfloat16), ((1,), (1,))
    ).astype(jnp.bfloat16)
    copies[0].wait()
    moved = dot(chosen.astype(jnp.bfloat16), states[...]).astype(jnp.bfloat16)
    for k, out in enumerate(outs):
        span = slice(k * local * room, (k + 1) * local * room)
        out[:, :width] = moved[span]
        out[:, width:] = tags[span]


def weights_body(*refs):
    sources, outs, sems = refs[1:5], refs[5:9], refs[9]
    copies = [
        pltpu.make_async_copy(source, target, sems.at[i])
        for i, (source, target) in enumerate(zip(sources, outs))
    ]
    for copy in copies:
        copy.start()
    for copy in copies:
        copy.wait()


def silu_of(pre):
    return (pre / (1.0 + jnp.exp(-pre))).astype(jnp.bfloat16)


def student(rows, student_up):
    pre = dot(rows, student_up[...])
    sig = 1.0 / (1.0 + jnp.exp(-pre))
    return silu_of(pre), sig * (1.0 + pre * (1.0 - sig))


def forward_body(local, room, first, *refs):
    count = len(refs) - 9 - (not first)
    blocks, refs = refs[:count], refs[count:]
    if not first:
        earlier, refs = refs[0], refs[1:]
    teach_in, teach_out, student_up, student_down = refs[:4]
    tags_out, counts_out, error_out, packed, rows_out = refs[4:]
    width = rows_out.shape[1]
    full = [block[...] for block in blocks]
    counts = None if first else earlier[...]
    for block in full:
        mine = jnp.floor(block[:1, width:].astype(jnp.float32) * 0.5)
        counts = mine if counts is None else counts + mine
    counts_out[...] = counts
    for l in range(local):
        span = slice(l * count * room, (l + 1) * count * room)
        for k, block in enumerate(full):
            start = (l * count + k) * room
            rows_out[start : start + room] = block[l * room : (l + 1) * room, :width]
            tag = block[l * room : (l + 1) * room, width:].astype(jnp.float32)
            if l == 0:
                head = lax.broadcasted_iota(jnp.int32, tag.shape, 0) == 0
                tag = jnp.where(head, tag - 2.0 * jnp.floor(tag * 0.5), tag)
            tags_out[start : start + room] = tag
        rows = rows_out[span]
        hidden = dot(rows, teach_in[l])
        hidden = (hidden / (1.0 + jnp.exp(-hidden))).astype(jnp.bfloat16)
        act = silu_of(dot(rows, student_up[...]))
        error_out[span] = dot(act, student_down[...], ((1,), (1,))) - dot(hidden, teach_out[l])
    pack(error_out[...], packed)


def chosen_columns(columns, owners, studs):
    height = columns // (owners * studs)
    shape = (owners * height, columns)
    row = lax.broadcasted_iota(jnp.int32, shape, 0)
    column = lax.broadcasted_iota(jnp.int32, shape, 1)
    owner = partner_to(owners, lax.axis_index("teach"), row // height)
    wanted = (owner * studs + lax.axis_index("stud")) * height + row % height
    return (column == wanted).astype(jnp.float32).astype(jnp.bfloat16)


def turn(value, owners, studs):
    chosen = chosen_columns(value.shape[1], owners, studs)
    return dot(chosen, value, ((1,), (1,))).astype(jnp.bfloat16)


def ahead_body(owners, studs, *refs):
    parts, student_up, (turned, act, slope) = refs[:-5], refs[-5], refs[-3:]
    rows = jnp.concatenate([part[...] for part in parts])
    turned[...] = turn(rows, owners, studs)
    act[...], slope[...] = student(rows, student_up)


def pair_body(*refs):
    for i in range(2):
        own, arrived = refs[2 * i : 2 * i + 2]
        total, packed = refs[2 * i + 4 : 2 * i + 6]
        value = own[...] + unpack(arrived)
        total[...] = value
        pack(value, packed)


def scale_body(*refs):
    second, first, tags, counts, scaled = refs[:2], refs[2:4], refs[4:6], refs[6:-1], refs[-1]
    all_counts = counts[0][...]
    for piece in counts[1:]:
        all_counts = all_counts + piece[...]
    inverse = jnp.where(all_counts > 0, 2.0 / all_counts, 0.0)
    start = 0
    for (own, arrived), tag in zip((first, second), tags):
        weight = jnp.sum(tag[...] * inverse, axis=1, keepdims=True)
        span = slice(start, start + own.shape[0])
        scaled[span] = ((own[...] + unpack(arrived)) * weight).astype(scaled.dtype)
        start += own.shape[0]


def backward_body(owners, studs, earlier, scaled, turned, act, slope, student_down, *refs):
    error = scaled[...]
    down = dot(turn(error, owners, studs), act[...])
    pre_grad = (dot(error, student_down[...]) * slope[...]).astype(jnp.bfloat16)
    up = dot(turned[...], pre_grad)
    if earlier:
        up, down = up + refs[0][...], down + refs[1][...]
    outs = refs[2 * earlier :]
    if len(outs) == 2:
        outs[0][...], outs[1][...] = up, down
        return
    high, low = up.shape[0] // owners, down.shape[0] // owners
    for k, out in enumerate(outs):
        block = [up[k * high : (k + 1) * high], down[k * low : (k + 1) * low]]
        out[...] = jnp.concatenate(block).astype(out.dtype)


def closing_body(*refs):
    pieces, (grad_up, grad_down, up, down, sems) = refs[:-5], refs[-5:]
    total = pieces[0][...]
    for piece in pieces[1:]:
        total = total + piece[...].astype(jnp.float32)
    cut = up.shape[0]
    up[...] = total[:cut]
    first = pltpu.make_async_copy(up, grad_up, sems.at[0])
    first.start()
    down[...] = total[cut:]
    second = pltpu.make_async_copy(down, grad_down, sems.at[1])
    second.start()
    first.wait()
    second.wait()


def kernel(body, outs, operands, flops, scratch=(), params=SMALL, places=None, to=VMEM):
    return pl.pallas_call(
        body,
        out_shape=outs,
        in_specs=places or [VMEM] * len(operands),
        out_specs=[to] * len(outs),
        scratch_shapes=list(scratch),
        cost_estimate=pl.CostEstimate(flops=flops, bytes_accessed=0, transcendentals=0),
        compiler_params=params,
    )(*operands)


def on_device(states, task_ids, student_batch, teach_in, teach_out, student_up, student_down):
    row_count, width = states.shape
    owners, studs, parts = lax.axis_size("teach"), lax.axis_size("stud"), lax.axis_size("mdl")
    local, _, hidden = teach_in.shape
    actions = teach_out.shape[2]
    units = student_up.shape[1]
    teachers, batches = owners * local, owners * studs
    room = up_to(3 * row_count // (2 * teachers), ROW_TILE)
    extra = up_to(batches, LANES)
    slots = teachers * room
    f32, bf16 = jnp.float32, jnp.bfloat16

    def shape(rows, columns, dtype):
        return jax.ShapeDtypeStruct((rows, columns), dtype)

    height = slots // 2
    half, packed = shape(height, actions, f32), shape(height + PACK_ROWS, actions, f32)
    state = [shape(slots, units, bf16), shape(slots, units, f32)]
    tokens = [ids.reshape(1, row_count) for ids in (task_ids, student_batch)]
    blocks = kernel(
        functools.partial(dispatch_body, owners, local, room, extra),
        [pltpu.VMEM((local * room, width + extra), bf16)] * owners,
        (states, *tokens),
        2 * slots * row_count * width,
        [pltpu.VMEM(a.shape, a.dtype) for a in (states, *tokens)] + [pltpu.SemaphoreType.DMA((3,))],
        LARGE,
        [HBM] * 3,
    )
    arrived = {k: send(blocks[k], "teach", k) for k in range(owners - 1, 0, -1)}
    weights = (teach_in, teach_out, student_up, student_down)
    weights = kernel(
        weights_body,
        [pltpu.VMEM(w.shape, w.dtype) for w in weights],
        (blocks[0], *[pltpu.with_memory_space_constraint(w, pltpu.HBM) for w in weights]),
        0,
        [pltpu.SemaphoreType.DMA((4,))],
        SMALL,
        [VMEM] + [HBM] * 4,
    )
    def forward(blocks, *earlier):
        rows = len(blocks) * local * room
        return kernel(
            functools.partial(forward_body, local, room, not earlier),
            [shape(rows, extra, f32), shape(1, extra, f32), half, packed, shape(rows, width, bf16)],
            (*blocks, *earlier, *weights),
            0,
        )

    steps = [1 << i for i in range(parts.bit_length() - 1)]
    blocks = [blocks[0]] + list(arrived.values())
    near, far = blocks[: owners // 2], blocks[owners // 2 :]
    second_tags, counts, second, second_out, second_rows = forward(near)
    second_in = cross(second_out, steps[-1])
    first_tags, counts, first, first_out, first_rows = forward(far, counts)
    first_in = cross(first_out, steps[0])
    rows, tags = (first_rows, second_rows), (first_tags, second_tags)
    all_counts, mates = [counts], []
    for k in range(1, studs):
        all_counts.append(send(counts, "stud", k))
        mates.append([send(part, "stud", k) for part in rows])
    first_in, second_in, all_counts, mates = lax.optimization_barrier(
        (first_in, second_in, all_counts, mates)
    )
    for there, back in zip(steps[1:], steps[-2::-1]):
        first, first_out, second, second_out = kernel(
            pair_body, [half, packed] * 2, (first, first_in, second, second_in), 0
        )
        first_in, second_in = cross(first_out, there), cross(second_out, back)
    ahead = functools.partial(ahead_body, owners, studs)
    turned = shape(width // studs, slots, bf16)
    ours, *known = [
        kernel(ahead, [turned] + state, (*group, weights[2], second), 0) for group in (rows, *mates)
    ]
    sums = (second, second_in, first, first_in)
    sums, all_counts, known, ours = lax.optimization_barrier((sums, all_counts, known, ours))
    (scaled,) = kernel(scale_body, [shape(slots, actions, bf16)], (*sums, *tags, *all_counts), 0)
    work = 6 * slots * width * units
    grads = [shape(width // studs, units, f32), shape(actions // studs, units, f32)]
    heights = [g.shape[0] // owners for g in grads]
    blocks = [shape(sum(heights), units, f32)] + [shape(sum(heights), units, bf16)] * (owners - 1)
    errors = [scaled] + [send(scaled, "stud", k) for k in range(1, studs)]
    states = [ours] + known
    sums = []
    for k, (error, state) in enumerate(zip(errors, states)):
        sums = kernel(
            functools.partial(backward_body, owners, studs, k > 0),
            blocks if k == studs - 1 else grads,
            (error, *state, weights[3], *sums),
            work,
        )
    pieces = [sums[0]] + [send(sums[k], "teach", k) for k in range(owners - 1, 0, -1)]
    outs = [shape(h, units, f32) for h in heights]
    return kernel(
        closing_body,
        outs,
        pieces,
        0,
        [pltpu.VMEM(o.shape, f32) for o in outs] + [pltpu.SemaphoreType.DMA((2,))],
        to=HBM,
    )


def solution(mesh):
    in_specs = (
        P(("teach", "stud"), None),
        P(("teach", "stud"), None),
        P(("teach", "stud"), None),
        P("teach", None, "mdl"),
        P("teach", "mdl", None),
        P(None, "mdl"),
        P(None, "mdl"),
    )
    out_specs = (P(("teach", "stud"), "mdl"), P(("teach", "stud"), "mdl"))
    return jax.shard_map(
        on_device, mesh=mesh, in_specs=in_specs, out_specs=out_specs, check_vma=False
    )
```

```python
import functools

import jax
import jax.numpy as jnp
from jax import lax
from jax.experimental import pallas as pl
from jax.experimental.pallas import tpu as pltpu
from jax.sharding import PartitionSpec as P

LANES = 128
ROW_TILE = 16
PACK_ROWS = 8
PACK_TOP = 14.0
TINY = 1e-37
VMEM = pl.BlockSpec(memory_space=pltpu.VMEM)
HBM = pl.BlockSpec(memory_space=pltpu.HBM)
SMALL = pltpu.CompilerParams(vmem_limit_bytes=16 * 1024 * 1024)
LARGE = pltpu.CompilerParams(vmem_limit_bytes=56 * 1024 * 1024)


def up_to(value, step):
    return -(-value // step) * step


def is_power(size):
    return size & (size - 1) == 0


def partner_to(size, me, step):
    return me ^ step if is_power(size) else (me + step) % size


def partner_from(size, me, step):
    return me ^ step if is_power(size) else (me + size - step) % size


def send(block, axis, step):
    size = lax.axis_size(axis)
    return lax.ppermute(block, axis, [(i, partner_to(size, i, step)) for i in range(size)])


def pack(value, out):
    height = value.shape[0]
    largest = jnp.max(jnp.max(jnp.abs(value), axis=0, keepdims=True), axis=1, keepdims=True)
    power = jnp.clip(jnp.ceil(jnp.log2(jnp.maximum(largest, TINY))), -100.0, 100.0)
    out[:height] = value * jnp.exp2(PACK_TOP - power)
    out[height:] = jnp.broadcast_to(power, (PACK_ROWS, value.shape[1]))


def unpack(block):
    height = block.shape[0] - PACK_ROWS
    return block[:height] * jnp.exp2(block[height : height + 1, :1] - PACK_TOP)


def cross(block, step):
    return send(block.astype(jnp.float16), "mdl", step).astype(jnp.float32)


def dot(left, right, contract=((1,), (0,))):
    return lax.dot_general(left, right, (contract, ((), ())), preferred_element_type=jnp.float32)


def dispatch_body(owners, local, room, extra, *refs):
    sources, refs = refs[:3], refs[3:]
    outs, refs = refs[:owners], refs[owners:]
    states, task, batch, sems = refs
    rows, width = states.shape
    copies = [
        pltpu.make_async_copy(source, target, sems.at[i])
        for i, (source, target) in enumerate(zip(sources, (states, task, batch)))
    ]
    for i in (1, 2, 0):
        copies[i].start()
    copies[1].wait()
    copies[2].wait()
    me = lax.axis_index("teach")
    task_list, batch_list = task[...], batch[...]
    group = up_to(owners * local, ROW_TILE)
    named = lax.broadcasted_iota(jnp.int32, (group, rows), 0) == task_list
    earlier = lax.broadcasted_iota(jnp.int32, (rows, rows), 0) < lax.broadcasted_iota(
        jnp.int32, (rows, rows), 1
    )
    named = named.astype(jnp.float32)
    before = dot(named.astype(jnp.bfloat16), earlier.astype(jnp.float32).astype(jnp.bfloat16))
    before = jnp.sum(before * named, axis=0, keepdims=True).astype(jnp.int32)
    owner = task_list // local if local > 1 else task_list
    step = owner ^ me if is_power(owners) else (owner - me + owners) % owners
    place = step * local + task_list % local if local > 1 else step
    slot = place * room + before
    index = lax.broadcasted_iota(jnp.int32, (owners * local * room, rows), 0)
    chosen = (index == slot).astype(jnp.float32)
    head = (index % (local * room) == 0).astype(jnp.float32)
    member = (lax.broadcasted_iota(jnp.int32, (extra, rows), 0) == batch_list).astype(jnp.float32)
    tags = dot(
        (chosen + 2.0 * head).astype(jnp.bfloat16), member.astype(jnp.bfloat16), ((1,), (1,))
    ).astype(jnp.bfloat16)
    copies[0].wait()
    moved = dot(chosen.astype(jnp.bfloat16), states[...]).astype(jnp.bfloat16)
    for k, out in enumerate(outs):
        span = slice(k * local * room, (k + 1) * local * room)
        out[:, :width] = moved[span]
        out[:, width:] = tags[span]


def weights_body(*refs):
    sources, outs, sems = refs[1:5], refs[5:9], refs[9]
    copies = [
        pltpu.make_async_copy(source, target, sems.at[i])
        for i, (source, target) in enumerate(zip(sources, outs))
    ]
    for copy in copies:
        copy.start()
    for copy in copies:
        copy.wait()


def silu_of(pre):
    return (pre / (1.0 + jnp.exp(-pre))).astype(jnp.bfloat16)


def student(rows, student_up):
    pre = dot(rows, student_up[...])
    sig = 1.0 / (1.0 + jnp.exp(-pre))
    return silu_of(pre), sig * (1.0 + pre * (1.0 - sig))


def forward_body(local, room, first, *refs):
    count = len(refs) - 9 - (not first)
    blocks, refs = refs[:count], refs[count:]
    if not first:
        earlier, refs = refs[0], refs[1:]
    teach_in, teach_out, student_up, student_down = refs[:4]
    tags_out, counts_out, error_out, packed, rows_out = refs[4:]
    width = rows_out.shape[1]
    full = [block[...] for block in blocks]
    counts = None if first else earlier[...]
    for block in full:
        mine = jnp.floor(block[:1, width:].astype(jnp.float32) * 0.5)
        counts = mine if counts is None else counts + mine
    counts_out[...] = counts
    for l in range(local):
        span = slice(l * count * room, (l + 1) * count * room)
        for k, block in enumerate(full):
            start = (l * count + k) * room
            rows_out[start : start + room] = block[l * room : (l + 1) * room, :width]
            tag = block[l * room : (l + 1) * room, width:].astype(jnp.float32)
            if l == 0:
                head = lax.broadcasted_iota(jnp.int32, tag.shape, 0) == 0
                tag = jnp.where(head, tag - 2.0 * jnp.floor(tag * 0.5), tag)
            tags_out[start : start + room] = tag
        rows = rows_out[span]
        hidden = dot(rows, teach_in[l])
        hidden = (hidden / (1.0 + jnp.exp(-hidden))).astype(jnp.bfloat16)
        act = silu_of(dot(rows, student_up[...]))
        error_out[span] = dot(act, student_down[...], ((1,), (1,))) - dot(hidden, teach_out[l])
    pack(error_out[...], packed)


def chosen_columns(columns, owners, studs):
    height = columns // (owners * studs)
    shape = (owners * height, columns)
    row = lax.broadcasted_iota(jnp.int32, shape, 0)
    column = lax.broadcasted_iota(jnp.int32, shape, 1)
    owner = partner_to(owners, lax.axis_index("teach"), row // height)
    wanted = (owner * studs + lax.axis_index("stud")) * height + row % height
    return (column == wanted).astype(jnp.float32).astype(jnp.bfloat16)


def turn(value, chosen):
    return dot(chosen, value, ((1,), (1,))).astype(jnp.bfloat16)


def ahead_body(owners, studs, count, *refs):
    parts, student_up, outs = refs[:count], refs[count], refs[count + 2 :]
    chosen = chosen_columns(parts[0].shape[1], owners, studs)
    for i, part in enumerate(parts):
        turned, act, slope = outs[3 * i : 3 * i + 3]
        rows = part[...]
        turned[...] = turn(rows, chosen)
        act[...], slope[...] = student(rows, student_up)
    if len(outs) > 3 * count:
        outs[-1][...] = chosen_columns(outs[-1].shape[1], owners, studs)


def pair_body(own, arrived, *refs):
    total, packed = refs[-2:]
    value = own[...] + unpack(arrived)
    total[...] = value
    pack(value, packed)


def scale_body(own, arrived, tags, *refs):
    counts, scaled = refs[:-1], refs[-1]
    all_counts = counts[0][...]
    for piece in counts[1:]:
        all_counts = all_counts + piece[...]
    inverse = jnp.where(all_counts > 0, 2.0 / all_counts, 0.0)
    weight = jnp.sum(tags[...] * inverse, axis=1, keepdims=True)
    scaled[...] = ((own[...] + unpack(arrived)) * weight).astype(scaled.dtype)


def backward_body(owners, earlier, scaled, turned, act, slope, chosen, student_down, *refs):
    error = scaled[...]
    down = dot(turn(error, chosen[...]), act[...])
    pre_grad = (dot(error, student_down[...]) * slope[...]).astype(jnp.bfloat16)
    up = dot(turned[...], pre_grad)
    if earlier:
        up, down = up + refs[0][...], down + refs[1][...]
    outs = refs[2 * earlier :]
    if len(outs) == 2:
        outs[0][...], outs[1][...] = up, down
        return
    high, low = up.shape[0] // owners, down.shape[0] // owners
    for k, out in enumerate(outs):
        block = [up[k * high : (k + 1) * high], down[k * low : (k + 1) * low]]
        out[...] = jnp.concatenate(block).astype(out.dtype)


def closing_body(*refs):
    pieces, (grad_up, grad_down, up, down, sems) = refs[:-5], refs[-5:]
    total = pieces[0][...]
    for piece in pieces[1:]:
        total = total + piece[...].astype(jnp.float32)
    cut = up.shape[0]
    up[...] = total[:cut]
    first = pltpu.make_async_copy(up, grad_up, sems.at[0])
    first.start()
    down[...] = total[cut:]
    second = pltpu.make_async_copy(down, grad_down, sems.at[1])
    second.start()
    first.wait()
    second.wait()


def kernel(body, outs, operands, flops, scratch=(), params=SMALL, places=None, to=VMEM):
    return pl.pallas_call(
        body,
        out_shape=outs,
        in_specs=places or [VMEM] * len(operands),
        out_specs=[to] * len(outs),
        scratch_shapes=list(scratch),
        cost_estimate=pl.CostEstimate(flops=flops, bytes_accessed=0, transcendentals=0),
        compiler_params=params,
    )(*operands)


def on_device(states, task_ids, student_batch, teach_in, teach_out, student_up, student_down):
    row_count, width = states.shape
    owners, studs, parts = lax.axis_size("teach"), lax.axis_size("stud"), lax.axis_size("mdl")
    local, _, hidden = teach_in.shape
    actions = teach_out.shape[2]
    units = student_up.shape[1]
    teachers, batches = owners * local, owners * studs
    room = up_to(3 * row_count // (2 * teachers), ROW_TILE)
    extra = up_to(batches, LANES)
    slots = teachers * room
    f32, bf16 = jnp.float32, jnp.bfloat16

    def shape(rows, columns, dtype):
        return jax.ShapeDtypeStruct((rows, columns), dtype)

    height = slots // 2
    half, packed = shape(height, actions, f32), shape(height + PACK_ROWS, actions, f32)
    state = [shape(width // studs, height, bf16), shape(height, units, bf16), shape(height, units, f32)]
    tokens = [ids.reshape(1, row_count) for ids in (task_ids, student_batch)]
    blocks = kernel(
        functools.partial(dispatch_body, owners, local, room, extra),
        [pltpu.VMEM((local * room, width + extra), bf16)] * owners,
        (states, *tokens),
        2 * slots * row_count * width,
        [pltpu.VMEM(a.shape, a.dtype) for a in (states, *tokens)] + [pltpu.SemaphoreType.DMA((3,))],
        LARGE,
        [HBM] * 3,
    )
    arrived = {k: send(blocks[k], "teach", k) for k in range(owners - 1, 0, -1)}
    weights = (teach_in, teach_out, student_up, student_down)
    weights = kernel(
        weights_body,
        [pltpu.VMEM(w.shape, w.dtype) for w in weights],
        (blocks[0], *[pltpu.with_memory_space_constraint(w, pltpu.HBM) for w in weights]),
        0,
        [pltpu.SemaphoreType.DMA((4,))],
        SMALL,
        [VMEM] + [HBM] * 4,
    )
    def forward(blocks, *earlier):
        rows = len(blocks) * local * room
        return kernel(
            functools.partial(forward_body, local, room, not earlier),
            [shape(rows, extra, f32), shape(1, extra, f32), half, packed, shape(rows, width, bf16)],
            (*blocks, *earlier, *weights),
            0,
        )

    steps = [1 << i for i in range(parts.bit_length() - 1)]
    blocks = [blocks[0]] + list(arrived.values())
    near, far = blocks[: owners // 2], blocks[owners // 2 :]
    second_tags, counts, second, second_out, second_rows = forward(near)
    second_in = cross(second_out, steps[-1])
    first_tags, counts, first, first_out, first_rows = forward(far, counts)
    first_in = cross(first_out, steps[0])
    rows, tags = (first_rows, second_rows), (first_tags, second_tags)
    all_counts, mates = [counts], []
    for k in range(1, studs):
        all_counts.append(send(counts, "stud", k))
        mates.append([send(part, "stud", k) for part in rows])
    second_in, all_counts, mates = lax.optimization_barrier((second_in, all_counts, mates))
    for there, back in zip(steps[1:], steps[-2::-1]):
        second, second_out = kernel(pair_body, [half, packed], (second, second_in), 0)
        second_in = cross(second_out, back)
        first, first_out = kernel(pair_body, [half, packed], (first, first_in, second), 0)
        first_in = cross(first_out, there)
    ahead = functools.partial(ahead_body, owners, studs, 2)
    *ours, chosen = kernel(
        ahead, state * 2 + [shape(actions // studs, actions, bf16)], (*rows, weights[2], first), 0
    )
    known = [ours] + [kernel(ahead, state * 2, (*theirs, weights[2], first), 0) for theirs in mates]
    grads = [shape(width // studs, units, f32), shape(actions // studs, units, f32)]
    heights = [g.shape[0] // owners for g in grads]
    blocks = [shape(sum(heights), units, f32)] + [shape(sum(heights), units, bf16)] * (owners - 1)

    def scale(part, own, arrived):
        (scaled,) = kernel(
            scale_body, [shape(height, actions, bf16)], (own, arrived, tags[part], *all_counts), 0
        )
        return [scaled] + [send(scaled, "stud", k) for k in range(1, studs)]

    def backward(k, part, sums, last=False):
        return kernel(
            functools.partial(backward_body, owners, len(sums) > 0),
            blocks if last else grads,
            (errors[part][k], *known[k][3 * part : 3 * part + 3], chosen, weights[3], *sums),
            0,
        )

    errors = {1: scale(1, second, second_in)}
    sums = backward(0, 1, [])
    first_in, known, chosen, sums = lax.optimization_barrier((first_in, known, chosen, sums))
    errors[0] = scale(0, first, first_in)
    order = [(0, 0)] + [(k, part) for k in range(1, studs) for part in (1, 0)]
    for k, part in order:
        sums = backward(k, part, sums, (k, part) == order[-1])
    pieces = [sums[0]] + [send(sums[k], "teach", k) for k in range(owners - 1, 0, -1)]
    outs = [shape(h, units, f32) for h in heights]
    return kernel(
        closing_body,
        outs,
        pieces,
        0,
        [pltpu.VMEM(o.shape, f32) for o in outs] + [pltpu.SemaphoreType.DMA((2,))],
        to=HBM,
    )


def solution(mesh):
    in_specs = (
        P(("teach", "stud"), None),
        P(("teach", "stud"), None),
        P(("teach", "stud"), None),
        P("teach", None, "mdl"),
        P("teach", "mdl", None),
        P(None, "mdl"),
        P(None, "mdl"),
    )
    out_specs = (P(("teach", "stud"), "mdl"), P(("teach", "stud"), "mdl"))
    return jax.shard_map(
        on_device, mesh=mesh, in_specs=in_specs, out_specs=out_specs, check_vma=False
    )
```

```python
import functools

import jax
import jax.numpy as jnp
from jax import lax
from jax.experimental import pallas as pl
from jax.experimental.pallas import tpu as pltpu
from jax.sharding import PartitionSpec as P

LANES = 128
ROW_TILE = 16
PACK_ROWS = 8
PACK_TOP = 14.0
TINY = 1e-37
VMEM = pl.BlockSpec(memory_space=pltpu.VMEM)
HBM = pl.BlockSpec(memory_space=pltpu.HBM)
SMALL = pltpu.CompilerParams(vmem_limit_bytes=16 * 1024 * 1024)
LARGE = pltpu.CompilerParams(vmem_limit_bytes=56 * 1024 * 1024)


def up_to(value, step):
    return -(-value // step) * step


def is_power(size):
    return size & (size - 1) == 0


def partner_to(size, me, step):
    return me ^ step if is_power(size) else (me + step) % size


def partner_from(size, me, step):
    return me ^ step if is_power(size) else (me + size - step) % size


def send(block, axis, step):
    size = lax.axis_size(axis)
    return lax.ppermute(block, axis, [(i, partner_to(size, i, step)) for i in range(size)])


def pack(value, out):
    height = value.shape[0]
    largest = jnp.max(jnp.max(jnp.abs(value), axis=0, keepdims=True), axis=1, keepdims=True)
    power = jnp.clip(jnp.ceil(jnp.log2(jnp.maximum(largest, TINY))), -100.0, 100.0)
    out[:height] = value * jnp.exp2(PACK_TOP - power)
    out[height:] = jnp.broadcast_to(power, (PACK_ROWS, value.shape[1]))


def unpack(block):
    height = block.shape[0] - PACK_ROWS
    return block[:height] * jnp.exp2(block[height : height + 1, :1] - PACK_TOP)


def cross(block, step):
    return send(block.astype(jnp.float16), "mdl", step).astype(jnp.float32)


def dot(left, right, contract=((1,), (0,))):
    return lax.dot_general(left, right, (contract, ((), ())), preferred_element_type=jnp.float32)


def dispatch_body(owners, local, room, extra, *refs):
    sources, refs = refs[:7], refs[7:]
    outs, refs = refs[:owners], refs[owners:]
    weights, (states, task, batch, sems) = refs[:4], refs[4:]
    rows, width = states.shape
    copies = [
        pltpu.make_async_copy(source, target, sems.at[i])
        for i, (source, target) in enumerate(zip(sources, (states, task, batch, *weights)))
    ]
    for i in (1, 2, 0, 3, 4, 5, 6):
        copies[i].start()
    copies[1].wait()
    copies[2].wait()
    me = lax.axis_index("teach")
    task_list, batch_list = task[...], batch[...]
    group = up_to(owners * local, ROW_TILE)
    named = lax.broadcasted_iota(jnp.int32, (group, rows), 0) == task_list
    earlier = lax.broadcasted_iota(jnp.int32, (rows, rows), 0) < lax.broadcasted_iota(
        jnp.int32, (rows, rows), 1
    )
    named = named.astype(jnp.float32)
    before = dot(named.astype(jnp.bfloat16), earlier.astype(jnp.float32).astype(jnp.bfloat16))
    before = jnp.sum(before * named, axis=0, keepdims=True).astype(jnp.int32)
    owner = task_list // local if local > 1 else task_list
    step = owner ^ me if is_power(owners) else (owner - me + owners) % owners
    place = step * local + task_list % local if local > 1 else step
    slot = place * room + before
    index = lax.broadcasted_iota(jnp.int32, (owners * local * room, rows), 0)
    chosen = (index == slot).astype(jnp.float32)
    head = (index % (local * room) == 0).astype(jnp.float32)
    member = (lax.broadcasted_iota(jnp.int32, (extra, rows), 0) == batch_list).astype(jnp.float32)
    tags = dot(
        (chosen + 2.0 * head).astype(jnp.bfloat16), member.astype(jnp.bfloat16), ((1,), (1,))
    ).astype(jnp.bfloat16)
    copies[0].wait()
    moved = dot(chosen.astype(jnp.bfloat16), states[...]).astype(jnp.bfloat16)
    for k, out in enumerate(outs):
        span = slice(k * local * room, (k + 1) * local * room)
        out[:, :width] = moved[span]
        out[:, width:] = tags[span]
    for copy in copies[3:]:
        copy.wait()


def silu_of(pre):
    return (pre / (1.0 + jnp.exp(-pre))).astype(jnp.bfloat16)


def student(rows, student_up):
    pre = dot(rows, student_up[...])
    sig = 1.0 / (1.0 + jnp.exp(-pre))
    return silu_of(pre), sig * (1.0 + pre * (1.0 - sig))


def forward_body(local, room, first, *refs):
    count = len(refs) - 9 - (not first)
    blocks, refs = refs[:count], refs[count:]
    if not first:
        earlier, refs = refs[0], refs[1:]
    teach_in, teach_out, student_up, student_down = refs[:4]
    tags_out, counts_out, error_out, packed, rows_out = refs[4:]
    width = rows_out.shape[1]
    full = [block[...] for block in blocks]
    counts = None if first else earlier[...]
    for block in full:
        mine = jnp.floor(block[:1, width:].astype(jnp.float32) * 0.5)
        counts = mine if counts is None else counts + mine
    counts_out[...] = counts
    for l in range(local):
        span = slice(l * count * room, (l + 1) * count * room)
        for k, block in enumerate(full):
            start = (l * count + k) * room
            rows_out[start : start + room] = block[l * room : (l + 1) * room, :width]
            tag = block[l * room : (l + 1) * room, width:].astype(jnp.float32)
            if l == 0:
                head = lax.broadcasted_iota(jnp.int32, tag.shape, 0) == 0
                tag = jnp.where(head, tag - 2.0 * jnp.floor(tag * 0.5), tag)
            tags_out[start : start + room] = tag
        rows = rows_out[span]
        hidden = dot(rows, teach_in[l])
        hidden = (hidden / (1.0 + jnp.exp(-hidden))).astype(jnp.bfloat16)
        act = silu_of(dot(rows, student_up[...]))
        error_out[span] = dot(act, student_down[...], ((1,), (1,))) - dot(hidden, teach_out[l])
    pack(error_out[...], packed)


def chosen_columns(columns, owners, studs):
    height = columns // (owners * studs)
    shape = (owners * height, columns)
    row = lax.broadcasted_iota(jnp.int32, shape, 0)
    column = lax.broadcasted_iota(jnp.int32, shape, 1)
    owner = partner_to(owners, lax.axis_index("teach"), row // height)
    wanted = (owner * studs + lax.axis_index("stud")) * height + row % height
    return (column == wanted).astype(jnp.float32).astype(jnp.bfloat16)


def turn(value, chosen):
    return dot(chosen, value, ((1,), (1,))).astype(jnp.bfloat16)


def ahead_body(owners, studs, count, *refs):
    parts, student_up, outs = refs[:count], refs[count], refs[count + 2 :]
    chosen = chosen_columns(parts[0].shape[1], owners, studs)
    for i, part in enumerate(parts):
        turned, act, slope = outs[3 * i : 3 * i + 3]
        rows = part[...]
        turned[...] = turn(rows, chosen)
        act[...], slope[...] = student(rows, student_up)
    if len(outs) > 3 * count:
        outs[-1][...] = chosen_columns(outs[-1].shape[1], owners, studs)


def pair_body(*refs):
    for i in range(2):
        own, arrived = refs[2 * i : 2 * i + 2]
        total, packed = refs[2 * i + 4 : 2 * i + 6]
        value = own[...] + unpack(arrived)
        total[...] = value
        pack(value, packed)


def scale_body(own, arrived, tags, *refs):
    counts, scaled = refs[:-1], refs[-1]
    all_counts = counts[0][...]
    for piece in counts[1:]:
        all_counts = all_counts + piece[...]
    inverse = jnp.where(all_counts > 0, 2.0 / all_counts, 0.0)
    weight = jnp.sum(tags[...] * inverse, axis=1, keepdims=True)
    scaled[...] = ((own[...] + unpack(arrived)) * weight).astype(scaled.dtype)


def backward_body(owners, earlier, scaled, turned, act, slope, chosen, student_down, *refs):
    error = scaled[...]
    down = dot(turn(error, chosen[...]), act[...])
    pre_grad = (dot(error, student_down[...]) * slope[...]).astype(jnp.bfloat16)
    up = dot(turned[...], pre_grad)
    if earlier:
        up, down = up + refs[0][...], down + refs[1][...]
    outs = refs[2 * earlier :]
    if len(outs) == 2:
        outs[0][...], outs[1][...] = up, down
        return
    high, low = up.shape[0] // owners, down.shape[0] // owners
    for k, out in enumerate(outs):
        block = [up[k * high : (k + 1) * high], down[k * low : (k + 1) * low]]
        out[...] = jnp.concatenate(block).astype(out.dtype)


def closing_body(*refs):
    pieces, (grad_up, grad_down, up, down, sems) = refs[:-5], refs[-5:]
    total = pieces[0][...]
    for piece in pieces[1:]:
        total = total + piece[...].astype(jnp.float32)
    cut = up.shape[0]
    up[...] = total[:cut]
    first = pltpu.make_async_copy(up, grad_up, sems.at[0])
    first.start()
    down[...] = total[cut:]
    second = pltpu.make_async_copy(down, grad_down, sems.at[1])
    second.start()
    first.wait()
    second.wait()


def kernel(body, outs, operands, flops, scratch=(), params=SMALL, places=None, to=VMEM):
    return pl.pallas_call(
        body,
        out_shape=outs,
        in_specs=places or [VMEM] * len(operands),
        out_specs=[to] * len(outs),
        scratch_shapes=list(scratch),
        cost_estimate=pl.CostEstimate(flops=flops, bytes_accessed=0, transcendentals=0),
        compiler_params=params,
    )(*operands)


def on_device(states, task_ids, student_batch, teach_in, teach_out, student_up, student_down):
    row_count, width = states.shape
    owners, studs, parts = lax.axis_size("teach"), lax.axis_size("stud"), lax.axis_size("mdl")
    local, _, hidden = teach_in.shape
    actions = teach_out.shape[2]
    units = student_up.shape[1]
    teachers, batches = owners * local, owners * studs
    room = up_to(3 * row_count // (2 * teachers), ROW_TILE)
    extra = up_to(batches, LANES)
    slots = teachers * room
    f32, bf16 = jnp.float32, jnp.bfloat16

    def shape(rows, columns, dtype):
        return jax.ShapeDtypeStruct((rows, columns), dtype)

    height = slots // 2
    half, packed = shape(height, actions, f32), shape(height + PACK_ROWS, actions, f32)
    state = [shape(width // studs, height, bf16), shape(height, units, bf16), shape(height, units, f32)]
    tokens = [ids.reshape(1, row_count) for ids in (task_ids, student_batch)]
    weights = (teach_in, teach_out, student_up, student_down)
    results = kernel(
        functools.partial(dispatch_body, owners, local, room, extra),
        [pltpu.VMEM((local * room, width + extra), bf16)] * owners
        + [pltpu.VMEM(w.shape, w.dtype) for w in weights],
        (states, *tokens, *weights),
        0,
        [pltpu.VMEM(a.shape, a.dtype) for a in (states, *tokens)] + [pltpu.SemaphoreType.DMA((7,))],
        LARGE,
        [HBM] * 7,
    )
    blocks, weights = results[:owners], results[owners:]
    middle = owners // 2
    near = [blocks[0]] + [send(blocks[k], "teach", k) for k in range(1, middle)]
    far = [send(blocks[k], "teach", k) for k in range(owners - 1, middle - 1, -1)]

    def forward(blocks, *earlier):
        rows = len(blocks) * local * room
        return kernel(
            functools.partial(forward_body, local, room, not earlier),
            [shape(rows, extra, f32), shape(1, extra, f32), half, packed, shape(rows, width, bf16)],
            (*blocks, *earlier, *weights),
            0,
        )

    steps = [1 << i for i in range(parts.bit_length() - 1)]
    second_tags, counts, second, second_out, second_rows = forward(near)
    second_in = cross(second_out, steps[-1])
    first_tags, counts, first, first_out, first_rows = forward(far, counts)
    first_in = cross(first_out, steps[0])
    rows, tags = (first_rows, second_rows), (first_tags, second_tags)
    all_counts, mates = [counts], []
    for k in range(1, studs):
        all_counts.append(send(counts, "stud", k))
        mates.append([send(part, "stud", k) for part in rows])
    first_in, second_in, all_counts, mates = lax.optimization_barrier(
        (first_in, second_in, all_counts, mates)
    )
    for there, back in zip(steps[1:], steps[-2::-1]):
        first, first_out, second, second_out = kernel(
            pair_body, [half, packed] * 2, (first, first_in, second, second_in), 0
        )
        first_in, second_in = cross(first_out, there), cross(second_out, back)
    ahead = functools.partial(ahead_body, owners, studs, 2)
    *ours, chosen = kernel(
        ahead, state * 2 + [shape(actions // studs, actions, bf16)], (*rows, weights[2], first), 0
    )
    known = [ours] + [kernel(ahead, state * 2, (*theirs, weights[2], first), 0) for theirs in mates]
    grads = [shape(width // studs, units, f32), shape(actions // studs, units, f32)]
    heights = [g.shape[0] // owners for g in grads]
    blocks = [shape(sum(heights), units, f32)] + [shape(sum(heights), units, bf16)] * (owners - 1)

    def scale(part, own, arrived):
        (scaled,) = kernel(
            scale_body, [shape(height, actions, bf16)], (own, arrived, tags[part], *all_counts), 0
        )
        return [scaled] + [send(scaled, "stud", k) for k in range(1, studs)]

    def backward(k, part, sums, last=False):
        return kernel(
            functools.partial(backward_body, owners, len(sums) > 0),
            blocks if last else grads,
            (errors[part][k], *known[k][3 * part : 3 * part + 3], chosen, weights[3], *sums),
            0,
        )

    errors = {0: scale(0, first, first_in)}
    sums = backward(0, 0, [])
    second_in, known, chosen, sums = lax.optimization_barrier((second_in, known, chosen, sums))
    errors[1] = scale(1, second, second_in)
    order = [(0, 1)] + [(k, part) for k in range(1, studs) for part in (0, 1)]
    for k, part in order:
        sums = backward(k, part, sums, (k, part) == order[-1])
    pieces = [sums[0]] + [send(sums[k], "teach", k) for k in range(owners - 1, 0, -1)]
    outs = [shape(h, units, f32) for h in heights]
    return kernel(
        closing_body,
        outs,
        pieces,
        0,
        [pltpu.VMEM(o.shape, f32) for o in outs] + [pltpu.SemaphoreType.DMA((2,))],
        to=HBM,
    )


def solution(mesh):
    in_specs = (
        P(("teach", "stud"), None),
        P(("teach", "stud"), None),
        P(("teach", "stud"), None),
        P("teach", None, "mdl"),
        P("teach", "mdl", None),
        P(None, "mdl"),
        P(None, "mdl"),
    )
    out_specs = (P(("teach", "stud"), "mdl"), P(("teach", "stud"), "mdl"))
    return jax.shard_map(
        on_device, mesh=mesh, in_specs=in_specs, out_specs=out_specs, check_vma=False
    )
```

```python
import functools

import jax
import jax.numpy as jnp
from jax import lax
from jax.experimental import pallas as pl
from jax.experimental.pallas import tpu as pltpu
from jax.sharding import PartitionSpec as P

LANES = 128
ROW_TILE = 16
PACK_ROWS = 8
PACK_TOP = 14.0
TINY = 1e-37
VMEM = pl.BlockSpec(memory_space=pltpu.VMEM)
HBM = pl.BlockSpec(memory_space=pltpu.HBM)
SMALL = pltpu.CompilerParams(vmem_limit_bytes=16 * 1024 * 1024)
LARGE = pltpu.CompilerParams(vmem_limit_bytes=56 * 1024 * 1024)


def up_to(value, step):
    return -(-value // step) * step


def is_power(size):
    return size & (size - 1) == 0


def partner_to(size, me, step):
    return me ^ step if is_power(size) else (me + step) % size


def partner_from(size, me, step):
    return me ^ step if is_power(size) else (me + size - step) % size


def send(block, axis, step):
    size = lax.axis_size(axis)
    return lax.ppermute(block, axis, [(i, partner_to(size, i, step)) for i in range(size)])


def pack(value, out):
    height = value.shape[0]
    largest = jnp.max(jnp.max(jnp.abs(value), axis=0, keepdims=True), axis=1, keepdims=True)
    power = jnp.clip(jnp.ceil(jnp.log2(jnp.maximum(largest, TINY))), -100.0, 100.0)
    out[:height] = value * jnp.exp2(PACK_TOP - power)
    out[height:] = jnp.broadcast_to(power, (PACK_ROWS, value.shape[1]))


def unpack(block):
    height = block.shape[0] - PACK_ROWS
    return block[:height] * jnp.exp2(block[height : height + 1, :1] - PACK_TOP)


def cross(block, step):
    return send(block.astype(jnp.float16), "mdl", step).astype(jnp.float32)


def dot(left, right, contract=((1,), (0,))):
    return lax.dot_general(left, right, (contract, ((), ())), preferred_element_type=jnp.float32)


def dispatch_body(owners, local, room, extra, *refs):
    sources, refs = refs[:7], refs[7:]
    outs, refs = refs[:owners], refs[owners:]
    weights, (states, task, batch, sems) = refs[:4], refs[4:]
    rows, width = states.shape
    copies = [
        pltpu.make_async_copy(source, target, sems.at[i])
        for i, (source, target) in enumerate(zip(sources, (states, task, batch, *weights)))
    ]
    for i in (1, 2, 0, 3, 4, 5, 6):
        copies[i].start()
    copies[1].wait()
    copies[2].wait()
    me = lax.axis_index("teach")
    task_list, batch_list = task[...], batch[...]
    group = up_to(owners * local, ROW_TILE)
    named = lax.broadcasted_iota(jnp.int32, (group, rows), 0) == task_list
    earlier = lax.broadcasted_iota(jnp.int32, (rows, rows), 0) < lax.broadcasted_iota(
        jnp.int32, (rows, rows), 1
    )
    named = named.astype(jnp.float32)
    before = dot(named.astype(jnp.bfloat16), earlier.astype(jnp.float32).astype(jnp.bfloat16))
    before = jnp.sum(before * named, axis=0, keepdims=True).astype(jnp.int32)
    owner = task_list // local if local > 1 else task_list
    step = owner ^ me if is_power(owners) else (owner - me + owners) % owners
    place = step * local + task_list % local if local > 1 else step
    slot = place * room + before
    index = lax.broadcasted_iota(jnp.int32, (owners * local * room, rows), 0)
    chosen = (index == slot).astype(jnp.float32)
    head = (index % (local * room) == 0).astype(jnp.float32)
    member = (lax.broadcasted_iota(jnp.int32, (extra, rows), 0) == batch_list).astype(jnp.float32)
    tags = dot(
        (chosen + 2.0 * head).astype(jnp.bfloat16), member.astype(jnp.bfloat16), ((1,), (1,))
    ).astype(jnp.bfloat16)
    copies[0].wait()
    moved = dot(chosen.astype(jnp.bfloat16), states[...]).astype(jnp.bfloat16)
    for k, out in enumerate(outs):
        span = slice(k * local * room, (k + 1) * local * room)
        out[:, :width] = moved[span]
        out[:, width:] = tags[span]
    for copy in copies[3:]:
        copy.wait()


def silu_of(pre):
    return (pre / (1.0 + jnp.exp(-pre))).astype(jnp.bfloat16)


def student(rows, student_up):
    pre = dot(rows, student_up[...])
    sig = 1.0 / (1.0 + jnp.exp(-pre))
    return silu_of(pre), sig * (1.0 + pre * (1.0 - sig))


def forward_body(local, room, first, *refs):
    count = len(refs) - 9 - (not first)
    blocks, refs = refs[:count], refs[count:]
    if not first:
        earlier, refs = refs[0], refs[1:]
    teach_in, teach_out, student_up, student_down = refs[:4]
    tags_out, counts_out, error_out, packed, rows_out = refs[4:]
    width = rows_out.shape[1]
    full = [block[...] for block in blocks]
    counts = None if first else earlier[...]
    for block in full:
        mine = jnp.floor(block[:1, width:].astype(jnp.float32) * 0.5)
        counts = mine if counts is None else counts + mine
    counts_out[...] = counts
    for l in range(local):
        span = slice(l * count * room, (l + 1) * count * room)
        for k, block in enumerate(full):
            start = (l * count + k) * room
            rows_out[start : start + room] = block[l * room : (l + 1) * room, :width]
            tag = block[l * room : (l + 1) * room, width:].astype(jnp.float32)
            if l == 0:
                head = lax.broadcasted_iota(jnp.int32, tag.shape, 0) == 0
                tag = jnp.where(head, tag - 2.0 * jnp.floor(tag * 0.5), tag)
            tags_out[start : start + room] = tag
        rows = rows_out[span]
        hidden = dot(rows, teach_in[l])
        hidden = (hidden / (1.0 + jnp.exp(-hidden))).astype(jnp.bfloat16)
        act = silu_of(dot(rows, student_up[...]))
        error_out[span] = dot(act, student_down[...], ((1,), (1,))) - dot(hidden, teach_out[l])
    pack(error_out[...], packed)


def chosen_columns(columns, owners, studs):
    height = columns // (owners * studs)
    shape = (owners * height, columns)
    row = lax.broadcasted_iota(jnp.int32, shape, 0)
    column = lax.broadcasted_iota(jnp.int32, shape, 1)
    owner = partner_to(owners, lax.axis_index("teach"), row // height)
    wanted = (owner * studs + lax.axis_index("stud")) * height + row % height
    return (column == wanted).astype(jnp.float32).astype(jnp.bfloat16)


def turn(value, chosen):
    return dot(chosen, value, ((1,), (1,))).astype(jnp.bfloat16)


def ahead_body(owners, studs, *refs):
    parts, student_up, outs = refs[:2], refs[2], refs[4:]
    turned, act, slope = outs[:3]
    rows = jnp.concatenate([part[...] for part in parts])
    turned[...] = turn(rows, chosen_columns(rows.shape[1], owners, studs))
    act[...], slope[...] = student(rows, student_up)
    if len(outs) > 3:
        outs[3][...] = chosen_columns(outs[3].shape[1], owners, studs)


def pair_body(*refs):
    for i in range(2):
        own, arrived = refs[2 * i : 2 * i + 2]
        total, packed = refs[2 * i + 4 : 2 * i + 6]
        value = own[...] + unpack(arrived)
        total[...] = value
        pack(value, packed)


def scale_body(*refs):
    halves, tags, counts, scaled = (refs[2:4], refs[:2]), refs[4:6], refs[6:-1], refs[-1]
    all_counts = counts[0][...]
    for piece in counts[1:]:
        all_counts = all_counts + piece[...]
    inverse = jnp.where(all_counts > 0, 2.0 / all_counts, 0.0)
    start = 0
    for (own, arrived), tag in zip(halves, tags):
        weight = jnp.sum(tag[...] * inverse, axis=1, keepdims=True)
        span = slice(start, start + own.shape[0])
        scaled[span] = ((own[...] + unpack(arrived)) * weight).astype(scaled.dtype)
        start += own.shape[0]


def backward_body(owners, earlier, scaled, turned, act, slope, chosen, student_down, *refs):
    error = scaled[...]
    down = dot(turn(error, chosen[...]), act[...])
    pre_grad = (dot(error, student_down[...]) * slope[...]).astype(jnp.bfloat16)
    up = dot(turned[...], pre_grad)
    if earlier:
        up, down = up + refs[0][...], down + refs[1][...]
    outs = refs[2 * earlier :]
    if len(outs) == 2:
        outs[0][...], outs[1][...] = up, down
        return
    high, low = up.shape[0] // owners, down.shape[0] // owners
    for k, out in enumerate(outs):
        block = [up[k * high : (k + 1) * high], down[k * low : (k + 1) * low]]
        out[...] = jnp.concatenate(block).astype(out.dtype)


def closing_body(*refs):
    pieces, (grad_up, grad_down, up, down, sems) = refs[:-5], refs[-5:]
    total = pieces[0][...]
    for piece in pieces[1:]:
        total = total + piece[...].astype(jnp.float32)
    cut = up.shape[0]
    up[...] = total[:cut]
    first = pltpu.make_async_copy(up, grad_up, sems.at[0])
    first.start()
    down[...] = total[cut:]
    second = pltpu.make_async_copy(down, grad_down, sems.at[1])
    second.start()
    first.wait()
    second.wait()


def kernel(body, outs, operands, flops, scratch=(), params=SMALL, places=None, to=VMEM):
    return pl.pallas_call(
        body,
        out_shape=outs,
        in_specs=places or [VMEM] * len(operands),
        out_specs=[to] * len(outs),
        scratch_shapes=list(scratch),
        cost_estimate=pl.CostEstimate(flops=flops, bytes_accessed=0, transcendentals=0),
        compiler_params=params,
    )(*operands)


def on_device(states, task_ids, student_batch, teach_in, teach_out, student_up, student_down):
    row_count, width = states.shape
    owners, studs, parts = lax.axis_size("teach"), lax.axis_size("stud"), lax.axis_size("mdl")
    local, _, hidden = teach_in.shape
    actions = teach_out.shape[2]
    units = student_up.shape[1]
    teachers, batches = owners * local, owners * studs
    room = up_to(3 * row_count // (2 * teachers), ROW_TILE)
    extra = up_to(batches, LANES)
    slots = teachers * room
    f32, bf16 = jnp.float32, jnp.bfloat16

    def shape(rows, columns, dtype):
        return jax.ShapeDtypeStruct((rows, columns), dtype)

    height = slots // 2
    half, packed = shape(height, actions, f32), shape(height + PACK_ROWS, actions, f32)
    state = [shape(width // studs, slots, bf16), shape(slots, units, bf16), shape(slots, units, f32)]
    tokens = [ids.reshape(1, row_count) for ids in (task_ids, student_batch)]
    weights = (teach_in, teach_out, student_up, student_down)
    results = kernel(
        functools.partial(dispatch_body, owners, local, room, extra),
        [pltpu.VMEM((local * room, width + extra), bf16)] * owners
        + [pltpu.VMEM(w.shape, w.dtype) for w in weights],
        (states, *tokens, *weights),
        0,
        [pltpu.VMEM(a.shape, a.dtype) for a in (states, *tokens)] + [pltpu.SemaphoreType.DMA((7,))],
        LARGE,
        [HBM] * 7,
    )
    blocks, weights = results[:owners], results[owners:]
    middle = owners // 2
    near = [blocks[0]] + [send(blocks[k], "teach", k) for k in range(1, middle)]
    far = [send(blocks[k], "teach", k) for k in range(owners - 1, middle - 1, -1)]

    def forward(blocks, *earlier):
        rows = len(blocks) * local * room
        return kernel(
            functools.partial(forward_body, local, room, not earlier),
            [shape(rows, extra, f32), shape(1, extra, f32), half, packed, shape(rows, width, bf16)],
            (*blocks, *earlier, *weights),
            0,
        )

    steps = [1 << i for i in range(parts.bit_length() - 1)]
    second_tags, counts, second, second_out, second_rows = forward(near)
    second_in = cross(second_out, steps[-1])
    first_tags, counts, first, first_out, first_rows = forward(far, counts)
    first_in = cross(first_out, steps[0])
    rows, tags = (first_rows, second_rows), (first_tags, second_tags)
    all_counts, mates = [counts], []
    for k in range(1, studs):
        all_counts.append(send(counts, "stud", k))
        mates.append([send(part, "stud", k) for part in rows])
    first_in, second_in, all_counts, mates = lax.optimization_barrier(
        (first_in, second_in, all_counts, mates)
    )
    for there, back in zip(steps[1:], steps[-2::-1]):
        first, first_out, second, second_out = kernel(
            pair_body, [half, packed] * 2, (first, first_in, second, second_in), 0
        )
        first_in, second_in = cross(first_out, there), cross(second_out, back)
    ahead = functools.partial(ahead_body, owners, studs)
    *ours, chosen = kernel(
        ahead, state + [shape(actions // studs, actions, bf16)], (*rows, weights[2], first), 0
    )
    known = [ours] + [kernel(ahead, state, (*theirs, weights[2], first), 0) for theirs in mates]
    sums = (second, second_in, first, first_in)
    sums, all_counts, known, chosen = lax.optimization_barrier((sums, all_counts, known, chosen))
    (scaled,) = kernel(scale_body, [shape(slots, actions, bf16)], (*sums, *tags, *all_counts), 0)
    errors = [scaled] + [send(scaled, "stud", k) for k in range(1, studs)]
    grads = [shape(width // studs, units, f32), shape(actions // studs, units, f32)]
    heights = [g.shape[0] // owners for g in grads]
    blocks = [shape(sum(heights), units, f32)] + [shape(sum(heights), units, bf16)] * (owners - 1)
    sums = []
    for k, (error, group) in enumerate(zip(errors, known)):
        sums = kernel(
            functools.partial(backward_body, owners, k > 0),
            blocks if k == studs - 1 else grads,
            (error, *group, chosen, weights[3], *sums),
            0,
        )
    pieces = [sums[0]] + [send(sums[k], "teach", k) for k in range(owners - 1, 0, -1)]
    outs = [shape(h, units, f32) for h in heights]
    return kernel(
        closing_body,
        outs,
        pieces,
        0,
        [pltpu.VMEM(o.shape, f32) for o in outs] + [pltpu.SemaphoreType.DMA((2,))],
        to=HBM,
    )


def solution(mesh):
    in_specs = (
        P(("teach", "stud"), None),
        P(("teach", "stud"), None),
        P(("teach", "stud"), None),
        P("teach", None, "mdl"),
        P("teach", "mdl", None),
        P(None, "mdl"),
        P(None, "mdl"),
    )
    out_specs = (P(("teach", "stud"), "mdl"), P(("teach", "stud"), "mdl"))
    return jax.shard_map(
        on_device, mesh=mesh, in_specs=in_specs, out_specs=out_specs, check_vma=False
    )
```

```python
import functools

import jax
import jax.numpy as jnp
from jax import lax
from jax.experimental import pallas as pl
from jax.experimental.pallas import tpu as pltpu
from jax.sharding import PartitionSpec as P

LANES = 128
ROW_TILE = 16
POWER_ROWS = 8
PACK_TOP = 14.0
TINY = 1e-37
VMEM = pl.BlockSpec(memory_space=pltpu.VMEM)
HBM = pl.BlockSpec(memory_space=pltpu.HBM)
SMALL = pltpu.CompilerParams(vmem_limit_bytes=16 * 1024 * 1024)
LARGE = pltpu.CompilerParams(vmem_limit_bytes=56 * 1024 * 1024)


def up_to(value, step):
    return -(-value // step) * step


def is_power(size):
    return size & (size - 1) == 0


def partner_to(size, me, step):
    return me ^ step if is_power(size) else (me + step) % size


def partner_from(size, me, step):
    return me ^ step if is_power(size) else (me + size - step) % size


def send(block, axis, step):
    size = lax.axis_size(axis)
    return lax.ppermute(block, axis, [(i, partner_to(size, i, step)) for i in range(size)])


def pack(value, out, power_out=None):
    height = value.shape[0]
    largest = jnp.max(jnp.max(jnp.abs(value), axis=0, keepdims=True), axis=1, keepdims=True)
    power = jnp.clip(jnp.ceil(jnp.log2(jnp.maximum(largest, TINY))), -100.0, 100.0)
    out[:height] = value * jnp.exp2(PACK_TOP - power)
    place = out.at[height:] if power_out is None else power_out
    place[...] = jnp.broadcast_to(power, place.shape)


def unpack(block, power=None):
    height = block.shape[0] - (POWER_ROWS if power is None else 0)
    power = block[height : height + 1, :1] if power is None else power[:1, :1]
    return block[:height] * jnp.exp2(power - PACK_TOP)


def cross(block, step, power=None):
    arrived = [send(block.astype(jnp.float16), "mdl", step).astype(jnp.float32)]
    return arrived if power is None else arrived + [send(power, "mdl", step)]


def dot(left, right, contract=((1,), (0,))):
    return lax.dot_general(left, right, (contract, ((), ())), preferred_element_type=jnp.float32)


def dispatch_body(owners, local, room, extra, *refs):
    sources, refs = refs[:7], refs[7:]
    outs, refs = refs[:owners], refs[owners:]
    weights, (states, task, batch, sems) = refs[:4], refs[4:]
    rows, width = states.shape
    copies = [
        pltpu.make_async_copy(source, target, sems.at[i])
        for i, (source, target) in enumerate(zip(sources, (states, task, batch, *weights)))
    ]
    for i in (1, 2, 0, 3, 4, 5, 6):
        copies[i].start()
    copies[1].wait()
    copies[2].wait()
    me = lax.axis_index("teach")
    task_list, batch_list = task[...], batch[...]
    group = up_to(owners * local, ROW_TILE)
    named = lax.broadcasted_iota(jnp.int32, (group, rows), 0) == task_list
    earlier = lax.broadcasted_iota(jnp.int32, (rows, rows), 0) < lax.broadcasted_iota(
        jnp.int32, (rows, rows), 1
    )
    named = named.astype(jnp.float32)
    before = dot(named.astype(jnp.bfloat16), earlier.astype(jnp.float32).astype(jnp.bfloat16))
    before = jnp.sum(before * named, axis=0, keepdims=True).astype(jnp.int32)
    owner = task_list // local if local > 1 else task_list
    step = owner ^ me if is_power(owners) else (owner - me + owners) % owners
    place = step * local + task_list % local if local > 1 else step
    slot = place * room + before
    index = lax.broadcasted_iota(jnp.int32, (owners * local * room, rows), 0)
    chosen = (index == slot).astype(jnp.float32)
    head = (index % (local * room) == 0).astype(jnp.float32)
    member = (lax.broadcasted_iota(jnp.int32, (extra, rows), 0) == batch_list).astype(jnp.float32)
    tags = dot(
        (chosen + 2.0 * head).astype(jnp.bfloat16), member.astype(jnp.bfloat16), ((1,), (1,))
    ).astype(jnp.bfloat16)
    copies[0].wait()
    moved = dot(chosen.astype(jnp.bfloat16), states[...]).astype(jnp.bfloat16)
    for k, out in enumerate(outs):
        span = slice(k * local * room, (k + 1) * local * room)
        out[:, :width] = moved[span]
        out[:, width:] = tags[span]
    for copy in copies[3:]:
        copy.wait()


def silu_of(pre):
    return (pre / (1.0 + jnp.exp(-pre))).astype(jnp.bfloat16)


def student(rows, student_up):
    pre = dot(rows, student_up[...])
    sig = 1.0 / (1.0 + jnp.exp(-pre))
    return silu_of(pre), sig * (1.0 + pre * (1.0 - sig))


def forward_body(local, room, first, *refs):
    count = len(refs) - (9 if first else 11)
    blocks, refs = refs[:count], refs[count:]
    if not first:
        earlier, refs = refs[0], refs[1:]
    teach_in, teach_out, student_up, student_down = refs[:4]
    tags_out, counts_out, rows_out, error_out, *message = refs[4:]
    width = rows_out.shape[1]
    full = [block[...] for block in blocks]
    counts = None if first else earlier[...]
    for block in full:
        mine = jnp.floor(block[:1, width:].astype(jnp.float32) * 0.5)
        counts = mine if counts is None else counts + mine
    counts_out[...] = counts
    for l in range(local):
        span = slice(l * count * room, (l + 1) * count * room)
        for k, block in enumerate(full):
            start = (l * count + k) * room
            rows_out[start : start + room] = block[l * room : (l + 1) * room, :width]
            tag = block[l * room : (l + 1) * room, width:].astype(jnp.float32)
            if l == 0:
                head = lax.broadcasted_iota(jnp.int32, tag.shape, 0) == 0
                tag = jnp.where(head, tag - 2.0 * jnp.floor(tag * 0.5), tag)
            tags_out[start : start + room] = tag
        rows = rows_out[span]
        hidden = dot(rows, teach_in[l])
        hidden = (hidden / (1.0 + jnp.exp(-hidden))).astype(jnp.bfloat16)
        act = silu_of(dot(rows, student_up[...]))
        error_out[span] = dot(act, student_down[...], ((1,), (1,))) - dot(hidden, teach_out[l])
    pack(error_out[...], *message)


def chosen_columns(columns, owners, studs):
    height = columns // (owners * studs)
    shape = (owners * height, columns)
    row = lax.broadcasted_iota(jnp.int32, shape, 0)
    column = lax.broadcasted_iota(jnp.int32, shape, 1)
    owner = partner_to(owners, lax.axis_index("teach"), row // height)
    wanted = (owner * studs + lax.axis_index("stud")) * height + row % height
    return (column == wanted).astype(jnp.float32).astype(jnp.bfloat16)


def turn(value, chosen):
    return dot(chosen, value, ((1,), (1,))).astype(jnp.bfloat16)


def ahead_body(owners, studs, *refs):
    parts, student_up, outs = refs[:2], refs[2], refs[4:]
    turned, act, slope = outs[:3]
    rows = jnp.concatenate([part[...] for part in parts])
    turned[...] = turn(rows, chosen_columns(rows.shape[1], owners, studs))
    act[...], slope[...] = student(rows, student_up)
    if len(outs) > 3:
        outs[3][...] = chosen_columns(outs[3].shape[1], owners, studs)


def pair_body(sizes, *refs):
    refs, outs = refs[:-6], refs[-6:]
    for i, size in enumerate(sizes):
        own, arrived, refs = refs[0], refs[1 : 1 + size], refs[1 + size :]
        total, packed, power = outs[3 * i : 3 * i + 3]
        value = own[...] + unpack(*arrived)
        total[...] = value
        pack(value, packed, power)


def scale_body(*refs):
    halves, tags, counts, scaled = (refs[:3], refs[3:6]), refs[6:8], refs[8:-1], refs[-1]
    all_counts = counts[0][...]
    for piece in counts[1:]:
        all_counts = all_counts + piece[...]
    inverse = jnp.where(all_counts > 0, 2.0 / all_counts, 0.0)
    start = 0
    for (own, arrived, power), tag in zip(halves, tags):
        weight = jnp.sum(tag[...] * inverse, axis=1, keepdims=True)
        span = slice(start, start + own.shape[0])
        scaled[span] = ((own[...] + unpack(arrived, power)) * weight).astype(scaled.dtype)
        start += own.shape[0]


def backward_body(owners, earlier, scaled, turned, act, slope, chosen, student_down, *refs):
    error = scaled[...]
    down = dot(turn(error, chosen[...]), act[...])
    pre_grad = (dot(error, student_down[...]) * slope[...]).astype(jnp.bfloat16)
    up = dot(turned[...], pre_grad)
    if earlier:
        up, down = up + refs[0][...], down + refs[1][...]
    outs = refs[2 * earlier :]
    if len(outs) == 2:
        outs[0][...], outs[1][...] = up, down
        return
    high, low = up.shape[0] // owners, down.shape[0] // owners
    for k, out in enumerate(outs):
        block = [up[k * high : (k + 1) * high], down[k * low : (k + 1) * low]]
        out[...] = jnp.concatenate(block).astype(out.dtype)


def closing_body(*refs):
    pieces, (grad_up, grad_down, up, down, sems) = refs[:-5], refs[-5:]
    total = pieces[0][...]
    for piece in pieces[1:]:
        total = total + piece[...].astype(jnp.float32)
    cut = up.shape[0]
    up[...] = total[:cut]
    first = pltpu.make_async_copy(up, grad_up, sems.at[0])
    first.start()
    down[...] = total[cut:]
    second = pltpu.make_async_copy(down, grad_down, sems.at[1])
    second.start()
    first.wait()
    second.wait()


def kernel(body, outs, operands, flops, scratch=(), params=SMALL, places=None, to=VMEM):
    return pl.pallas_call(
        body,
        out_shape=outs,
        in_specs=places or [VMEM] * len(operands),
        out_specs=[to] * len(outs),
        scratch_shapes=list(scratch),
        cost_estimate=pl.CostEstimate(flops=flops, bytes_accessed=0, transcendentals=0),
        compiler_params=params,
    )(*operands)


def on_device(states, task_ids, student_batch, teach_in, teach_out, student_up, student_down):
    row_count, width = states.shape
    owners, studs, parts = lax.axis_size("teach"), lax.axis_size("stud"), lax.axis_size("mdl")
    local, _, hidden = teach_in.shape
    actions = teach_out.shape[2]
    units = student_up.shape[1]
    teachers, batches = owners * local, owners * studs
    room = up_to(3 * row_count // (2 * teachers), ROW_TILE)
    extra = up_to(batches, LANES)
    slots = teachers * room
    f32, bf16 = jnp.float32, jnp.bfloat16

    def shape(rows, columns, dtype):
        return jax.ShapeDtypeStruct((rows, columns), dtype)

    height = slots // 2
    half, power = shape(height, actions, f32), shape(POWER_ROWS, LANES, f32)
    packed = shape(height + POWER_ROWS, actions, f32)
    state = [shape(width // studs, slots, bf16), shape(slots, units, bf16), shape(slots, units, f32)]
    tokens = [ids.reshape(1, row_count) for ids in (task_ids, student_batch)]
    weights = (teach_in, teach_out, student_up, student_down)
    results = kernel(
        functools.partial(dispatch_body, owners, local, room, extra),
        [pltpu.VMEM((local * room, width + extra), bf16)] * owners
        + [pltpu.VMEM(w.shape, w.dtype) for w in weights],
        (states, *tokens, *weights),
        0,
        [pltpu.VMEM(a.shape, a.dtype) for a in (states, *tokens)] + [pltpu.SemaphoreType.DMA((7,))],
        LARGE,
        [HBM] * 7,
    )
    blocks, weights = results[:owners], results[owners:]
    middle = owners // 2
    near = [blocks[0]] + [send(blocks[k], "teach", k) for k in range(1, middle)]
    far = [send(blocks[k], "teach", k) for k in range(owners - 1, middle - 1, -1)]

    def forward(blocks, message, *earlier):
        rows = len(blocks) * local * room
        return kernel(
            functools.partial(forward_body, local, room, not earlier),
            [shape(rows, extra, f32), shape(1, extra, f32), shape(rows, width, bf16), half, *message],
            (*blocks, *earlier, *weights),
            0,
        )

    steps = [1 << i for i in range(parts.bit_length() - 1)]
    second_tags, counts, second_rows, second, second_out = forward(near, [packed])
    second_in = cross(second_out, steps[-1])
    first_tags, counts, first_rows, first, first_out, first_power = forward(
        far, [half, power], counts
    )
    first_in = cross(first_out, steps[0], first_power)
    rows, tags = (first_rows, second_rows), (first_tags, second_tags)
    all_counts, mates = [counts], []
    for k in range(1, studs):
        all_counts.append(send(counts, "stud", k))
        mates.append([send(part, "stud", k) for part in rows])
    first_in, second_in, mates = lax.optimization_barrier((first_in, second_in, mates))
    for there, back in zip(steps[1:], steps[-2::-1]):
        first, first_out, first_power, second, second_out, second_power = kernel(
            functools.partial(pair_body, (len(first_in), len(second_in))),
            [half, half, power] * 2,
            (first, *first_in, second, *second_in),
            0,
        )
        first_in = cross(first_out, there, first_power)
        second_in = cross(second_out, back, second_power)
    ahead = functools.partial(ahead_body, owners, studs)
    *ours, chosen = kernel(
        ahead, state + [shape(actions // studs, actions, bf16)], (*rows, weights[2], first), 0
    )
    known = [ours] + [kernel(ahead, state, (*theirs, weights[2], first), 0) for theirs in mates]
    sums = (first, *first_in, second, *second_in)
    sums, all_counts, known, chosen = lax.optimization_barrier((sums, all_counts, known, chosen))
    (scaled,) = kernel(scale_body, [shape(slots, actions, bf16)], (*sums, *tags, *all_counts), 0)
    errors = [scaled] + [send(scaled, "stud", k) for k in range(1, studs)]
    grads = [shape(width // studs, units, f32), shape(actions // studs, units, f32)]
    heights = [g.shape[0] // owners for g in grads]
    blocks = [shape(sum(heights), units, f32)] + [shape(sum(heights), units, bf16)] * (owners - 1)
    sums = []
    for k, (error, group) in enumerate(zip(errors, known)):
        sums = kernel(
            functools.partial(backward_body, owners, k > 0),
            blocks if k == studs - 1 else grads,
            (error, *group, chosen, weights[3], *sums),
            0,
        )
    pieces = [sums[0]] + [send(sums[k], "teach", k) for k in range(owners - 1, 0, -1)]
    outs = [shape(h, units, f32) for h in heights]
    return kernel(
        closing_body,
        outs,
        pieces,
        0,
        [pltpu.VMEM(o.shape, f32) for o in outs] + [pltpu.SemaphoreType.DMA((2,))],
        to=HBM,
    )


def solution(mesh):
    in_specs = (
        P(("teach", "stud"), None),
        P(("teach", "stud"), None),
        P(("teach", "stud"), None),
        P("teach", None, "mdl"),
        P("teach", "mdl", None),
        P(None, "mdl"),
        P(None, "mdl"),
    )
    out_specs = (P(("teach", "stud"), "mdl"), P(("teach", "stud"), "mdl"))
    return jax.shard_map(
        on_device, mesh=mesh, in_specs=in_specs, out_specs=out_specs, check_vma=False
    )
```

```python
import functools

import jax
import jax.numpy as jnp
from jax import lax
from jax.experimental import pallas as pl
from jax.experimental.pallas import tpu as pltpu
from jax.sharding import PartitionSpec as P

LANES = 128
ROW_TILE = 16
PACK_ROWS = 8
PACK_TOP = 14.0
TINY = 1e-37
VMEM = pl.BlockSpec(memory_space=pltpu.VMEM)
HBM = pl.BlockSpec(memory_space=pltpu.HBM)
SMALL = pltpu.CompilerParams(vmem_limit_bytes=16 * 1024 * 1024)
LARGE = pltpu.CompilerParams(vmem_limit_bytes=56 * 1024 * 1024)


def up_to(value, step):
    return -(-value // step) * step


def is_power(size):
    return size & (size - 1) == 0


def partner_to(size, me, step):
    return me ^ step if is_power(size) else (me + step) % size


def partner_from(size, me, step):
    return me ^ step if is_power(size) else (me + size - step) % size


def send(block, axis, step):
    size = lax.axis_size(axis)
    return lax.ppermute(block, axis, [(i, partner_to(size, i, step)) for i in range(size)])


def pack(value, out):
    height = value.shape[0]
    largest = jnp.max(jnp.max(jnp.abs(value), axis=0, keepdims=True), axis=1, keepdims=True)
    power = jnp.clip(jnp.ceil(jnp.log2(jnp.maximum(largest, TINY))), -100.0, 100.0)
    out[:height] = value * jnp.exp2(PACK_TOP - power)
    out[height:] = jnp.broadcast_to(power, (PACK_ROWS, value.shape[1]))


def unpack(block, height):
    return block[:height] * jnp.exp2(block[height : height + 1, :1] - PACK_TOP)


def cross(block, step):
    return send(block.astype(jnp.float16), "mdl", step).astype(jnp.float32)


def dot(left, right, contract=((1,), (0,))):
    return lax.dot_general(left, right, (contract, ((), ())), preferred_element_type=jnp.float32)


def dispatch_body(owners, local, room, extra, *refs):
    sources, refs = refs[:7], refs[7:]
    outs, refs = refs[:owners], refs[owners:]
    weights, (states, task, batch, sems) = refs[:4], refs[4:]
    rows, width = states.shape
    copies = [
        pltpu.make_async_copy(source, target, sems.at[i])
        for i, (source, target) in enumerate(zip(sources, (states, task, batch, *weights)))
    ]
    for i in (1, 2, 0, 3, 4, 5, 6):
        copies[i].start()
    copies[1].wait()
    copies[2].wait()
    me = lax.axis_index("teach")
    task_list, batch_list = task[...], batch[...]
    group = up_to(owners * local, ROW_TILE)
    named = lax.broadcasted_iota(jnp.int32, (group, rows), 0) == task_list
    earlier = lax.broadcasted_iota(jnp.int32, (rows, rows), 0) < lax.broadcasted_iota(
        jnp.int32, (rows, rows), 1
    )
    named = named.astype(jnp.float32)
    before = dot(named.astype(jnp.bfloat16), earlier.astype(jnp.float32).astype(jnp.bfloat16))
    before = jnp.sum(before * named, axis=0, keepdims=True).astype(jnp.int32)
    owner = task_list // local if local > 1 else task_list
    step = owner ^ me if is_power(owners) else (owner - me + owners) % owners
    place = step * local + task_list % local if local > 1 else step
    slot = place * room + before
    index = lax.broadcasted_iota(jnp.int32, (owners * local * room, rows), 0)
    chosen = (index == slot).astype(jnp.float32)
    head = (index % (local * room) == 0).astype(jnp.float32)
    member = (lax.broadcasted_iota(jnp.int32, (extra, rows), 0) == batch_list).astype(jnp.float32)
    tags = dot(
        (chosen + 2.0 * head).astype(jnp.bfloat16), member.astype(jnp.bfloat16), ((1,), (1,))
    ).astype(jnp.bfloat16)
    copies[0].wait()
    moved = dot(chosen.astype(jnp.bfloat16), states[...]).astype(jnp.bfloat16)
    for k, out in enumerate(outs):
        span = slice(k * local * room, (k + 1) * local * room)
        out[:, :width] = moved[span]
        out[:, width:] = tags[span]
    for copy in copies[3:]:
        copy.wait()


def silu_of(pre):
    return (pre / (1.0 + jnp.exp(-pre))).astype(jnp.bfloat16)


def student(rows, student_up):
    pre = dot(rows, student_up[...])
    sig = 1.0 / (1.0 + jnp.exp(-pre))
    return silu_of(pre), sig * (1.0 + pre * (1.0 - sig))


def forward_body(local, room, first, *refs):
    count = len(refs) - 9 - (not first)
    blocks, refs = refs[:count], refs[count:]
    if not first:
        earlier, refs = refs[0], refs[1:]
    teach_in, teach_out, student_up, student_down = refs[:4]
    tags_out, counts_out, error_out, packed, rows_out = refs[4:]
    width = rows_out.shape[1]
    full = [block[...] for block in blocks]
    counts = None if first else earlier[...]
    for block in full:
        mine = jnp.floor(block[:1, width:].astype(jnp.float32) * 0.5)
        counts = mine if counts is None else counts + mine
    counts_out[...] = counts
    for l in range(local):
        span = slice(l * count * room, (l + 1) * count * room)
        for k, block in enumerate(full):
            start = (l * count + k) * room
            rows_out[start : start + room] = block[l * room : (l + 1) * room, :width]
            tag = block[l * room : (l + 1) * room, width:].astype(jnp.float32)
            if l == 0:
                head = lax.broadcasted_iota(jnp.int32, tag.shape, 0) == 0
                tag = jnp.where(head, tag - 2.0 * jnp.floor(tag * 0.5), tag)
            tags_out[start : start + room] = tag
        rows = rows_out[span]
        hidden = dot(rows, teach_in[l])
        hidden = (hidden / (1.0 + jnp.exp(-hidden))).astype(jnp.bfloat16)
        act = silu_of(dot(rows, student_up[...]))
        error_out[span] = dot(act, student_down[...], ((1,), (1,))) - dot(hidden, teach_out[l])
    pack(error_out[...], packed)


def chosen_columns(columns, owners, studs):
    height = columns // (owners * studs)
    shape = (owners * height, columns)
    row = lax.broadcasted_iota(jnp.int32, shape, 0)
    column = lax.broadcasted_iota(jnp.int32, shape, 1)
    owner = partner_to(owners, lax.axis_index("teach"), row // height)
    wanted = (owner * studs + lax.axis_index("stud")) * height + row % height
    return (column == wanted).astype(jnp.float32).astype(jnp.bfloat16)


def turn(value, chosen):
    return dot(chosen, value, ((1,), (1,))).astype(jnp.bfloat16)


def ahead_body(owners, studs, *refs):
    parts, student_up, outs = refs[:2], refs[2], refs[4:]
    turned, act, slope = outs[:3]
    rows = jnp.concatenate([part[...] for part in parts])
    turned[...] = turn(rows, chosen_columns(rows.shape[1], owners, studs))
    act[...], slope[...] = student(rows, student_up)
    if len(outs) > 3:
        outs[3][...] = chosen_columns(outs[3].shape[1], owners, studs)


def pair_body(own, arrived, *refs):
    total, packed = refs[-2:]
    value = own[...] + unpack(arrived, own.shape[0])
    total[...] = value
    pack(value, packed)


def scale_body(*refs):
    halves, tags, counts, scaled = (refs[:2], refs[2:4]), refs[4:6], refs[6:-1], refs[-1]
    all_counts = counts[0][...]
    for piece in counts[1:]:
        all_counts = all_counts + piece[...]
    inverse = jnp.where(all_counts > 0, 2.0 / all_counts, 0.0)
    start = 0
    for (own, arrived), tag in zip(halves, tags):
        weight = jnp.sum(tag[...] * inverse, axis=1, keepdims=True)
        span = slice(start, start + own.shape[0])
        scaled[span] = ((own[...] + unpack(arrived, own.shape[0])) * weight).astype(scaled.dtype)
        start += own.shape[0]


def backward_body(owners, earlier, scaled, turned, act, slope, chosen, student_down, *refs):
    error = scaled[...]
    down = dot(turn(error, chosen[...]), act[...])
    pre_grad = (dot(error, student_down[...]) * slope[...]).astype(jnp.bfloat16)
    up = dot(turned[...], pre_grad)
    if earlier:
        up, down = up + refs[0][...], down + refs[1][...]
    outs = refs[2 * earlier :]
    if len(outs) == 2:
        outs[0][...], outs[1][...] = up, down
        return
    high, low = up.shape[0] // owners, down.shape[0] // owners
    for k, out in enumerate(outs):
        block = [up[k * high : (k + 1) * high], down[k * low : (k + 1) * low]]
        out[...] = jnp.concatenate(block).astype(out.dtype)


def closing_body(*refs):
    pieces, (grad_up, grad_down, up, down, sems) = refs[:-5], refs[-5:]
    total = pieces[0][...]
    for piece in pieces[1:]:
        total = total + piece[...].astype(jnp.float32)
    cut = up.shape[0]
    up[...] = total[:cut]
    first = pltpu.make_async_copy(up, grad_up, sems.at[0])
    first.start()
    down[...] = total[cut:]
    second = pltpu.make_async_copy(down, grad_down, sems.at[1])
    second.start()
    first.wait()
    second.wait()


def kernel(body, outs, operands, flops, scratch=(), params=SMALL, places=None, to=VMEM):
    return pl.pallas_call(
        body,
        out_shape=outs,
        in_specs=places or [VMEM] * len(operands),
        out_specs=[to] * len(outs),
        scratch_shapes=list(scratch),
        cost_estimate=pl.CostEstimate(flops=flops, bytes_accessed=0, transcendentals=0),
        compiler_params=params,
    )(*operands)


def on_device(states, task_ids, student_batch, teach_in, teach_out, student_up, student_down):
    row_count, width = states.shape
    owners, studs, parts = lax.axis_size("teach"), lax.axis_size("stud"), lax.axis_size("mdl")
    local, _, hidden = teach_in.shape
    actions = teach_out.shape[2]
    units = student_up.shape[1]
    teachers, batches = owners * local, owners * studs
    room = up_to(3 * row_count // (2 * teachers), ROW_TILE)
    extra = up_to(batches, LANES)
    slots = teachers * room
    f32, bf16 = jnp.float32, jnp.bfloat16

    def shape(rows, columns, dtype):
        return jax.ShapeDtypeStruct((rows, columns), dtype)

    height = slots // 2
    half, packed = shape(height, actions, f32), shape(height + PACK_ROWS, actions, f32)
    state = [shape(width // studs, slots, bf16), shape(slots, units, bf16), shape(slots, units, f32)]
    tokens = [ids.reshape(1, row_count) for ids in (task_ids, student_batch)]
    weights = (teach_in, teach_out, student_up, student_down)
    results = kernel(
        functools.partial(dispatch_body, owners, local, room, extra),
        [pltpu.VMEM((local * room, width + extra), bf16)] * owners
        + [pltpu.VMEM(w.shape, w.dtype) for w in weights],
        (states, *tokens, *weights),
        0,
        [pltpu.VMEM(a.shape, a.dtype) for a in (states, *tokens)] + [pltpu.SemaphoreType.DMA((7,))],
        LARGE,
        [HBM] * 7,
    )
    blocks, weights = results[:owners], results[owners:]
    middle = owners // 2
    near = [blocks[0]] + [send(blocks[k], "teach", k) for k in range(1, middle)]
    far = [send(blocks[k], "teach", k) for k in range(owners - 1, middle - 1, -1)]

    def forward(blocks, *earlier):
        rows = len(blocks) * local * room
        return kernel(
            functools.partial(forward_body, local, room, not earlier),
            [shape(rows, extra, f32), shape(1, extra, f32), half, packed, shape(rows, width, bf16)],
            (*blocks, *earlier, *weights),
            0,
        )

    steps = [1 << i for i in range(parts.bit_length() - 1)]
    second_tags, counts, second, second_out, second_rows = forward(near)
    second_in = cross(second_out, steps[0])
    first_tags, counts, first, first_out, first_rows = forward(far, counts)
    first_in = cross(first_out, steps[-1])
    rows, tags = (first_rows, second_rows), (first_tags, second_tags)
    all_counts, mates = [counts], []
    for k in range(1, studs):
        all_counts.append(send(counts, "stud", k))
        mates.append([send(part, "stud", k) for part in rows])
    second_in, all_counts = lax.optimization_barrier((second_in, all_counts))
    for there, back in zip(steps[1:], steps[-2::-1]):
        second, second_out = kernel(pair_body, [half, packed], (second, second_in), 0)
        second_in = cross(second_out, there)
        first, first_out = kernel(pair_body, [half, packed], (first, first_in, second), 0)
        first_in = cross(first_out, back)
    ahead = functools.partial(ahead_body, owners, studs)
    *ours, chosen = kernel(
        ahead, state + [shape(actions // studs, actions, bf16)], (*rows, weights[2], first), 0
    )
    known = [ours] + [kernel(ahead, state, (*theirs, weights[2], first), 0) for theirs in mates]
    sums = (first, first_in, second, second_in)
    sums, all_counts, known, chosen = lax.optimization_barrier((sums, all_counts, known, chosen))
    (scaled,) = kernel(scale_body, [shape(slots, actions, bf16)], (*sums, *tags, *all_counts), 0)
    errors = [scaled] + [send(scaled, "stud", k) for k in range(1, studs)]
    grads = [shape(width // studs, units, f32), shape(actions // studs, units, f32)]
    heights = [g.shape[0] // owners for g in grads]
    blocks = [shape(sum(heights), units, f32)] + [shape(sum(heights), units, bf16)] * (owners - 1)
    sums = []
    for k, (error, group) in enumerate(zip(errors, known)):
        sums = kernel(
            functools.partial(backward_body, owners, k > 0),
            blocks if k == studs - 1 else grads,
            (error, *group, chosen, weights[3], *sums),
            0,
        )
    pieces = [sums[0]] + [send(sums[k], "teach", k) for k in range(owners - 1, 0, -1)]
    outs = [shape(h, units, f32) for h in heights]
    return kernel(
        closing_body,
        outs,
        pieces,
        0,
        [pltpu.VMEM(o.shape, f32) for o in outs] + [pltpu.SemaphoreType.DMA((2,))],
        to=HBM,
    )


def solution(mesh):
    in_specs = (
        P(("teach", "stud"), None),
        P(("teach", "stud"), None),
        P(("teach", "stud"), None),
        P("teach", None, "mdl"),
        P("teach", "mdl", None),
        P(None, "mdl"),
        P(None, "mdl"),
    )
    out_specs = (P(("teach", "stud"), "mdl"), P(("teach", "stud"), "mdl"))
    return jax.shard_map(
        on_device, mesh=mesh, in_specs=in_specs, out_specs=out_specs, check_vma=False
    )
```

```python
import functools

import jax
import jax.numpy as jnp
from jax import lax
from jax.experimental import pallas as pl
from jax.experimental.pallas import tpu as pltpu
from jax.sharding import PartitionSpec as P

LANES = 128
ROW_TILE = 16
PACK_ROWS = 8
PACK_TOP = 14.0
TINY = 1e-37
VMEM = pl.BlockSpec(memory_space=pltpu.VMEM)
HBM = pl.BlockSpec(memory_space=pltpu.HBM)
SMALL = pltpu.CompilerParams(vmem_limit_bytes=16 * 1024 * 1024)
LARGE = pltpu.CompilerParams(vmem_limit_bytes=56 * 1024 * 1024)


def up_to(value, step):
    return -(-value // step) * step


def is_power(size):
    return size & (size - 1) == 0


def partner_to(size, me, step):
    return me ^ step if is_power(size) else (me + step) % size


def partner_from(size, me, step):
    return me ^ step if is_power(size) else (me + size - step) % size


def send(block, axis, step, parity=None):
    size = lax.axis_size(axis)
    sources = [i for i in range(size) if parity is None or i & 1 == parity]
    return lax.ppermute(block, axis, [(i, partner_to(size, i, step)) for i in sources])


def pack(value, out):
    height = value.shape[0]
    largest = jnp.max(jnp.max(jnp.abs(value), axis=0, keepdims=True), axis=1, keepdims=True)
    power = jnp.clip(jnp.ceil(jnp.log2(jnp.maximum(largest, TINY))), -100.0, 100.0)
    out[:height] = value * jnp.exp2(PACK_TOP - power)
    out[height:] = jnp.broadcast_to(power, (PACK_ROWS, value.shape[1]))


def unpack(block):
    height = block.shape[0] - PACK_ROWS
    return block[:height] * jnp.exp2(block[height : height + 1, :1] - PACK_TOP)


def cross(block, step, parity=None):
    return send(block.astype(jnp.float16), "mdl", step, parity).astype(jnp.float32)


def dot(left, right, contract=((1,), (0,))):
    return lax.dot_general(left, right, (contract, ((), ())), preferred_element_type=jnp.float32)


def dispatch_body(owners, local, room, extra, *refs):
    sources, refs = refs[:7], refs[7:]
    outs, refs = refs[:owners], refs[owners:]
    weights, (states, task, batch, sems) = refs[:4], refs[4:]
    rows, width = states.shape
    copies = [
        pltpu.make_async_copy(source, target, sems.at[i])
        for i, (source, target) in enumerate(zip(sources, (states, task, batch, *weights)))
    ]
    for i in (1, 2, 0, 3, 4, 5, 6):
        copies[i].start()
    copies[1].wait()
    copies[2].wait()
    me = lax.axis_index("teach")
    task_list, batch_list = task[...], batch[...]
    group = up_to(owners * local, ROW_TILE)
    named = lax.broadcasted_iota(jnp.int32, (group, rows), 0) == task_list
    earlier = lax.broadcasted_iota(jnp.int32, (rows, rows), 0) < lax.broadcasted_iota(
        jnp.int32, (rows, rows), 1
    )
    named = named.astype(jnp.float32)
    before = dot(named.astype(jnp.bfloat16), earlier.astype(jnp.float32).astype(jnp.bfloat16))
    before = jnp.sum(before * named, axis=0, keepdims=True).astype(jnp.int32)
    owner = task_list // local if local > 1 else task_list
    step = owner ^ me if is_power(owners) else (owner - me + owners) % owners
    place = step * local + task_list % local if local > 1 else step
    slot = place * room + before
    index = lax.broadcasted_iota(jnp.int32, (owners * local * room, rows), 0)
    chosen = (index == slot).astype(jnp.float32)
    head = (index % (local * room) == 0).astype(jnp.float32)
    member = (lax.broadcasted_iota(jnp.int32, (extra, rows), 0) == batch_list).astype(jnp.float32)
    tags = dot(
        (chosen + 2.0 * head).astype(jnp.bfloat16), member.astype(jnp.bfloat16), ((1,), (1,))
    ).astype(jnp.bfloat16)
    copies[0].wait()
    moved = dot(chosen.astype(jnp.bfloat16), states[...]).astype(jnp.bfloat16)
    for k, out in enumerate(outs):
        span = slice(k * local * room, (k + 1) * local * room)
        out[:, :width] = moved[span]
        out[:, width:] = tags[span]
    for copy in copies[3:]:
        copy.wait()


def silu_of(pre):
    return (pre / (1.0 + jnp.exp(-pre))).astype(jnp.bfloat16)


def student(rows, student_up):
    pre = dot(rows, student_up[...])
    sig = 1.0 / (1.0 + jnp.exp(-pre))
    return silu_of(pre), sig * (1.0 + pre * (1.0 - sig))


def forward_body(local, room, first, *refs):
    count = len(refs) - 9 - (not first)
    blocks, refs = refs[:count], refs[count:]
    if not first:
        earlier, refs = refs[0], refs[1:]
    teach_in, teach_out, student_up, student_down = refs[:4]
    tags_out, counts_out, error_out, packed, rows_out = refs[4:]
    width = rows_out.shape[1]
    full = [block[...] for block in blocks]
    counts = None if first else earlier[...]
    for block in full:
        mine = jnp.floor(block[:1, width:].astype(jnp.float32) * 0.5)
        counts = mine if counts is None else counts + mine
    counts_out[...] = counts
    for l in range(local):
        span = slice(l * count * room, (l + 1) * count * room)
        for k, block in enumerate(full):
            start = (l * count + k) * room
            rows_out[start : start + room] = block[l * room : (l + 1) * room, :width]
            tag = block[l * room : (l + 1) * room, width:].astype(jnp.float32)
            if l == 0:
                head = lax.broadcasted_iota(jnp.int32, tag.shape, 0) == 0
                tag = jnp.where(head, tag - 2.0 * jnp.floor(tag * 0.5), tag)
            tags_out[start : start + room] = tag
        rows = rows_out[span]
        hidden = dot(rows, teach_in[l])
        hidden = (hidden / (1.0 + jnp.exp(-hidden))).astype(jnp.bfloat16)
        act = silu_of(dot(rows, student_up[...]))
        error_out[span] = dot(act, student_down[...], ((1,), (1,))) - dot(hidden, teach_out[l])
    pack(error_out[...], packed)


def chosen_columns(columns, owners, studs):
    height = columns // (owners * studs)
    shape = (owners * height, columns)
    row = lax.broadcasted_iota(jnp.int32, shape, 0)
    column = lax.broadcasted_iota(jnp.int32, shape, 1)
    owner = partner_to(owners, lax.axis_index("teach"), row // height)
    wanted = (owner * studs + lax.axis_index("stud")) * height + row % height
    return (column == wanted).astype(jnp.float32).astype(jnp.bfloat16)


def turn(value, chosen):
    return dot(chosen, value, ((1,), (1,))).astype(jnp.bfloat16)


def ahead_body(owners, studs, *refs):
    parts, student_up, outs = refs[:2], refs[2], refs[4:]
    turned, act, slope = outs[:3]
    rows = jnp.concatenate([part[...] for part in parts])
    turned[...] = turn(rows, chosen_columns(rows.shape[1], owners, studs))
    act[...], slope[...] = student(rows, student_up)
    if len(outs) > 3:
        outs[3][...] = chosen_columns(outs[3].shape[1], owners, studs)


def pair_body(own, arrived, *refs):
    total, packed = refs[-2:]
    value = own[...] + unpack(arrived)
    total[...] = value
    pack(value, packed)


def scale_body(*refs):
    halves, tags, counts, scaled = ((refs[0], refs[1], refs[4]), refs[2:4]), refs[5:7], refs[7:-1], refs[-1]
    all_counts = counts[0][...]
    for piece in counts[1:]:
        all_counts = all_counts + piece[...]
    inverse = jnp.where(all_counts > 0, 2.0 / all_counts, 0.0)
    start = 0
    for (own, *arrived), tag in zip(halves, tags):
        weight = jnp.sum(tag[...] * inverse, axis=1, keepdims=True)
        span = slice(start, start + own.shape[0])
        message = arrived[0][...]
        for piece in arrived[1:]:
            message = message + piece[...]
        scaled[span] = ((own[...] + unpack(message)) * weight).astype(scaled.dtype)
        start += own.shape[0]


def backward_body(owners, earlier, scaled, turned, act, slope, chosen, student_down, *refs):
    error = scaled[...]
    down = dot(turn(error, chosen[...]), act[...])
    pre_grad = (dot(error, student_down[...]) * slope[...]).astype(jnp.bfloat16)
    up = dot(turned[...], pre_grad)
    if earlier:
        up, down = up + refs[0][...], down + refs[1][...]
    outs = refs[2 * earlier :]
    if len(outs) == 2:
        outs[0][...], outs[1][...] = up, down
        return
    high, low = up.shape[0] // owners, down.shape[0] // owners
    for k, out in enumerate(outs):
        block = [up[k * high : (k + 1) * high], down[k * low : (k + 1) * low]]
        out[...] = jnp.concatenate(block).astype(out.dtype)


def closing_body(*refs):
    pieces, (grad_up, grad_down, up, down, sems) = refs[:-5], refs[-5:]
    total = pieces[0][...]
    for piece in pieces[1:]:
        total = total + piece[...].astype(jnp.float32)
    cut = up.shape[0]
    up[...] = total[:cut]
    first = pltpu.make_async_copy(up, grad_up, sems.at[0])
    first.start()
    down[...] = total[cut:]
    second = pltpu.make_async_copy(down, grad_down, sems.at[1])
    second.start()
    first.wait()
    second.wait()


def kernel(body, outs, operands, flops, scratch=(), params=SMALL, places=None, to=VMEM):
    return pl.pallas_call(
        body,
        out_shape=outs,
        in_specs=places or [VMEM] * len(operands),
        out_specs=[to] * len(outs),
        scratch_shapes=list(scratch),
        cost_estimate=pl.CostEstimate(flops=flops, bytes_accessed=0, transcendentals=0),
        compiler_params=params,
    )(*operands)


def on_device(states, task_ids, student_batch, teach_in, teach_out, student_up, student_down):
    row_count, width = states.shape
    owners, studs, parts = lax.axis_size("teach"), lax.axis_size("stud"), lax.axis_size("mdl")
    local, _, hidden = teach_in.shape
    actions = teach_out.shape[2]
    units = student_up.shape[1]
    teachers, batches = owners * local, owners * studs
    room = up_to(3 * row_count // (2 * teachers), ROW_TILE)
    extra = up_to(batches, LANES)
    slots = teachers * room
    f32, bf16 = jnp.float32, jnp.bfloat16

    def shape(rows, columns, dtype):
        return jax.ShapeDtypeStruct((rows, columns), dtype)

    height = slots // 2
    half, packed = shape(height, actions, f32), shape(height + PACK_ROWS, actions, f32)
    state = [shape(width // studs, slots, bf16), shape(slots, units, bf16), shape(slots, units, f32)]
    tokens = [ids.reshape(1, row_count) for ids in (task_ids, student_batch)]
    weights = (teach_in, teach_out, student_up, student_down)
    results = kernel(
        functools.partial(dispatch_body, owners, local, room, extra),
        [pltpu.VMEM((local * room, width + extra), bf16)] * owners
        + [pltpu.VMEM(w.shape, w.dtype) for w in weights],
        (states, *tokens, *weights),
        0,
        [pltpu.VMEM(a.shape, a.dtype) for a in (states, *tokens)] + [pltpu.SemaphoreType.DMA((7,))],
        LARGE,
        [HBM] * 7,
    )
    blocks, weights = results[:owners], results[owners:]
    middle = owners // 2
    near = [blocks[0]] + [send(blocks[k], "teach", k) for k in range(1, middle)]
    far = [send(blocks[k], "teach", k) for k in range(owners - 1, middle - 1, -1)]

    def forward(blocks, *earlier):
        rows = len(blocks) * local * room
        return kernel(
            functools.partial(forward_body, local, room, not earlier),
            [shape(rows, extra, f32), shape(1, extra, f32), half, packed, shape(rows, width, bf16)],
            (*blocks, *earlier, *weights),
            0,
        )

    steps = [1 << i for i in range(parts.bit_length() - 1)]
    second_tags, counts, second, second_out, second_rows = forward(near)
    second_in = cross(second_out, steps[-1])
    first_tags, counts, first, first_out, first_rows = forward(far, counts)
    first_in = cross(first_out, steps[0])
    rows, tags = (first_rows, second_rows), (first_tags, second_tags)
    all_counts, mates = [counts], []
    for k in range(1, studs):
        all_counts.append(send(counts, "stud", k))
        mates.append([send(part, "stud", k) for part in rows])
    second_in, all_counts, mates = lax.optimization_barrier((second_in, all_counts, mates))
    for there, back in zip(steps[1:], steps[-2::-1]):
        second, second_out = kernel(pair_body, [half, packed], (second, second_in), 0)
        first, first_out = kernel(pair_body, [half, packed], (first, first_in, second), 0)
        first_out, second_out = lax.optimization_barrier((first_out, second_out))
        first_in = [cross(first_out, there, parity) for parity in (0, 1)]
        second_in = cross(second_out, back)
    ahead = functools.partial(ahead_body, owners, studs)
    *ours, chosen = kernel(
        ahead, state + [shape(actions // studs, actions, bf16)], (*rows, weights[2], first), 0
    )
    known = [ours] + [kernel(ahead, state, (*theirs, weights[2], first), 0) for theirs in mates]
    sums = (first, first_in[0], second, second_in, first_in[1])
    sums, all_counts, known, chosen = lax.optimization_barrier((sums, all_counts, known, chosen))
    (scaled,) = kernel(scale_body, [shape(slots, actions, bf16)], (*sums, *tags, *all_counts), 0)
    errors = [scaled] + [send(scaled, "stud", k) for k in range(1, studs)]
    grads = [shape(width // studs, units, f32), shape(actions // studs, units, f32)]
    heights = [g.shape[0] // owners for g in grads]
    blocks = [shape(sum(heights), units, f32)] + [shape(sum(heights), units, bf16)] * (owners - 1)
    sums = []
    for k, (error, group) in enumerate(zip(errors, known)):
        sums = kernel(
            functools.partial(backward_body, owners, k > 0),
            blocks if k == studs - 1 else grads,
            (error, *group, chosen, weights[3], *sums),
            0,
        )
    pieces = [sums[0]] + [send(sums[k], "teach", k) for k in range(owners - 1, 0, -1)]
    outs = [shape(h, units, f32) for h in heights]
    return kernel(
        closing_body,
        outs,
        pieces,
        0,
        [pltpu.VMEM(o.shape, f32) for o in outs] + [pltpu.SemaphoreType.DMA((2,))],
        to=HBM,
    )


def solution(mesh):
    in_specs = (
        P(("teach", "stud"), None),
        P(("teach", "stud"), None),
        P(("teach", "stud"), None),
        P("teach", None, "mdl"),
        P("teach", "mdl", None),
        P(None, "mdl"),
        P(None, "mdl"),
    )
    out_specs = (P(("teach", "stud"), "mdl"), P(("teach", "stud"), "mdl"))
    return jax.shard_map(
        on_device, mesh=mesh, in_specs=in_specs, out_specs=out_specs, check_vma=False
    )
```

```python
import functools

import jax
import jax.numpy as jnp
from jax import lax
from jax.experimental import pallas as pl
from jax.experimental.pallas import tpu as pltpu
from jax.sharding import PartitionSpec as P

LANES = 128
ROW_TILE = 16
PACK_ROWS = 8
PACK_TOP = 14.0
TINY = 1e-37
VMEM = pl.BlockSpec(memory_space=pltpu.VMEM)
HBM = pl.BlockSpec(memory_space=pltpu.HBM)
SMALL = pltpu.CompilerParams(vmem_limit_bytes=16 * 1024 * 1024)
LARGE = pltpu.CompilerParams(vmem_limit_bytes=56 * 1024 * 1024)


def up_to(value, step):
    return -(-value // step) * step


def is_power(size):
    return size & (size - 1) == 0


def partner_to(size, me, step):
    return me ^ step if is_power(size) else (me + step) % size


def partner_from(size, me, step):
    return me ^ step if is_power(size) else (me + size - step) % size


def send(block, axis, step):
    size = lax.axis_size(axis)
    return lax.ppermute(block, axis, [(i, partner_to(size, i, step)) for i in range(size)])


def pack(value, out):
    height = value.shape[0]
    largest = jnp.max(jnp.max(jnp.abs(value), axis=0, keepdims=True), axis=1, keepdims=True)
    power = jnp.clip(jnp.ceil(jnp.log2(jnp.maximum(largest, TINY))), -100.0, 100.0)
    out[:height] = value * jnp.exp2(PACK_TOP - power)
    out[height:] = jnp.broadcast_to(power, (PACK_ROWS, value.shape[1]))


def unpack(block):
    height = block.shape[0] - PACK_ROWS
    return block[:height] * jnp.exp2(block[height : height + 1, :1] - PACK_TOP)


def cross(block, step):
    return send(block.astype(jnp.float16), "mdl", step).astype(jnp.float32)


def dot(left, right, contract=((1,), (0,))):
    return lax.dot_general(left, right, (contract, ((), ())), preferred_element_type=jnp.float32)


def dispatch_body(owners, local, room, extra, *refs):
    sources, refs = refs[:7], refs[7:]
    outs, refs = refs[:owners], refs[owners:]
    weights, (states, task, batch, sems) = refs[:4], refs[4:]
    rows, width = states.shape
    copies = [
        pltpu.make_async_copy(source, target, sems.at[i])
        for i, (source, target) in enumerate(zip(sources, (states, task, batch, *weights)))
    ]
    for i in (1, 2, 0, 3, 4, 5, 6):
        copies[i].start()
    copies[1].wait()
    copies[2].wait()
    me = lax.axis_index("teach")
    task_list, batch_list = task[...], batch[...]
    group = up_to(owners * local, ROW_TILE)
    named = lax.broadcasted_iota(jnp.int32, (group, rows), 0) == task_list
    earlier = lax.broadcasted_iota(jnp.int32, (rows, rows), 0) < lax.broadcasted_iota(
        jnp.int32, (rows, rows), 1
    )
    named = named.astype(jnp.float32)
    before = dot(named.astype(jnp.bfloat16), earlier.astype(jnp.float32).astype(jnp.bfloat16))
    before = jnp.sum(before * named, axis=0, keepdims=True).astype(jnp.int32)
    owner = task_list // local if local > 1 else task_list
    step = owner ^ me if is_power(owners) else (owner - me + owners) % owners
    place = step * local + task_list % local if local > 1 else step
    slot = place * room + before
    index = lax.broadcasted_iota(jnp.int32, (owners * local * room, rows), 0)
    chosen = (index == slot).astype(jnp.float32)
    head = (index % (local * room) == 0).astype(jnp.float32)
    member = (lax.broadcasted_iota(jnp.int32, (extra, rows), 0) == batch_list).astype(jnp.float32)
    tags = dot(
        (chosen + 2.0 * head).astype(jnp.bfloat16), member.astype(jnp.bfloat16), ((1,), (1,))
    ).astype(jnp.bfloat16)
    copies[0].wait()
    moved = dot(chosen.astype(jnp.bfloat16), states[...]).astype(jnp.bfloat16)
    for k, out in enumerate(outs):
        span = slice(k * local * room, (k + 1) * local * room)
        out[:, :width] = moved[span]
        out[:, width:] = tags[span]
    for copy in copies[3:]:
        copy.wait()


def silu_of(pre):
    return (pre / (1.0 + jnp.exp(-pre))).astype(jnp.bfloat16)


def student(rows, student_up):
    pre = dot(rows, student_up[...])
    sig = 1.0 / (1.0 + jnp.exp(-pre))
    return silu_of(pre), sig * (1.0 + pre * (1.0 - sig))


def forward_body(local, room, first, *refs):
    count = len(refs) - 9 - (not first)
    blocks, refs = refs[:count], refs[count:]
    if not first:
        earlier, refs = refs[0], refs[1:]
    teach_in, teach_out, student_up, student_down = refs[:4]
    tags_out, counts_out, error_out, packed, rows_out = refs[4:]
    width = rows_out.shape[1]
    full = [block[...] for block in blocks]
    counts = None if first else earlier[...]
    for block in full:
        mine = jnp.floor(block[:1, width:].astype(jnp.float32) * 0.5)
        counts = mine if counts is None else counts + mine
    counts_out[...] = counts
    for l in range(local):
        span = slice(l * count * room, (l + 1) * count * room)
        for k, block in enumerate(full):
            start = (l * count + k) * room
            rows_out[start : start + room] = block[l * room : (l + 1) * room, :width]
            tag = block[l * room : (l + 1) * room, width:].astype(jnp.float32)
            if l == 0:
                head = lax.broadcasted_iota(jnp.int32, tag.shape, 0) == 0
                tag = jnp.where(head, tag - 2.0 * jnp.floor(tag * 0.5), tag)
            tags_out[start : start + room] = tag
        rows = rows_out[span]
        hidden = dot(rows, teach_in[l])
        hidden = (hidden / (1.0 + jnp.exp(-hidden))).astype(jnp.bfloat16)
        act = silu_of(dot(rows, student_up[...]))
        error_out[span] = dot(act, student_down[...], ((1,), (1,))) - dot(hidden, teach_out[l])
    pack(error_out[...], packed)


def chosen_columns(columns, owners, studs):
    height = columns // (owners * studs)
    shape = (owners * height, columns)
    row = lax.broadcasted_iota(jnp.int32, shape, 0)
    column = lax.broadcasted_iota(jnp.int32, shape, 1)
    owner = partner_to(owners, lax.axis_index("teach"), row // height)
    wanted = (owner * studs + lax.axis_index("stud")) * height + row % height
    return (column == wanted).astype(jnp.float32).astype(jnp.bfloat16)


def turn(value, chosen):
    return dot(chosen, value, ((1,), (1,))).astype(jnp.bfloat16)


def ahead_body(owners, studs, *refs):
    parts, student_up, outs = refs[:2], refs[2], refs[4:]
    turned, act, slope = outs[:3]
    rows = jnp.concatenate([part[...] for part in parts])
    turned[...] = turn(rows, chosen_columns(rows.shape[1], owners, studs))
    act[...], slope[...] = student(rows, student_up)
    if len(outs) > 3:
        outs[3][...] = chosen_columns(outs[3].shape[1], owners, studs)


def pair_body(own, arrived, *refs):
    total, packed = refs[-2:]
    value = own[...] + unpack(arrived)
    total[...] = value
    pack(value, packed)


def scale_body(*refs):
    halves, tags, counts, scaled = (refs[2:4], refs[:2]), refs[4:6], refs[6:-1], refs[-1]
    all_counts = counts[0][...]
    for piece in counts[1:]:
        all_counts = all_counts + piece[...]
    inverse = jnp.where(all_counts > 0, 2.0 / all_counts, 0.0)
    start = 0
    for (own, arrived), tag in zip(halves, tags):
        weight = jnp.sum(tag[...] * inverse, axis=1, keepdims=True)
        span = slice(start, start + own.shape[0])
        scaled[span] = ((own[...] + unpack(arrived)) * weight).astype(scaled.dtype)
        start += own.shape[0]


def backward_body(owners, earlier, scaled, turned, act, slope, chosen, student_down, *refs):
    error = scaled[...]
    down = dot(turn(error, chosen[...]), act[...])
    pre_grad = (dot(error, student_down[...]) * slope[...]).astype(jnp.bfloat16)
    up = dot(turned[...], pre_grad)
    if earlier:
        up, down = up + refs[0][...], down + refs[1][...]
    outs = refs[2 * earlier :]
    if len(outs) == 2:
        outs[0][...], outs[1][...] = up, down
        return
    high, low = up.shape[0] // owners, down.shape[0] // owners
    for k, out in enumerate(outs):
        block = [up[k * high : (k + 1) * high], down[k * low : (k + 1) * low]]
        out[...] = jnp.concatenate(block).astype(out.dtype)


def closing_body(*refs):
    pieces, (grad_up, grad_down, up, down, sems) = refs[:-5], refs[-5:]
    total = pieces[0][...]
    for piece in pieces[1:]:
        total = total + piece[...].astype(jnp.float32)
    cut = up.shape[0]
    up[...] = total[:cut]
    first = pltpu.make_async_copy(up, grad_up, sems.at[0])
    first.start()
    down[...] = total[cut:]
    second = pltpu.make_async_copy(down, grad_down, sems.at[1])
    second.start()
    first.wait()
    second.wait()


def kernel(body, outs, operands, flops, scratch=(), params=SMALL, places=None, to=VMEM):
    return pl.pallas_call(
        body,
        out_shape=outs,
        in_specs=places or [VMEM] * len(operands),
        out_specs=[to] * len(outs),
        scratch_shapes=list(scratch),
        cost_estimate=pl.CostEstimate(flops=flops, bytes_accessed=0, transcendentals=0),
        compiler_params=params,
    )(*operands)


def on_device(states, task_ids, student_batch, teach_in, teach_out, student_up, student_down):
    row_count, width = states.shape
    owners, studs, parts = lax.axis_size("teach"), lax.axis_size("stud"), lax.axis_size("mdl")
    local, _, hidden = teach_in.shape
    actions = teach_out.shape[2]
    units = student_up.shape[1]
    teachers, batches = owners * local, owners * studs
    room = up_to(3 * row_count // (2 * teachers), ROW_TILE)
    extra = up_to(batches, LANES)
    slots = teachers * room
    f32, bf16 = jnp.float32, jnp.bfloat16

    def shape(rows, columns, dtype):
        return jax.ShapeDtypeStruct((rows, columns), dtype)

    height = slots // 2
    half, packed = shape(height, actions, f32), shape(height + PACK_ROWS, actions, f32)
    state = [shape(width // studs, slots, bf16), shape(slots, units, bf16), shape(slots, units, f32)]
    tokens = [ids.reshape(1, row_count) for ids in (task_ids, student_batch)]
    weights = (teach_in, teach_out, student_up, student_down)
    results = kernel(
        functools.partial(dispatch_body, owners, local, room, extra),
        [pltpu.VMEM((local * room, width + extra), bf16)] * owners
        + [pltpu.VMEM(w.shape, w.dtype) for w in weights],
        (states, *tokens, *weights),
        0,
        [pltpu.VMEM(a.shape, a.dtype) for a in (states, *tokens)] + [pltpu.SemaphoreType.DMA((7,))],
        LARGE,
        [HBM] * 7,
    )
    blocks, weights = results[:owners], results[owners:]
    middle = owners // 2
    near = [blocks[0]] + [send(blocks[k], "teach", k) for k in range(1, middle)]
    far = [send(blocks[k], "teach", k) for k in range(owners - 1, middle - 1, -1)]

    def forward(blocks, *earlier):
        rows = len(blocks) * local * room
        return kernel(
            functools.partial(forward_body, local, room, not earlier),
            [shape(rows, extra, f32), shape(1, extra, f32), half, packed, shape(rows, width, bf16)],
            (*blocks, *earlier, *weights),
            0,
        )

    steps = [1 << i for i in range(parts.bit_length() - 1)]
    second_tags, counts, second, second_out, second_rows = forward(near)
    second_in = cross(second_out, steps[-1])
    first_tags, counts, first, first_out, first_rows = forward(far, counts)
    first_in = cross(first_out, steps[0])
    rows, tags = (first_rows, second_rows), (first_tags, second_tags)
    all_counts, mates = [counts], []
    for k in range(1, studs):
        all_counts.append(send(counts, "stud", k))
        mates.append([send(part, "stud", k) for part in rows])
    second_in, all_counts, mates = lax.optimization_barrier((second_in, all_counts, mates))
    for there, back in zip(steps[1:], steps[-2::-1]):
        second, second_out = kernel(pair_body, [half, packed], (second, second_in), 0)
        first, first_out = kernel(pair_body, [half, packed], (first, first_in, second), 0)
        first_out, second_out = lax.optimization_barrier((first_out, second_out))
        first_in, second_in = cross(first_out, there), cross(second_out, back)
    ahead = functools.partial(ahead_body, owners, studs)
    *ours, chosen = kernel(
        ahead, state + [shape(actions // studs, actions, bf16)], (*rows, weights[2], first), 0
    )
    known = [ours] + [kernel(ahead, state, (*theirs, weights[2], first), 0) for theirs in mates]
    sums = (second, second_in, first, first_in)
    sums, all_counts, known, chosen = lax.optimization_barrier((sums, all_counts, known, chosen))
    (scaled,) = kernel(scale_body, [shape(slots, actions, bf16)], (*sums, *tags, *all_counts), 0)
    errors = [scaled] + [send(scaled, "stud", k) for k in range(1, studs)]
    grads = [shape(width // studs, units, f32), shape(actions // studs, units, f32)]
    heights = [g.shape[0] // owners for g in grads]
    blocks = [shape(sum(heights), units, f32)] + [shape(sum(heights), units, bf16)] * (owners - 1)
    sums = []
    for k, (error, group) in enumerate(zip(errors, known)):
        sums = kernel(
            functools.partial(backward_body, owners, k > 0),
            blocks if k == studs - 1 else grads,
            (error, *group, chosen, weights[3], *sums),
            0,
        )
    pieces = [sums[0]] + [send(sums[k], "teach", k) for k in range(owners - 1, 0, -1)]
    outs = [shape(h, units, f32) for h in heights]
    return kernel(
        closing_body,
        outs,
        pieces,
        0,
        [pltpu.VMEM(o.shape, f32) for o in outs] + [pltpu.SemaphoreType.DMA((2,))],
        to=HBM,
    )


def solution(mesh):
    in_specs = (
        P(("teach", "stud"), None),
        P(("teach", "stud"), None),
        P(("teach", "stud"), None),
        P("teach", None, "mdl"),
        P("teach", "mdl", None),
        P(None, "mdl"),
        P(None, "mdl"),
    )
    out_specs = (P(("teach", "stud"), "mdl"), P(("teach", "stud"), "mdl"))
    return jax.shard_map(
        on_device, mesh=mesh, in_specs=in_specs, out_specs=out_specs, check_vma=False
    )
```

```python
import functools

import jax
import jax.numpy as jnp
from jax import lax
from jax.experimental import pallas as pl
from jax.experimental.pallas import tpu as pltpu
from jax.sharding import PartitionSpec as P

LANES = 128
ROW_TILE = 16
PACK_ROWS = 8
PACK_TOP = 14.0
TINY = 1e-37
VMEM = pl.BlockSpec(memory_space=pltpu.VMEM)
HBM = pl.BlockSpec(memory_space=pltpu.HBM)
SMALL = pltpu.CompilerParams(vmem_limit_bytes=16 * 1024 * 1024)
LARGE = pltpu.CompilerParams(vmem_limit_bytes=56 * 1024 * 1024)


def up_to(value, step):
    return -(-value // step) * step


def is_power(size):
    return size & (size - 1) == 0


def partner_to(size, me, step):
    return me ^ step if is_power(size) else (me + step) % size


def partner_from(size, me, step):
    return me ^ step if is_power(size) else (me + size - step) % size


def send(block, axis, step):
    size = lax.axis_size(axis)
    return lax.ppermute(block, axis, [(i, partner_to(size, i, step)) for i in range(size)])


def pack(value, out):
    height = value.shape[0]
    largest = jnp.max(jnp.max(jnp.abs(value), axis=0, keepdims=True), axis=1, keepdims=True)
    power = jnp.clip(jnp.ceil(jnp.log2(jnp.maximum(largest, TINY))), -100.0, 100.0)
    out[:height] = value * jnp.exp2(PACK_TOP - power)
    out[height:] = jnp.broadcast_to(power, (PACK_ROWS, value.shape[1]))


def unpack(block):
    height = block.shape[0] - PACK_ROWS
    return block[:height] * jnp.exp2(block[height : height + 1, :1] - PACK_TOP)


def cross(block, step):
    return send(block.astype(jnp.float16), "mdl", step).astype(jnp.float32)


def dot(left, right, contract=((1,), (0,))):
    return lax.dot_general(left, right, (contract, ((), ())), preferred_element_type=jnp.float32)


def dispatch_body(owners, local, room, extra, *refs):
    sources, refs = refs[:7], refs[7:]
    outs, refs = refs[:owners], refs[owners:]
    weights, (states, task, batch, sems) = refs[:4], refs[4:]
    rows, width = states.shape
    copies = [
        pltpu.make_async_copy(source, target, sems.at[i])
        for i, (source, target) in enumerate(zip(sources, (states, task, batch, *weights)))
    ]
    for i in (1, 2, 0, 3, 4, 5, 6):
        copies[i].start()
    copies[1].wait()
    copies[2].wait()
    me = lax.axis_index("teach")
    task_list, batch_list = task[...], batch[...]
    group = up_to(owners * local, ROW_TILE)
    named = lax.broadcasted_iota(jnp.int32, (group, rows), 0) == task_list
    earlier = lax.broadcasted_iota(jnp.int32, (rows, rows), 0) < lax.broadcasted_iota(
        jnp.int32, (rows, rows), 1
    )
    named = named.astype(jnp.float32)
    before = dot(named.astype(jnp.bfloat16), earlier.astype(jnp.float32).astype(jnp.bfloat16))
    before = jnp.sum(before * named, axis=0, keepdims=True).astype(jnp.int32)
    owner = task_list // local if local > 1 else task_list
    step = owner ^ me if is_power(owners) else (owner - me + owners) % owners
    place = step * local + task_list % local if local > 1 else step
    slot = place * room + before
    index = lax.broadcasted_iota(jnp.int32, (owners * local * room, rows), 0)
    chosen = (index == slot).astype(jnp.float32)
    head = (index % (local * room) == 0).astype(jnp.float32)
    member = (lax.broadcasted_iota(jnp.int32, (extra, rows), 0) == batch_list).astype(jnp.float32)
    tags = dot(
        (chosen + 2.0 * head).astype(jnp.bfloat16), member.astype(jnp.bfloat16), ((1,), (1,))
    ).astype(jnp.bfloat16)
    copies[0].wait()
    moved = dot(chosen.astype(jnp.bfloat16), states[...]).astype(jnp.bfloat16)
    for k, out in enumerate(outs):
        span = slice(k * local * room, (k + 1) * local * room)
        out[:, :width] = moved[span]
        out[:, width:] = tags[span]
    for copy in copies[3:]:
        copy.wait()


def silu_of(pre):
    return (pre / (1.0 + jnp.exp(-pre))).astype(jnp.bfloat16)


def student(rows, student_up):
    pre = dot(rows, student_up[...])
    sig = 1.0 / (1.0 + jnp.exp(-pre))
    return silu_of(pre), sig * (1.0 + pre * (1.0 - sig))


def forward_body(local, room, first, *refs):
    count = len(refs) - 9 - (not first)
    blocks, refs = refs[:count], refs[count:]
    if not first:
        earlier, refs = refs[0], refs[1:]
    teach_in, teach_out, student_up, student_down = refs[:4]
    tags_out, counts_out, error_out, packed, rows_out = refs[4:]
    width = rows_out.shape[1]
    full = [block[...] for block in blocks]
    counts = None if first else earlier[...]
    for block in full:
        mine = jnp.floor(block[:1, width:].astype(jnp.float32) * 0.5)
        counts = mine if counts is None else counts + mine
    counts_out[...] = counts
    for l in range(local):
        span = slice(l * count * room, (l + 1) * count * room)
        for k, block in enumerate(full):
            start = (l * count + k) * room
            rows_out[start : start + room] = block[l * room : (l + 1) * room, :width]
            tag = block[l * room : (l + 1) * room, width:].astype(jnp.float32)
            if l == 0:
                head = lax.broadcasted_iota(jnp.int32, tag.shape, 0) == 0
                tag = jnp.where(head, tag - 2.0 * jnp.floor(tag * 0.5), tag)
            tags_out[start : start + room] = tag
        rows = rows_out[span]
        hidden = dot(rows, teach_in[l])
        hidden = (hidden / (1.0 + jnp.exp(-hidden))).astype(jnp.bfloat16)
        act = silu_of(dot(rows, student_up[...]))
        error_out[span] = dot(act, student_down[...], ((1,), (1,))) - dot(hidden, teach_out[l])
    pack(error_out[...], packed)


def chosen_columns(columns, owners, studs):
    height = columns // (owners * studs)
    shape = (owners * height, columns)
    row = lax.broadcasted_iota(jnp.int32, shape, 0)
    column = lax.broadcasted_iota(jnp.int32, shape, 1)
    owner = partner_to(owners, lax.axis_index("teach"), row // height)
    wanted = (owner * studs + lax.axis_index("stud")) * height + row % height
    return (column == wanted).astype(jnp.float32).astype(jnp.bfloat16)


def turn(value, chosen):
    return dot(chosen, value, ((1,), (1,))).astype(jnp.bfloat16)


def ahead_body(owners, studs, *refs):
    parts, student_up, outs = refs[:2], refs[2], refs[4:]
    turned, act, slope = outs[:3]
    rows = jnp.concatenate([part[...] for part in parts])
    turned[...] = turn(rows, chosen_columns(rows.shape[1], owners, studs))
    act[...], slope[...] = student(rows, student_up)
    if len(outs) > 3:
        outs[3][...] = chosen_columns(outs[3].shape[1], owners, studs)


def pair_body(own, arrived, *refs):
    total, packed = refs[-2:]
    value = own[...] + unpack(arrived)
    total[...] = value
    pack(value, packed)


def scale_body(*refs):
    halves, tags, counts, scaled = (refs[2:4], refs[:2]), refs[4:6], refs[6:-1], refs[-1]
    all_counts = counts[0][...]
    for piece in counts[1:]:
        all_counts = all_counts + piece[...]
    inverse = jnp.where(all_counts > 0, 2.0 / all_counts, 0.0)
    start = 0
    for (own, arrived), tag in zip(halves, tags):
        weight = jnp.sum(tag[...] * inverse, axis=1, keepdims=True)
        span = slice(start, start + own.shape[0])
        scaled[span] = ((own[...] + unpack(arrived)) * weight).astype(scaled.dtype)
        start += own.shape[0]


def backward_body(owners, earlier, scaled, turned, act, slope, chosen, student_down, *refs):
    error = scaled[...]
    down = dot(turn(error, chosen[...]), act[...])
    pre_grad = (dot(error, student_down[...]) * slope[...]).astype(jnp.bfloat16)
    up = dot(turned[...], pre_grad)
    if earlier:
        up, down = up + refs[0][...], down + refs[1][...]
    outs = refs[2 * earlier :]
    if len(outs) == 2:
        outs[0][...], outs[1][...] = up, down
        return
    high, low = up.shape[0] // owners, down.shape[0] // owners
    for k, out in enumerate(outs):
        block = [up[k * high : (k + 1) * high], down[k * low : (k + 1) * low]]
        out[...] = jnp.concatenate(block).astype(out.dtype)


def closing_body(*refs):
    pieces, (grad_up, grad_down, up, down, sems) = refs[:-5], refs[-5:]
    total = pieces[0][...]
    for piece in pieces[1:]:
        total = total + piece[...].astype(jnp.float32)
    cut = up.shape[0]
    up[...] = total[:cut]
    first = pltpu.make_async_copy(up, grad_up, sems.at[0])
    first.start()
    down[...] = total[cut:]
    second = pltpu.make_async_copy(down, grad_down, sems.at[1])
    second.start()
    first.wait()
    second.wait()


def kernel(body, outs, operands, flops, scratch=(), params=SMALL, places=None, to=VMEM):
    return pl.pallas_call(
        body,
        out_shape=outs,
        in_specs=places or [VMEM] * len(operands),
        out_specs=[to] * len(outs),
        scratch_shapes=list(scratch),
        cost_estimate=pl.CostEstimate(flops=flops, bytes_accessed=0, transcendentals=0),
        compiler_params=params,
    )(*operands)


def on_device(states, task_ids, student_batch, teach_in, teach_out, student_up, student_down):
    row_count, width = states.shape
    owners, studs, parts = lax.axis_size("teach"), lax.axis_size("stud"), lax.axis_size("mdl")
    local, _, hidden = teach_in.shape
    actions = teach_out.shape[2]
    units = student_up.shape[1]
    teachers, batches = owners * local, owners * studs
    room = up_to(3 * row_count // (2 * teachers), ROW_TILE)
    extra = up_to(batches, LANES)
    slots = teachers * room
    f32, bf16 = jnp.float32, jnp.bfloat16

    def shape(rows, columns, dtype):
        return jax.ShapeDtypeStruct((rows, columns), dtype)

    height = slots // 2
    half, packed = shape(height, actions, f32), shape(height + PACK_ROWS, actions, f32)
    state = [shape(width // studs, slots, bf16), shape(slots, units, bf16), shape(slots, units, f32)]
    tokens = [ids.reshape(1, row_count) for ids in (task_ids, student_batch)]
    weights = (teach_in, teach_out, student_up, student_down)
    results = kernel(
        functools.partial(dispatch_body, owners, local, room, extra),
        [pltpu.VMEM((local * room, width + extra), bf16)] * owners
        + [pltpu.VMEM(w.shape, w.dtype) for w in weights],
        (states, *tokens, *weights),
        0,
        [pltpu.VMEM(a.shape, a.dtype) for a in (states, *tokens)] + [pltpu.SemaphoreType.DMA((7,))],
        LARGE,
        [HBM] * 7,
    )
    blocks, weights = results[:owners], results[owners:]
    middle = owners // 2
    near = [blocks[0]] + [send(blocks[k], "teach", k) for k in range(owners - 1, middle, -1)]
    far = [send(blocks[k], "teach", k) for k in range(middle, 0, -1)]

    def forward(blocks, *earlier):
        rows = len(blocks) * local * room
        return kernel(
            functools.partial(forward_body, local, room, not earlier),
            [shape(rows, extra, f32), shape(1, extra, f32), half, packed, shape(rows, width, bf16)],
            (*blocks, *earlier, *weights),
            0,
        )

    steps = [1 << i for i in range(parts.bit_length() - 1)]
    second_tags, counts, second, second_out, second_rows = forward(near)
    second_in = cross(second_out, steps[-1])
    first_tags, counts, first, first_out, first_rows = forward(far, counts)
    first_in = cross(first_out, steps[0])
    rows, tags = (first_rows, second_rows), (first_tags, second_tags)
    all_counts, mates = [counts], []
    for k in range(1, studs):
        all_counts.append(send(counts, "stud", k))
        mates.append([send(part, "stud", k) for part in rows])
    second_in, all_counts, mates = lax.optimization_barrier((second_in, all_counts, mates))
    for there, back in zip(steps[1:], steps[-2::-1]):
        second, second_out = kernel(pair_body, [half, packed], (second, second_in), 0)
        first, first_out = kernel(pair_body, [half, packed], (first, first_in, second), 0)
        first_out, second_out = lax.optimization_barrier((first_out, second_out))
        first_in, second_in = cross(first_out, there), cross(second_out, back)
    ahead = functools.partial(ahead_body, owners, studs)
    *ours, chosen = kernel(
        ahead, state + [shape(actions // studs, actions, bf16)], (*rows, weights[2], first), 0
    )
    known = [ours] + [kernel(ahead, state, (*theirs, weights[2], first), 0) for theirs in mates]
    sums = (second, second_in, first, first_in)
    sums, all_counts, known, chosen = lax.optimization_barrier((sums, all_counts, known, chosen))
    (scaled,) = kernel(scale_body, [shape(slots, actions, bf16)], (*sums, *tags, *all_counts), 0)
    errors = [scaled] + [send(scaled, "stud", k) for k in range(1, studs)]
    grads = [shape(width // studs, units, f32), shape(actions // studs, units, f32)]
    heights = [g.shape[0] // owners for g in grads]
    blocks = [shape(sum(heights), units, f32)] + [shape(sum(heights), units, bf16)] * (owners - 1)
    sums = []
    for k, (error, group) in enumerate(zip(errors, known)):
        sums = kernel(
            functools.partial(backward_body, owners, k > 0),
            blocks if k == studs - 1 else grads,
            (error, *group, chosen, weights[3], *sums),
            0,
        )
    pieces = [sums[0]] + [send(sums[k], "teach", k) for k in range(owners - 1, 0, -1)]
    outs = [shape(h, units, f32) for h in heights]
    return kernel(
        closing_body,
        outs,
        pieces,
        0,
        [pltpu.VMEM(o.shape, f32) for o in outs] + [pltpu.SemaphoreType.DMA((2,))],
        to=HBM,
    )


def solution(mesh):
    in_specs = (
        P(("teach", "stud"), None),
        P(("teach", "stud"), None),
        P(("teach", "stud"), None),
        P("teach", None, "mdl"),
        P("teach", "mdl", None),
        P(None, "mdl"),
        P(None, "mdl"),
    )
    out_specs = (P(("teach", "stud"), "mdl"), P(("teach", "stud"), "mdl"))
    return jax.shard_map(
        on_device, mesh=mesh, in_specs=in_specs, out_specs=out_specs, check_vma=False
    )
```

```python
import functools

import jax
import jax.numpy as jnp
from jax import lax
from jax.experimental import pallas as pl
from jax.experimental.pallas import tpu as pltpu
from jax.sharding import PartitionSpec as P

LANES = 128
ROW_TILE = 16
PACK_ROWS = 8
PACK_TOP = 14.0
TINY = 1e-37
VMEM = pl.BlockSpec(memory_space=pltpu.VMEM)
HBM = pl.BlockSpec(memory_space=pltpu.HBM)
SMALL = pltpu.CompilerParams(vmem_limit_bytes=16 * 1024 * 1024)
LARGE = pltpu.CompilerParams(vmem_limit_bytes=56 * 1024 * 1024)


def up_to(value, step):
    return -(-value // step) * step


def is_power(size):
    return size & (size - 1) == 0


def partner_to(size, me, step):
    return me ^ step if is_power(size) else (me + step) % size


def partner_from(size, me, step):
    return me ^ step if is_power(size) else (me + size - step) % size


def send(block, axis, step):
    size = lax.axis_size(axis)
    return lax.ppermute(block, axis, [(i, partner_to(size, i, step)) for i in range(size)])


def pack(value, out):
    height = value.shape[0]
    largest = jnp.max(jnp.max(jnp.abs(value), axis=0, keepdims=True), axis=1, keepdims=True)
    power = jnp.clip(jnp.ceil(jnp.log2(jnp.maximum(largest, TINY))), -100.0, 100.0)
    out[:height] = value * jnp.exp2(PACK_TOP - power)
    out[height:] = jnp.broadcast_to(power, (PACK_ROWS, value.shape[1]))


def unpack(block):
    height = block.shape[0] - PACK_ROWS
    return block[:height] * jnp.exp2(block[height : height + 1, :1] - PACK_TOP)


def cross(block, step):
    return send(block.astype(jnp.float16), "mdl", step).astype(jnp.float32)


def dot(left, right, contract=((1,), (0,))):
    return lax.dot_general(left, right, (contract, ((), ())), preferred_element_type=jnp.float32)


def dispatch_body(owners, local, room, extra, *refs):
    sources, refs = refs[:7], refs[7:]
    outs, refs = refs[:owners], refs[owners:]
    weights, (states, task, batch, sems) = refs[:4], refs[4:]
    rows, width = states.shape
    copies = [
        pltpu.make_async_copy(source, target, sems.at[i])
        for i, (source, target) in enumerate(zip(sources, (states, task, batch, *weights)))
    ]
    for i in (1, 2, 0, 3, 4, 5, 6):
        copies[i].start()
    copies[1].wait()
    copies[2].wait()
    me = lax.axis_index("teach")
    task_list, batch_list = task[...], batch[...]
    group = up_to(owners * local, ROW_TILE)
    named = lax.broadcasted_iota(jnp.int32, (group, rows), 0) == task_list
    earlier = lax.broadcasted_iota(jnp.int32, (rows, rows), 0) < lax.broadcasted_iota(
        jnp.int32, (rows, rows), 1
    )
    named = named.astype(jnp.float32)
    before = dot(named.astype(jnp.bfloat16), earlier.astype(jnp.float32).astype(jnp.bfloat16))
    before = jnp.sum(before * named, axis=0, keepdims=True).astype(jnp.int32)
    owner = task_list // local if local > 1 else task_list
    step = owner ^ me if is_power(owners) else (owner - me + owners) % owners
    place = step * local + task_list % local if local > 1 else step
    slot = place * room + before
    index = lax.broadcasted_iota(jnp.int32, (owners * local * room, rows), 0)
    chosen = (index == slot).astype(jnp.float32)
    head = (index % (local * room) == 0).astype(jnp.float32)
    member = (lax.broadcasted_iota(jnp.int32, (extra, rows), 0) == batch_list).astype(jnp.float32)
    tags = dot(
        (chosen + 2.0 * head).astype(jnp.bfloat16), member.astype(jnp.bfloat16), ((1,), (1,))
    ).astype(jnp.bfloat16)
    copies[0].wait()
    moved = dot(chosen.astype(jnp.bfloat16), states[...]).astype(jnp.bfloat16)
    for k, out in enumerate(outs):
        span = slice(k * local * room, (k + 1) * local * room)
        out[:, :width] = moved[span]
        out[:, width:] = tags[span]
    for copy in copies[3:]:
        copy.wait()


def silu_of(pre):
    return (pre / (1.0 + jnp.exp(-pre))).astype(jnp.bfloat16)


def student(rows, student_up):
    pre = dot(rows, student_up[...])
    sig = 1.0 / (1.0 + jnp.exp(-pre))
    return silu_of(pre), sig * (1.0 + pre * (1.0 - sig))


def forward_body(local, room, first, *refs):
    count = len(refs) - 9 - (not first)
    blocks, refs = refs[:count], refs[count:]
    if not first:
        earlier, refs = refs[0], refs[1:]
    teach_in, teach_out, student_up, student_down = refs[:4]
    tags_out, counts_out, error_out, packed, rows_out = refs[4:]
    width = rows_out.shape[1]
    full = [block[...] for block in blocks]
    counts = None if first else earlier[...]
    for block in full:
        mine = jnp.floor(block[:1, width:].astype(jnp.float32) * 0.5)
        counts = mine if counts is None else counts + mine
    counts_out[...] = counts
    for l in range(local):
        span = slice(l * count * room, (l + 1) * count * room)
        for k, block in enumerate(full):
            start = (l * count + k) * room
            rows_out[start : start + room] = block[l * room : (l + 1) * room, :width]
            tag = block[l * room : (l + 1) * room, width:].astype(jnp.float32)
            if l == 0:
                head = lax.broadcasted_iota(jnp.int32, tag.shape, 0) == 0
                tag = jnp.where(head, tag - 2.0 * jnp.floor(tag * 0.5), tag)
            tags_out[start : start + room] = tag
        rows = rows_out[span]
        hidden = dot(rows, teach_in[l])
        hidden = (hidden / (1.0 + jnp.exp(-hidden))).astype(jnp.bfloat16)
        act = silu_of(dot(rows, student_up[...]))
        error_out[span] = dot(act, student_down[...], ((1,), (1,))) - dot(hidden, teach_out[l])
    pack(error_out[...], packed)


def chosen_columns(columns, owners, studs):
    height = columns // (owners * studs)
    shape = (owners * height, columns)
    row = lax.broadcasted_iota(jnp.int32, shape, 0)
    column = lax.broadcasted_iota(jnp.int32, shape, 1)
    owner = partner_to(owners, lax.axis_index("teach"), row // height)
    wanted = (owner * studs + lax.axis_index("stud")) * height + row % height
    return (column == wanted).astype(jnp.float32).astype(jnp.bfloat16)


def turn(value, chosen):
    return dot(chosen, value, ((1,), (1,))).astype(jnp.bfloat16)


def ahead_body(owners, studs, *refs):
    parts, student_up, outs = refs[:2], refs[2], refs[4:]
    turned, act, slope = outs[:3]
    rows = jnp.concatenate([part[...] for part in parts])
    turned[...] = turn(rows, chosen_columns(rows.shape[1], owners, studs))
    act[...], slope[...] = student(rows, student_up)
    if len(outs) > 3:
        outs[3][...] = chosen_columns(outs[3].shape[1], owners, studs)


def pair_body(*refs):
    for i in range(2):
        own, arrived = refs[2 * i : 2 * i + 2]
        total, packed = refs[2 * i + 4 : 2 * i + 6]
        value = own[...] + unpack(arrived)
        total[...] = value
        pack(value, packed)


def scale_body(*refs):
    halves, tags, counts, scaled = (refs[2:4], refs[:2]), refs[4:6], refs[6:-1], refs[-1]
    all_counts = counts[0][...]
    for piece in counts[1:]:
        all_counts = all_counts + piece[...]
    inverse = jnp.where(all_counts > 0, 2.0 / all_counts, 0.0)
    start = 0
    for (own, arrived), tag in zip(halves, tags):
        weight = jnp.sum(tag[...] * inverse, axis=1, keepdims=True)
        span = slice(start, start + own.shape[0])
        scaled[span] = ((own[...] + unpack(arrived)) * weight).astype(scaled.dtype)
        start += own.shape[0]


def backward_body(owners, earlier, scaled, turned, act, slope, chosen, student_down, *refs):
    error = scaled[...]
    down = dot(turn(error, chosen[...]), act[...])
    pre_grad = (dot(error, student_down[...]) * slope[...]).astype(jnp.bfloat16)
    up = dot(turned[...], pre_grad)
    if earlier:
        up, down = up + refs[0][...], down + refs[1][...]
    outs = refs[2 * earlier :]
    if len(outs) == 2:
        outs[0][...], outs[1][...] = up, down
        return
    high, low = up.shape[0] // owners, down.shape[0] // owners
    for k, out in enumerate(outs):
        block = [up[k * high : (k + 1) * high], down[k * low : (k + 1) * low]]
        out[...] = jnp.concatenate(block).astype(out.dtype)


def closing_body(*refs):
    pieces, (grad_up, grad_down, up, down, sems) = refs[:-5], refs[-5:]
    total = pieces[0][...]
    for piece in pieces[1:]:
        total = total + piece[...].astype(jnp.float32)
    cut = up.shape[0]
    up[...] = total[:cut]
    first = pltpu.make_async_copy(up, grad_up, sems.at[0])
    first.start()
    down[...] = total[cut:]
    second = pltpu.make_async_copy(down, grad_down, sems.at[1])
    second.start()
    first.wait()
    second.wait()


def kernel(body, outs, operands, flops, scratch=(), params=SMALL, places=None, to=VMEM):
    return pl.pallas_call(
        body,
        out_shape=outs,
        in_specs=places or [VMEM] * len(operands),
        out_specs=[to] * len(outs),
        scratch_shapes=list(scratch),
        cost_estimate=pl.CostEstimate(flops=flops, bytes_accessed=0, transcendentals=0),
        compiler_params=params,
    )(*operands)


def on_device(states, task_ids, student_batch, teach_in, teach_out, student_up, student_down):
    row_count, width = states.shape
    owners, studs, parts = lax.axis_size("teach"), lax.axis_size("stud"), lax.axis_size("mdl")
    local, _, hidden = teach_in.shape
    actions = teach_out.shape[2]
    units = student_up.shape[1]
    teachers, batches = owners * local, owners * studs
    room = up_to(3 * row_count // (2 * teachers), ROW_TILE)
    extra = up_to(batches, LANES)
    slots = teachers * room
    f32, bf16 = jnp.float32, jnp.bfloat16

    def shape(rows, columns, dtype):
        return jax.ShapeDtypeStruct((rows, columns), dtype)

    height = slots // 2
    half, packed = shape(height, actions, f32), shape(height + PACK_ROWS, actions, f32)
    state = [shape(width // studs, slots, bf16), shape(slots, units, bf16), shape(slots, units, f32)]
    tokens = [ids.reshape(1, row_count) for ids in (task_ids, student_batch)]
    weights = (teach_in, teach_out, student_up, student_down)
    results = kernel(
        functools.partial(dispatch_body, owners, local, room, extra),
        [pltpu.VMEM((local * room, width + extra), bf16)] * owners
        + [pltpu.VMEM(w.shape, w.dtype) for w in weights],
        (states, *tokens, *weights),
        0,
        [pltpu.VMEM(a.shape, a.dtype) for a in (states, *tokens)] + [pltpu.SemaphoreType.DMA((7,))],
        LARGE,
        [HBM] * 7,
    )
    blocks, weights = results[:owners], results[owners:]
    middle = owners // 2
    near = [blocks[0]] + [send(blocks[k], "teach", k) for k in range(1, middle)]
    far = [send(blocks[k], "teach", k) for k in range(owners - 1, middle - 1, -1)]

    def forward(blocks, *earlier):
        rows = len(blocks) * local * room
        return kernel(
            functools.partial(forward_body, local, room, not earlier),
            [shape(rows, extra, f32), shape(1, extra, f32), half, packed, shape(rows, width, bf16)],
            (*blocks, *earlier, *weights),
            0,
        )

    steps = [1 << i for i in range(parts.bit_length() - 1)]
    second_tags, counts, second, second_out, second_rows = forward(near)
    second_in = cross(second_out, steps[-1])
    first_tags, counts, first, first_out, first_rows = forward(far, counts)
    first_in = cross(first_out, steps[0])
    rows, tags = (first_rows, second_rows), (first_tags, second_tags)
    all_counts, mates = [counts], []
    for k in range(1, studs):
        all_counts.append(send(counts, "stud", k))
        mates.append([send(part, "stud", k) for part in rows])
    first_in, second_in, all_counts = lax.optimization_barrier((first_in, second_in, all_counts))
    for there, back in zip(steps[1:], steps[-2::-1]):
        first, first_out, second, second_out = kernel(
            pair_body, [half, packed] * 2, (first, first_in, second, second_in), 0
        )
        first_in, second_in = cross(first_out, there), cross(second_out, back)
    ahead = functools.partial(ahead_body, owners, studs)
    *ours, chosen = kernel(
        ahead, state + [shape(actions // studs, actions, bf16)], (*rows, weights[2], first), 0
    )
    known = [ours] + [kernel(ahead, state, (*theirs, weights[2], first), 0) for theirs in mates]
    sums = (second, second_in, first, first_in)
    sums, all_counts, known, chosen = lax.optimization_barrier((sums, all_counts, known, chosen))
    (scaled,) = kernel(scale_body, [shape(slots, actions, bf16)], (*sums, *tags, *all_counts), 0)
    errors = [scaled] + [send(scaled, "stud", k) for k in range(1, studs)]
    grads = [shape(width // studs, units, f32), shape(actions // studs, units, f32)]
    heights = [g.shape[0] // owners for g in grads]
    blocks = [shape(sum(heights), units, f32)] + [shape(sum(heights), units, bf16)] * (owners - 1)
    sums = []
    for k, (error, group) in enumerate(zip(errors, known)):
        sums = kernel(
            functools.partial(backward_body, owners, k > 0),
            blocks if k == studs - 1 else grads,
            (error, *group, chosen, weights[3], *sums),
            0,
        )
    pieces = [sums[0]] + [send(sums[k], "teach", k) for k in range(owners - 1, 0, -1)]
    outs = [shape(h, units, f32) for h in heights]
    return kernel(
        closing_body,
        outs,
        pieces,
        0,
        [pltpu.VMEM(o.shape, f32) for o in outs] + [pltpu.SemaphoreType.DMA((2,))],
        to=HBM,
    )


def solution(mesh):
    in_specs = (
        P(("teach", "stud"), None),
        P(("teach", "stud"), None),
        P(("teach", "stud"), None),
        P("teach", None, "mdl"),
        P("teach", "mdl", None),
        P(None, "mdl"),
        P(None, "mdl"),
    )
    out_specs = (P(("teach", "stud"), "mdl"), P(("teach", "stud"), "mdl"))
    return jax.shard_map(
        on_device, mesh=mesh, in_specs=in_specs, out_specs=out_specs, check_vma=False
    )
```

```python
import functools

import jax
import jax.numpy as jnp
from jax import lax
from jax.experimental import pallas as pl
from jax.experimental.pallas import tpu as pltpu
from jax.sharding import PartitionSpec as P

LANES = 128
ROW_TILE = 16
PACK_ROWS = 8
PACK_TOP = 14.0
TINY = 1e-37
VMEM = pl.BlockSpec(memory_space=pltpu.VMEM)
HBM = pl.BlockSpec(memory_space=pltpu.HBM)
SMALL = pltpu.CompilerParams(vmem_limit_bytes=16 * 1024 * 1024)
LARGE = pltpu.CompilerParams(vmem_limit_bytes=56 * 1024 * 1024)


def up_to(value, step):
    return -(-value // step) * step


def is_power(size):
    return size & (size - 1) == 0


def partner_to(size, me, step):
    return me ^ step if is_power(size) else (me + step) % size


def partner_from(size, me, step):
    return me ^ step if is_power(size) else (me + size - step) % size


def send(block, axis, step):
    size = lax.axis_size(axis)
    return lax.ppermute(block, axis, [(i, partner_to(size, i, step)) for i in range(size)])


def pack(value, out):
    height = value.shape[0]
    largest = jnp.max(jnp.max(jnp.abs(value), axis=0, keepdims=True), axis=1, keepdims=True)
    power = jnp.clip(jnp.ceil(jnp.log2(jnp.maximum(largest, TINY))), -100.0, 100.0)
    out[:height] = value * jnp.exp2(PACK_TOP - power)
    out[height:] = jnp.broadcast_to(power, (PACK_ROWS, value.shape[1]))


def unpack(block):
    height = block.shape[0] - PACK_ROWS
    return block[:height] * jnp.exp2(block[height : height + 1, :1] - PACK_TOP)


def cross(block, step):
    return send(block.astype(jnp.float16), "mdl", step).astype(jnp.float32)


def dot(left, right, contract=((1,), (0,))):
    return lax.dot_general(left, right, (contract, ((), ())), preferred_element_type=jnp.float32)


def dispatch_body(owners, local, room, extra, *refs):
    sources, refs = refs[:7], refs[7:]
    outs, refs = refs[:owners], refs[owners:]
    weights, (states, task, batch, sems) = refs[:4], refs[4:]
    rows, width = states.shape
    copies = [
        pltpu.make_async_copy(source, target, sems.at[i])
        for i, (source, target) in enumerate(zip(sources, (states, task, batch, *weights)))
    ]
    for i in (1, 2, 0, 3, 4, 5, 6):
        copies[i].start()
    copies[1].wait()
    copies[2].wait()
    me = lax.axis_index("teach")
    task_list, batch_list = task[...], batch[...]
    group = up_to(owners * local, ROW_TILE)
    named = lax.broadcasted_iota(jnp.int32, (group, rows), 0) == task_list
    earlier = lax.broadcasted_iota(jnp.int32, (rows, rows), 0) < lax.broadcasted_iota(
        jnp.int32, (rows, rows), 1
    )
    named = named.astype(jnp.float32)
    before = dot(named.astype(jnp.bfloat16), earlier.astype(jnp.float32).astype(jnp.bfloat16))
    before = jnp.sum(before * named, axis=0, keepdims=True).astype(jnp.int32)
    owner = task_list // local if local > 1 else task_list
    step = owner ^ me if is_power(owners) else (owner - me + owners) % owners
    place = step * local + task_list % local if local > 1 else step
    slot = place * room + before
    index = lax.broadcasted_iota(jnp.int32, (owners * local * room, rows), 0)
    chosen = (index == slot).astype(jnp.float32)
    head = (index % (local * room) == 0).astype(jnp.float32)
    member = (lax.broadcasted_iota(jnp.int32, (extra, rows), 0) == batch_list).astype(jnp.float32)
    tags = dot(
        (chosen + 2.0 * head).astype(jnp.bfloat16), member.astype(jnp.bfloat16), ((1,), (1,))
    ).astype(jnp.bfloat16)
    copies[0].wait()
    moved = dot(chosen.astype(jnp.bfloat16), states[...]).astype(jnp.bfloat16)
    for k, out in enumerate(outs):
        span = slice(k * local * room, (k + 1) * local * room)
        out[:, :width] = moved[span]
        out[:, width:] = tags[span]
    for copy in copies[3:]:
        copy.wait()


def silu_of(pre):
    return (pre / (1.0 + jnp.exp(-pre))).astype(jnp.bfloat16)


def student(rows, student_up):
    pre = dot(rows, student_up[...])
    sig = 1.0 / (1.0 + jnp.exp(-pre))
    return silu_of(pre), sig * (1.0 + pre * (1.0 - sig))


def forward_body(local, room, first, *refs):
    count = len(refs) - 9 - (not first)
    blocks, refs = refs[:count], refs[count:]
    if not first:
        earlier, refs = refs[0], refs[1:]
    teach_in, teach_out, student_up, student_down = refs[:4]
    tags_out, counts_out, error_out, packed, rows_out = refs[4:]
    width = rows_out.shape[1]
    full = [block[...] for block in blocks]
    counts = None if first else earlier[...]
    for block in full:
        mine = jnp.floor(block[:1, width:].astype(jnp.float32) * 0.5)
        counts = mine if counts is None else counts + mine
    counts_out[...] = counts
    for l in range(local):
        span = slice(l * count * room, (l + 1) * count * room)
        for k, block in enumerate(full):
            start = (l * count + k) * room
            rows_out[start : start + room] = block[l * room : (l + 1) * room, :width]
            tag = block[l * room : (l + 1) * room, width:].astype(jnp.float32)
            if l == 0:
                head = lax.broadcasted_iota(jnp.int32, tag.shape, 0) == 0
                tag = jnp.where(head, tag - 2.0 * jnp.floor(tag * 0.5), tag)
            tags_out[start : start + room] = tag
        rows = rows_out[span]
        hidden = dot(rows, teach_in[l])
        hidden = (hidden / (1.0 + jnp.exp(-hidden))).astype(jnp.bfloat16)
        act = silu_of(dot(rows, student_up[...]))
        error_out[span] = dot(act, student_down[...], ((1,), (1,))) - dot(hidden, teach_out[l])
    pack(error_out[...], packed)


def chosen_columns(columns, owners, studs):
    height = columns // (owners * studs)
    shape = (owners * height, columns)
    row = lax.broadcasted_iota(jnp.int32, shape, 0)
    column = lax.broadcasted_iota(jnp.int32, shape, 1)
    owner = partner_to(owners, lax.axis_index("teach"), row // height)
    wanted = (owner * studs + lax.axis_index("stud")) * height + row % height
    return (column == wanted).astype(jnp.float32).astype(jnp.bfloat16)


def turn(value, chosen):
    return dot(chosen, value, ((1,), (1,))).astype(jnp.bfloat16)


def ahead_body(owners, studs, *refs):
    parts, student_up, outs = refs[:2], refs[2], refs[4:]
    turned, act, slope = outs[:3]
    rows = jnp.concatenate([part[...] for part in parts])
    turned[...] = turn(rows, chosen_columns(rows.shape[1], owners, studs))
    act[...], slope[...] = student(rows, student_up)
    if len(outs) > 3:
        outs[3][...] = chosen_columns(outs[3].shape[1], owners, studs)


def pair_body(own, arrived, *refs):
    total, packed = refs[-2:]
    value = own[...] + unpack(arrived)
    total[...] = value
    pack(value, packed)


def scale_body(*refs):
    halves, tags, counts, scaled = (refs[2:4], refs[:2]), refs[4:6], refs[6:-1], refs[-1]
    all_counts = counts[0][...]
    for piece in counts[1:]:
        all_counts = all_counts + piece[...]
    inverse = jnp.where(all_counts > 0, 2.0 / all_counts, 0.0)
    start = 0
    for (own, arrived), tag in zip(halves, tags):
        weight = jnp.sum(tag[...] * inverse, axis=1, keepdims=True)
        span = slice(start, start + own.shape[0])
        scaled[span] = ((own[...] + unpack(arrived)) * weight).astype(scaled.dtype)
        start += own.shape[0]


def backward_body(owners, earlier, scaled, turned, act, slope, chosen, student_down, *refs):
    error = scaled[...]
    down = dot(turn(error, chosen[...]), act[...])
    pre_grad = (dot(error, student_down[...]) * slope[...]).astype(jnp.bfloat16)
    up = dot(turned[...], pre_grad)
    if earlier:
        up, down = up + refs[0][...], down + refs[1][...]
    outs = refs[2 * earlier :]
    if len(outs) == 2:
        outs[0][...], outs[1][...] = up, down
        return
    high, low = up.shape[0] // owners, down.shape[0] // owners
    for k, out in enumerate(outs):
        block = [up[k * high : (k + 1) * high], down[k * low : (k + 1) * low]]
        out[...] = jnp.concatenate(block).astype(out.dtype)


def closing_body(*refs):
    pieces, (grad_up, grad_down, up, down, sems) = refs[:-5], refs[-5:]
    total = pieces[0][...]
    for piece in pieces[1:]:
        total = total + piece[...].astype(jnp.float32)
    cut = up.shape[0]
    up[...] = total[:cut]
    first = pltpu.make_async_copy(up, grad_up, sems.at[0])
    first.start()
    down[...] = total[cut:]
    second = pltpu.make_async_copy(down, grad_down, sems.at[1])
    second.start()
    first.wait()
    second.wait()


def kernel(body, outs, operands, flops, scratch=(), params=SMALL, places=None, to=VMEM):
    return pl.pallas_call(
        body,
        out_shape=outs,
        in_specs=places or [VMEM] * len(operands),
        out_specs=[to] * len(outs),
        scratch_shapes=list(scratch),
        cost_estimate=pl.CostEstimate(flops=flops, bytes_accessed=0, transcendentals=0),
        compiler_params=params,
    )(*operands)


def on_device(states, task_ids, student_batch, teach_in, teach_out, student_up, student_down):
    row_count, width = states.shape
    owners, studs, parts = lax.axis_size("teach"), lax.axis_size("stud"), lax.axis_size("mdl")
    local, _, hidden = teach_in.shape
    actions = teach_out.shape[2]
    units = student_up.shape[1]
    teachers, batches = owners * local, owners * studs
    room = up_to(3 * row_count // (2 * teachers), ROW_TILE)
    extra = up_to(batches, LANES)
    slots = teachers * room
    f32, bf16 = jnp.float32, jnp.bfloat16

    def shape(rows, columns, dtype):
        return jax.ShapeDtypeStruct((rows, columns), dtype)

    height = slots // 2
    half, packed = shape(height, actions, f32), shape(height + PACK_ROWS, actions, f32)
    state = [shape(width // studs, slots, bf16), shape(slots, units, bf16), shape(slots, units, f32)]
    tokens = [ids.reshape(1, row_count) for ids in (task_ids, student_batch)]
    weights = (teach_in, teach_out, student_up, student_down)
    results = kernel(
        functools.partial(dispatch_body, owners, local, room, extra),
        [pltpu.VMEM((local * room, width + extra), bf16)] * owners
        + [pltpu.VMEM(w.shape, w.dtype) for w in weights],
        (states, *tokens, *weights),
        0,
        [pltpu.VMEM(a.shape, a.dtype) for a in (states, *tokens)] + [pltpu.SemaphoreType.DMA((7,))],
        LARGE,
        [HBM] * 7,
    )
    blocks, weights = results[:owners], results[owners:]
    middle = owners // 2
    near = [blocks[0]] + [send(blocks[k], "teach", k) for k in range(1, middle)]
    far = [send(blocks[k], "teach", k) for k in range(owners - 1, middle - 1, -1)]

    def forward(blocks, *earlier):
        rows = len(blocks) * local * room
        return kernel(
            functools.partial(forward_body, local, room, not earlier),
            [shape(rows, extra, f32), shape(1, extra, f32), half, packed, shape(rows, width, bf16)],
            (*blocks, *earlier, *weights),
            0,
        )

    steps = [1 << i for i in range(parts.bit_length() - 1)]
    second_tags, counts, second, second_out, second_rows = forward(near)
    second_in = cross(second_out, steps[-1])
    first_tags, counts, first, first_out, first_rows = forward(far, counts)
    first_in = cross(first_out, steps[0])
    rows, tags = (first_rows, second_rows), (first_tags, second_tags)
    all_counts, mates = [counts], []
    for k in range(1, studs):
        all_counts.append(send(counts, "stud", k))
        mates.append([send(part, "stud", k) for part in rows])
    second_in, all_counts = lax.optimization_barrier((second_in, all_counts))
    for there, back in zip(steps[1:], steps[-2::-1]):
        second, second_out = kernel(pair_body, [half, packed], (second, second_in), 0)
        first, first_out = kernel(pair_body, [half, packed], (first, first_in, second), 0)
        first_out, second_out = lax.optimization_barrier((first_out, second_out))
        first_in, second_in = cross(first_out, there), cross(second_out, back)
    ahead = functools.partial(ahead_body, owners, studs)
    *ours, chosen = kernel(
        ahead, state + [shape(actions // studs, actions, bf16)], (*rows, weights[2], first), 0
    )
    known = [ours] + [kernel(ahead, state, (*theirs, weights[2], first), 0) for theirs in mates]
    sums = (second, second_in, first, first_in)
    sums, all_counts, known, chosen = lax.optimization_barrier((sums, all_counts, known, chosen))
    (scaled,) = kernel(scale_body, [shape(slots, actions, bf16)], (*sums, *tags, *all_counts), 0)
    errors = [scaled] + [send(scaled, "stud", k) for k in range(1, studs)]
    grads = [shape(width // studs, units, f32), shape(actions // studs, units, f32)]
    heights = [g.shape[0] // owners for g in grads]
    blocks = [shape(sum(heights), units, f32)] + [shape(sum(heights), units, bf16)] * (owners - 1)
    sums = []
    for k, (error, group) in enumerate(zip(errors, known)):
        sums = kernel(
            functools.partial(backward_body, owners, k > 0),
            blocks if k == studs - 1 else grads,
            (error, *group, chosen, weights[3], *sums),
            0,
        )
    pieces = [sums[0]] + [send(sums[k], "teach", k) for k in range(owners - 1, 0, -1)]
    outs = [shape(h, units, f32) for h in heights]
    return kernel(
        closing_body,
        outs,
        pieces,
        0,
        [pltpu.VMEM(o.shape, f32) for o in outs] + [pltpu.SemaphoreType.DMA((2,))],
        to=HBM,
    )


def solution(mesh):
    in_specs = (
        P(("teach", "stud"), None),
        P(("teach", "stud"), None),
        P(("teach", "stud"), None),
        P("teach", None, "mdl"),
        P("teach", "mdl", None),
        P(None, "mdl"),
        P(None, "mdl"),
    )
    out_specs = (P(("teach", "stud"), "mdl"), P(("teach", "stud"), "mdl"))
    return jax.shard_map(
        on_device, mesh=mesh, in_specs=in_specs, out_specs=out_specs, check_vma=False
    )
```
